32 devices in a mesh: fsdp: 32 (over z, y, x, core).
Axes of the slice: x: 2, y: 2, z: 4, core: 2. Of those that a mesh axis runs over, the one named last changes fastest.
Arguments:
- images: bfloat16 [64, 196, 768], P('fsdp'), may hold values from -6 to 6
- labels: int32 [64], P('fsdp'), may hold values from 0 to 999
- valid: int32 [64], P('fsdp'), may hold values from 0 to 1, as said below
- layer_params: float32 [3, 1777664], P(None, 'fsdp')
- layer_momentum: float32 [3, 1777664], P(None, 'fsdp'), may hold values from -0.125 to 0.125
- layer_average: float32 [3, 1777664], P(None, 'fsdp')
- outer_params: float32 [757760], P('fsdp')
- outer_momentum: float32 [757760], P('fsdp'), may hold values from -0.125 to 0.125
- outer_average: float32 [757760], P('fsdp')
Outputs:
- loss_sum: float32 [], replicated
- image_count: float32 [], replicated
- layer_params_new: float32 [3, 1777664], P(None, 'fsdp')
- layer_momentum_new: float32 [3, 1777664], P(None, 'fsdp')
- layer_average_new: float32 [3, 1777664], P(None, 'fsdp')
- outer_params_new: float32 [757760], P('fsdp')
- outer_momentum_new: float32 [757760], P('fsdp')
- outer_average_new: float32 [757760], P('fsdp')
The draws below stay inside these ranges and needn't reach their ends.
Inputs may be any that keep to these rules, and one draw needn't show every extreme that they name: `valid`: the share of real images rises from about 0.3 in the first slots to all in the last; the last slot is always real.
All inputs are finite; a program needn't handle non-finite values.
Results may differ from the reference program's by a relative error of at most 0.012.
The reference program's roundings to bfloat16 on the way count: a program that leaves them out, or rounds other values in their place, can miss the bound.
Values may be sent and summed in bfloat16 or wider, within the bound.
No kernel may reach another device: no remote copies, remote signals or barrier semaphores. Data moves between devices by JAX's collectives and lax.ppermute only.
A program may use at most 192 MiB of HBM per device.

```python
import jax
import jax.numpy as jnp
from jax import lax

D = 384
HEADS = 6
HEAD = 64
FF = 1536
CLASSES = 1000
PATCH_IN = 768
PATCHES = 196
SEQ = 197
LAYERS = 3
IMAGES = 64
LAYER_P = 1774080
LAYER_FLAT = 1777664
OUTER_P = 757096
OUTER_FLAT = 757760


def unit_noise(key, shape):
    first_key = jax.random.fold_in(key, 0)
    normal_part = jax.random.normal(first_key, shape, jnp.float32)
    return normal_part


def layer_values(key):
    keys_list = jax.random.split(key, 8)
    gains = 1.0 + 0.25 * unit_noise(keys_list[0], (LAYERS, 2, D))
    biases = 0.3 * unit_noise(keys_list[1], (LAYERS, 6, D))
    bias_up = 0.3 * unit_noise(keys_list[2], (LAYERS, FF))
    w_qkv = unit_noise(keys_list[3], (LAYERS, 3 * D * D)) * D ** (-0.5)
    w_out = unit_noise(keys_list[4], (LAYERS, D * D)) * 4.0 * D ** (-0.5)
    w_up = unit_noise(keys_list[5], (LAYERS, D * FF)) * D ** (-0.5)
    w_down = unit_noise(keys_list[6], (LAYERS, FF * D)) * FF ** (-0.5)
    padding = 0.05 * unit_noise(keys_list[7], (LAYERS, LAYER_FLAT - LAYER_P))
    return jnp.concatenate([gains[:, 0], biases[:, 0], gains[:, 1], biases[:, 1], biases[:, 2:].reshape(LAYERS, 4 * D), bias_up, w_qkv, w_out, w_up, w_down, padding], 1)


def outer_values(key):
    keys_list = jax.random.split(key, 8)
    cls_token = unit_noise(keys_list[0], (D,))
    gain_final = 1.0 + 0.25 * unit_noise(keys_list[1], (D,))
    biases = 0.3 * unit_noise(keys_list[2], (2 * D,))
    bias_head = 0.3 * unit_noise(keys_list[3], (CLASSES,))
    position = 0.5 * unit_noise(keys_list[4], (SEQ * D,))
    w_patch = unit_noise(keys_list[5], (PATCH_IN * D,)) * PATCH_IN ** (-0.5)
    w_head = unit_noise(keys_list[6], (D * CLASSES,)) * 2.0 * D ** (-0.5)
    padding = 0.05 * unit_noise(keys_list[7], (OUTER_FLAT - OUTER_P,))
    return jnp.concatenate([cls_token, gain_final, biases, bias_head, position, w_patch, w_head, padding])


def draw_valid(key, part):
    key = jax.random.fold_in(key, 5)
    slots = jnp.arange(IMAGES, dtype=jnp.int32)
    limit = 300 + 700 * slots // (IMAGES - 1)
    return (jax.random.randint(key, (IMAGES,), 0, 1000) < limit).astype(jnp.int32)


def draw_layer_params(key, part):
    key = jax.random.fold_in(key, 1)
    return layer_values(key)


def draw_layer_average(key, part):
    key = jax.random.fold_in(key, 2)
    return layer_values(key)


def draw_outer_params(key, part):
    key = jax.random.fold_in(key, 3)
    return outer_values(key)


def draw_outer_average(key, part):
    key = jax.random.fold_in(key, 4)
    return outer_values(key)


def plant(result, key, least, high):
    dims = result.shape
    place = [jax.random.randint(jax.random.fold_in(key, axis), (), 0, dims[axis]) for axis in range(len(dims))]
    result = result.at[tuple(place)].set(least)
    longest = dims.index(max(dims))
    place[longest] = (place[longest] + 1) % dims[longest]
    return result.at[tuple(place)].set(high)


def steps_of(rng, dims, shards, least, largest):
    def one(dim, blocks):
        steps = jax.random.uniform(jax.random.fold_in(jax.random.fold_in(rng, 6), dim), (blocks,), jnp.float32, least / len(shards), largest / len(shards))
        return jnp.repeat(jnp.exp(steps), dims[dim] // blocks).reshape((-1,) + (1,) * (len(dims) - dim - 1))

    loudness = one(*shards[0])
    for cut in shards[1:]:
        loudness = loudness * one(*cut)
    return loudness


def gaussian(rng, shape, scale, most, cuts=(), kind=jnp.bfloat16):
    factor_of = steps_of(rng, shape, cuts, -0.22, 0.18) if cuts else 1.0
    drawn = jax.random.normal(rng, shape, jnp.float32) * scale * factor_of
    return jnp.minimum(jnp.maximum(drawn, -most), most).astype(kind)


def setup_inputs(seed: int = 0) -> dict:
    arg_keys = jax.random.split(jax.random.key(seed), 10)
    return {
        "images": gaussian(arg_keys[0], (IMAGES, PATCHES, PATCH_IN), 1.0, 6.0, ((0, 32),)),
        "labels": plant(jax.random.randint(arg_keys[1], (IMAGES,), 0, CLASSES), jax.random.fold_in(arg_keys[1], 1), 0, CLASSES - 1).astype(jnp.int32),
        "valid": draw_valid(jax.random.fold_in(arg_keys[9], 71), 0),
        "layer_params": draw_layer_params(jax.random.fold_in(arg_keys[9], 71), 0),
        "layer_momentum": gaussian(arg_keys[4], (LAYERS, LAYER_FLAT), (0.05 / (0.6 * IMAGES) ** 0.5), 0.125, ((1, 32),), jnp.float32),
        "layer_average": draw_layer_average(jax.random.fold_in(arg_keys[9], 71), 0),
        "outer_params": draw_outer_params(jax.random.fold_in(arg_keys[9], 71), 0),
        "outer_momentum": gaussian(arg_keys[7], (OUTER_FLAT,), (0.05 / (0.6 * IMAGES) ** 0.5), 0.125, ((0, 32),), jnp.float32),
        "outer_average": draw_outer_average(jax.random.fold_in(arg_keys[9], 71), 0),
    }


@jax.custom_vjp
def low(v):
    return lax.optimization_barrier(v.astype(jnp.bfloat16)).astype(jnp.float32)

@jax.custom_vjp
def low_back(v):
    return v

def low_keep(v):
    return (low(v), None)

def low_pass(kept, grad):
    return (grad,)

def back_keep(v):
    return (v, None)

def back_low(kept, grad):
    return (low(grad),)
low.defvjp(low_keep, low_pass)
low_back.defvjp(back_keep, back_low)
highest = lax.Precision.HIGHEST
eps_norm = 1e-06
smooth = 0.1
step_rate = 20.0

def matmul(left, right):
    return jnp.matmul(left, right, precision=highest)

def split_flat(flat_vec, widths):
    segments = []
    offset = 0
    for seg_width in widths:
        segments.append(flat_vec[offset:offset + seg_width])
        offset = offset + seg_width
    return segments

def layer_norm(values, gain, bias):
    center = values - lax.optimization_barrier(jnp.mean(values, -1, keepdims=True))
    spread = lax.optimization_barrier(jnp.mean(center * center, -1, keepdims=True))
    return center * lax.rsqrt(spread + eps_norm) * gain + bias

def gelu_value(values):
    return 0.5 * values * (1.0 + jax.scipy.special.erf(values * 0.7071067811865476))

def layer_apply(residual, flat_vec):
    segments = split_flat(flat_vec, [D] * 8 + [FF, 3 * D * D, D * D, D * FF, FF * D])
    gain_one, bias_one, gain_two, bias_two, bias_query, bias_value, bias_out, bias_down, bias_up = segments[:9]
    w_qkv = segments[9].reshape(D, 3 * D)
    w_out = segments[10].reshape(D, D)
    w_up = segments[11].reshape(D, FF)
    w_down = segments[12].reshape(FF, D)
    groups = residual.shape[0]
    normed_one = low(layer_norm(residual, gain_one, bias_one))
    bias_all = jnp.concatenate([bias_query, jnp.zeros_like(bias_query), bias_value])
    qkv = low(low_back(matmul(normed_one, w_qkv)) + bias_all).reshape(groups, SEQ, 3, HEADS, HEAD)
    raw_scores = jnp.einsum('gqhe,gkhe->ghqk', qkv[:, :, 0], qkv[:, :, 1], precision=highest)
    scores = low_back(raw_scores) * HEAD ** (-0.5)
    exponent = jnp.exp(scores - lax.optimization_barrier(jnp.max(scores, -1, keepdims=True)))
    attn_probs = exponent / lax.optimization_barrier(jnp.sum(exponent, -1, keepdims=True))
    attended = jnp.einsum('ghqk,gkhe->gqhe', low(attn_probs), qkv[:, :, 2], precision=highest)
    attended = low(low_back(attended.reshape(groups, SEQ, D)))
    residual = residual + low_back(matmul(attended, w_out)) + bias_out
    normed_two = low(layer_norm(residual, gain_two, bias_two))
    up_value = low_back(matmul(normed_two, w_up)) + bias_up
    active = low(gelu_value(up_value))
    return residual + low_back(matmul(active, w_down)) + bias_down

def group_loss(layer_lo, outer_lo, patches, labels, valid_float):
    segments = split_flat(outer_lo, [D] * 4 + [CLASSES, SEQ * D, PATCH_IN * D, D * CLASSES])
    cls_token, gain_final, bias_final, bias_patch, bias_head = segments[:5]
    position = segments[5].reshape(SEQ, D)
    w_patch = segments[6].reshape(PATCH_IN, D)
    w_head = segments[7].reshape(D, CLASSES)
    groups = patches.shape[0]
    embed = low_back(matmul(patches, w_patch)) + bias_patch
    leading = jnp.broadcast_to(cls_token, (groups, 1, D))
    residual = jnp.concatenate([leading, embed], 1) + position
    for layer_index in range(LAYERS):
        residual = layer_apply(residual, layer_lo[layer_index])
    normed_final = low(layer_norm(residual[:, 0], gain_final, bias_final))
    logits = low_back(matmul(normed_final, w_head)) + bias_head
    top_logit = lax.optimization_barrier(jnp.max(logits, -1, keepdims=True))
    log_total = jnp.log(lax.optimization_barrier(jnp.sum(jnp.exp(logits - top_logit), -1))) + top_logit[:, 0]
    onehot = (labels[:, None] == jnp.arange(CLASSES, dtype=jnp.int32)[None, :]).astype(jnp.float32)
    target = (1.0 - smooth) * onehot + smooth / CLASSES
    per_image = log_total - lax.optimization_barrier(jnp.sum(target * logits, -1))
    return jnp.sum(valid_float * per_image)

def nesterov(params, momentum, average, grads):
    momentum_new = 0.5 * momentum + grads
    params_new = params - step_rate * (grads + 0.5 * momentum_new)
    return (params_new, momentum_new, 0.5 * average + 0.5 * params_new)

def reference(images, labels, valid, layer_params, layer_momentum, layer_average, outer_params, outer_momentum, outer_average):
    group_images = 16
    groups_total = IMAGES // group_images
    patches = images.astype(jnp.float32).reshape(groups_total, group_images, PATCHES, PATCH_IN)
    label_groups = labels.reshape(groups_total, group_images)
    valid_float = valid.astype(jnp.float32)
    valid_groups = valid_float.reshape(groups_total, group_images)
    image_count = jnp.sum(valid_float)
    checked_loss = jax.checkpoint(group_loss)

    def objective(layer_flat, outer_flat):
        layer_lo = low(layer_flat)
        outer_lo = low(outer_flat)

        def group_step(carry_total, batch_items):
            return (carry_total + checked_loss(layer_lo, outer_lo, batch_items[0], batch_items[1], batch_items[2]), None)
        total_loss, unused = lax.scan(group_step, jnp.zeros((), jnp.float32), (patches, label_groups, valid_groups))
        return (total_loss / image_count, total_loss)
    mean_loss, backward_fn, loss_sum = jax.vjp(objective, layer_params, outer_params, has_aux=True)
    layer_grad, outer_grad = backward_fn(jnp.ones_like(mean_loss))
    layer_new, layer_mom_new, layer_avg_new = nesterov(layer_params, layer_momentum, layer_average, layer_grad)
    outer_new, outer_mom_new, outer_avg_new = nesterov(outer_params, outer_momentum, outer_average, outer_grad)
    return (loss_sum, image_count, layer_new, layer_mom_new, layer_avg_new, outer_new, outer_mom_new, outer_avg_new)
```

```python
import functools

import jax
import jax.numpy as jnp
import numpy as np
from jax import lax
from jax.experimental import pallas as pl
from jax.experimental.pallas import tpu as pltpu
from jax.sharding import PartitionSpec as P

D = 384
HEADS = 6
HEAD = 64
FF = 1536
CLASSES = 1000
CLASS_PAD = 1024
PATCH_IN = 768
PATCHES = 196
SEQ = 197
LAYERS = 3
LANES = 128

eps_norm = 1e-06
smooth = 0.1
step_rate = 20.0
root_half = 0.7071067811865476
inv_root_two_pi = 0.3989422804014327

VMEM_LIMIT = 56 * 1024 * 1024

ROW_VEC = 36
ROW_QKV = ROW_VEC
ROW_OUT = ROW_QKV + 3 * D * D // LANES
ROW_UP = ROW_OUT + D * D // LANES
ROW_DOWN = ROW_UP + D * FF // LANES
ROW_END = ROW_DOWN + D * FF // LANES

OUTER_SHIFT = 24
OROW_POS = (4 * D + CLASSES + OUTER_SHIFT) // LANES
OROW_PATCH = OROW_POS + SEQ * D // LANES
OROW_HEAD = OROW_PATCH + PATCH_IN * D // LANES


def round_up(value, unit):
    return (value + unit - 1) // unit * unit


def bits_of(devices):
    count = devices.bit_length() - 1
    assert 1 << count == devices
    return count


def slot_masks(devices):
    if devices == 32:
        first, second = [], []
        for slot in range(16):
            along_z = (slot & 3) * 8
            near, far = (slot >> 2) & 1, (slot >> 3) & 1
            first.append(along_z + near * 4 + far * 2)
            second.append(along_z + near * 2 + far * 4)
        return (first, second)
    plain = [2 * slot for slot in range(devices // 2)]
    return (plain, plain)


def swap(values, masks, devices):
    pairs = [(i, i ^ masks[i & 1]) for i in range(devices)]
    return lax.ppermute(values, "fsdp", pairs)


def gather_column(shard, devices):
    if devices == 32:
        column = jnp.stack([shard] + [swap(shard, (8 * k, 8 * k), devices) for k in (1, 2, 3)])
        column = jnp.concatenate([column, swap(column, (4, 2), devices)])
        column = jnp.concatenate([column, swap(column, (2, 4), devices)])
    else:
        column = shard[None]
        step = 2
        while step < devices:
            column = jnp.concatenate([column, swap(column, (step, step), devices)])
            step = step * 2
    return (column, swap(column, (1, 1), devices))


def scatter_sum(keep, send, devices):
    total = keep.astype(jnp.float32) + swap(send, (1, 1), devices).astype(jnp.float32)
    if devices == 32:
        low = total[8:].astype(jnp.bfloat16)
        total = total[:8] + swap(low, (2, 4), devices).astype(jnp.float32)
        low = total[4:].astype(jnp.bfloat16)
        total = total[:4] + swap(low, (4, 2), devices).astype(jnp.float32)
        low = total[1:].astype(jnp.bfloat16)
        parts = [swap(low[k - 1], (8 * k, 8 * k), devices).astype(jnp.float32) for k in (1, 2, 3)]
        return total[0] + ((parts[0] + parts[1]) + parts[2])
    while total.shape[0] > 1:
        half = total.shape[0] // 2
        low = total[half:].astype(jnp.bfloat16)
        total = total[:half] + swap(low, (2 * half, 2 * half), devices).astype(jnp.float32)
    return total[0]


def select_mask(core, masks, slot):
    first, second = masks[0][slot], masks[1][slot]
    if first == second:
        return first
    return jnp.where(core == 0, first, second)


def load_shards(mine_ref, theirs_ref, staged, sem, masks, half):
    me = lax.axis_index("fsdp")
    core = lax.rem(me, 2)
    copies = []
    for slot in range(half):
        own = jnp.bitwise_xor(me, select_mask(core, masks, slot))
        other = jnp.bitwise_xor(jnp.bitwise_xor(me, 1), select_mask(1 - core, masks, slot))
        copies.append(pltpu.make_async_copy(mine_ref.at[slot], staged.at[own], sem))
        copies.append(pltpu.make_async_copy(theirs_ref.at[slot], staged.at[other], sem))
    for copy in copies:
        copy.start()
    for copy in copies:
        copy.wait()


def store_shards(keep_ref, send_ref, staged, sem, masks, half):
    me = lax.axis_index("fsdp")
    core = lax.rem(me, 2)
    copies = []
    for slot in range(half):
        own = jnp.bitwise_xor(me, select_mask(core, masks, slot))
        other = jnp.bitwise_xor(jnp.bitwise_xor(me, 1), select_mask(1 - core, masks, slot))
        copies.append(pltpu.make_async_copy(staged.at[own], keep_ref.at[slot], sem))
        copies.append(pltpu.make_async_copy(staged.at[other], send_ref.at[slot], sem))
    for copy in copies:
        copy.start()
    for copy in copies:
        copy.wait()


def take_matrix(flat, row, height, width):
    blocks = width // LANES
    return [flat[pl.ds(row + c, height, stride=blocks), :] for c in range(blocks)]


def put_matrix(flat, row, matrix_ref, height, width):
    blocks = width // LANES
    for c in range(blocks):
        flat[pl.ds(row + c, height, stride=blocks), :] = matrix_ref[:, c * LANES : (c + 1) * LANES]


def unpack_layer_kernel(
    masks, half, rows, mine, theirs, vec_ref, qkv_ref, out_ref, up_ref, down_ref, staged, flat, sem
):
    load_shards(mine, theirs, staged, sem, masks, half)
    for shard in range(2 * half):
        flat[shard * rows : (shard + 1) * rows, :] = staged[shard, :rows, :].astype(jnp.float32)
    vec_ref[...] = flat[0:ROW_VEC, :]
    for ref, row in ((qkv_ref, ROW_QKV), (out_ref, ROW_OUT), (up_ref, ROW_UP), (down_ref, ROW_DOWN)):
        height, width = ref.shape
        for c, block in enumerate(take_matrix(flat, row, height, width)):
            ref[:, c * LANES : (c + 1) * LANES] = block.astype(jnp.bfloat16)


def unpack_layer(pieces, rows):
    mine, theirs = pieces
    half, padded = mine.shape[0], mine.shape[1]
    kernel = functools.partial(unpack_layer_kernel, slot_masks(2 * half), half, rows)
    return pl.pallas_call(
        kernel,
        out_shape=[
            jax.ShapeDtypeStruct((ROW_VEC, LANES), jnp.float32),
            jax.ShapeDtypeStruct((D, 3 * D), jnp.bfloat16),
            jax.ShapeDtypeStruct((D, D), jnp.bfloat16),
            jax.ShapeDtypeStruct((D, FF), jnp.bfloat16),
            jax.ShapeDtypeStruct((FF, D), jnp.bfloat16),
        ],
        in_specs=[pl.BlockSpec(memory_space=pl.ANY)] * 2,
        out_specs=[pl.BlockSpec(memory_space=pltpu.VMEM)] * 5,
        scratch_shapes=[
            pltpu.VMEM((2 * half, padded, LANES), jnp.bfloat16),
            pltpu.VMEM((round_up(2 * half * rows, 8), LANES), jnp.float32),
            pltpu.SemaphoreType.DMA,
        ],
        compiler_params=pltpu.CompilerParams(vmem_limit_bytes=VMEM_LIMIT),
        name="unpack_layer",
    )(mine, theirs)


def unpack_outer_kernel(
    masks, half, rows, mine, theirs, small_ref, pos_ref, patch_ref, head_ref, count_ref, staged, flat, head, sem
):
    load_shards(mine, theirs, staged, sem, masks, half)
    count = jnp.zeros((1, LANES), jnp.float32)
    for shard in range(2 * half):
        flat[shard * rows : (shard + 1) * rows, :] = staged[shard, :rows, :].astype(jnp.float32)
        tail = staged[shard, rows : rows + 2, :].astype(jnp.float32)
        count = count + tail[1:2]
        if shard + 1 < 2 * half:
            later = staged[shard + 1, 0:1, :].astype(jnp.float32)
            carry = tail[0:1] + later
        if shard > 0:
            flat[shard * rows : shard * rows + 1, :] = before
        before = carry
    count_ref[...] = count
    small_ref[...] = flat[0:OROW_POS, :]
    for c, block in enumerate(take_matrix(flat, OROW_POS, SEQ, D)):
        pos_ref[:, c * LANES : (c + 1) * LANES] = block
    for c, block in enumerate(take_matrix(flat, OROW_PATCH, PATCH_IN, D)):
        patch_ref[:, c * LANES : (c + 1) * LANES] = block.astype(jnp.bfloat16)
    lane = lax.broadcasted_iota(jnp.int32, (24, LANES), 1)
    for p in range(16):
        shift, base = (CLASSES * p) % LANES, OROW_HEAD + (CLASSES * p) // LANES
        part = [flat[pl.ds(base + c, 24, stride=125), :] for c in range(9 if shift else 8)]
        if shift:
            part = [pltpu.roll(block, LANES - shift, 1) for block in part]
        for c in range(8):
            block = jnp.where(lane < LANES - shift, part[c], part[c + 1]) if shift else part[c]
            if c == 7:
                block = jnp.where(lane < CLASSES - 7 * LANES, block, 0.0)
            head[c, pl.ds(p, 24, stride=16), :] = block
    for c in range(8):
        head_ref[:, c * LANES : (c + 1) * LANES] = head[c].astype(jnp.bfloat16)


def unpack_outer(pieces, rows):
    mine, theirs = pieces
    half, padded = mine.shape[0], mine.shape[1]
    kernel = functools.partial(unpack_outer_kernel, slot_masks(2 * half), half, rows)
    return pl.pallas_call(
        kernel,
        out_shape=[
            jax.ShapeDtypeStruct((OROW_POS, LANES), jnp.float32),
            jax.ShapeDtypeStruct((SEQ, D), jnp.float32),
            jax.ShapeDtypeStruct((PATCH_IN, D), jnp.bfloat16),
            jax.ShapeDtypeStruct((D, CLASS_PAD), jnp.bfloat16),
            jax.ShapeDtypeStruct((1, LANES), jnp.float32),
        ],
        in_specs=[pl.BlockSpec(memory_space=pl.ANY)] * 2,
        out_specs=[pl.BlockSpec(memory_space=pltpu.VMEM)] * 5,
        scratch_shapes=[
            pltpu.VMEM((2 * half, padded, LANES), jnp.bfloat16),
            pltpu.VMEM((round_up(2 * half * rows + 1, 8), LANES), jnp.float32),
            pltpu.VMEM((CLASS_PAD // LANES, D, LANES), jnp.float32),
            pltpu.SemaphoreType.DMA,
        ],
        compiler_params=pltpu.CompilerParams(vmem_limit_bytes=VMEM_LIMIT),
        name="unpack_outer",
    )(mine, theirs)


def pack_layer_kernel(
    masks, half, rows, spare, vec, qkv, out, up, down, extra, keep_ref, send_ref, staged, flat, sem
):
    flat[0:ROW_VEC, :] = vec[...]
    flat[ROW_END:, :] = jnp.zeros((flat.shape[0] - ROW_END, LANES), jnp.float32)
    for ref, row in ((qkv, ROW_QKV), (out, ROW_OUT), (up, ROW_UP), (down, ROW_DOWN)):
        put_matrix(flat, row, ref, *ref.shape)
    tail = extra[...]
    for shard in range(2 * half):
        staged[shard, :rows, :] = flat[shard * rows : (shard + 1) * rows, :].astype(jnp.bfloat16)
        staged[shard, rows : rows + spare, :] = tail
    store_shards(keep_ref, send_ref, staged, sem, masks, half)


def pack_layer(vec, matrices, extra, rows, padded, devices):
    half = devices // 2
    spare = padded - rows
    kernel = functools.partial(pack_layer_kernel, slot_masks(devices), half, rows, spare)
    shape = jax.ShapeDtypeStruct((half, padded, LANES), jnp.bfloat16)
    return pl.pallas_call(
        kernel,
        out_shape=[shape, shape],
        in_specs=[pl.BlockSpec(memory_space=pltpu.VMEM)] * 6,
        out_specs=[pl.BlockSpec(memory_space=pl.ANY)] * 2,
        scratch_shapes=[
            pltpu.VMEM((2 * half, padded, LANES), jnp.bfloat16),
            pltpu.VMEM((round_up(2 * half * rows, 8), LANES), jnp.float32),
            pltpu.SemaphoreType.DMA,
        ],
        compiler_params=pltpu.CompilerParams(vmem_limit_bytes=VMEM_LIMIT),
        name="pack_layer",
    )(vec, *matrices, extra)


def pack_outer_kernel(
    masks, half, rows, small, pos, patch, head_in, keep_ref, send_ref, staged, flat, head, sem
):
    for c in range(8):
        head[c] = head_in[:, c * LANES : (c + 1) * LANES]
    flat[0:OROW_POS, :] = small[...]
    put_matrix(flat, OROW_POS, pos, SEQ, D)
    put_matrix(flat, OROW_PATCH, patch, PATCH_IN, D)
    lane = lax.broadcasted_iota(jnp.int32, (24, LANES), 1)

    def block_of(p, c):
        return head[c, pl.ds(p, 24, stride=16), :]

    for i in range(125):
        p, start = LANES * i // CLASSES, LANES * i % CLASSES
        c, shift = start // LANES, start % LANES
        value = block_of(p, c)
        if shift:
            value = pltpu.roll(value, LANES - shift, 1)
            if c < 7:
                later = pltpu.roll(block_of(p, c + 1), LANES - shift, 1)
                value = jnp.where(lane < LANES - shift, value, later)
        here = CLASSES - start
        if here < LANES:
            value = jnp.where(lane < here, value, pltpu.roll(block_of(p + 1, 0), here, 1))
        flat[pl.ds(OROW_HEAD + i, 24, stride=125), :] = value
    end = OROW_HEAD + 24 * 125
    flat[end:, :] = jnp.zeros((flat.shape[0] - end, LANES), jnp.float32)
    for shard in range(2 * half):
        staged[shard, : rows + 1, :] = flat[shard * rows : (shard + 1) * rows + 1, :].astype(
            jnp.bfloat16
        )
    store_shards(keep_ref, send_ref, staged, sem, masks, half)


def pack_outer(small, pos, patch, head, rows, padded, devices):
    half = devices // 2
    kernel = functools.partial(pack_outer_kernel, slot_masks(devices), half, rows)
    shape = jax.ShapeDtypeStruct((half, padded, LANES), jnp.bfloat16)
    return pl.pallas_call(
        kernel,
        out_shape=[shape, shape],
        in_specs=[pl.BlockSpec(memory_space=pltpu.VMEM)] * 4,
        out_specs=[pl.BlockSpec(memory_space=pl.ANY)] * 2,
        scratch_shapes=[
            pltpu.VMEM((2 * half, padded, LANES), jnp.bfloat16),
            pltpu.VMEM((round_up(2 * half * rows + 1, 8), LANES), jnp.float32),
            pltpu.VMEM((CLASS_PAD // LANES, D, LANES), jnp.float32),
            pltpu.SemaphoreType.DMA,
        ],
        compiler_params=pltpu.CompilerParams(vmem_limit_bytes=VMEM_LIMIT),
        name="pack_outer",
    )(small, pos, patch, head)


def split_flat(flat_vec, widths):
    segments = []
    offset = 0
    for seg_width in widths:
        segments.append(flat_vec[offset : offset + seg_width])
        offset = offset + seg_width
    return segments


def contract_rows(left, right):
    return lax.dot_general(
        left, right, (((0,), (0,)), ((), ())), preferred_element_type=jnp.float32
    )


def contract_last(left, right):
    return lax.dot_general(
        left, right, (((1,), (1,)), ((), ())), preferred_element_type=jnp.float32
    )


def norm_parts(values):
    center = values - jnp.mean(values, -1, keepdims=True)
    inverse = lax.rsqrt(jnp.mean(center * center, -1, keepdims=True) + eps_norm)
    return (center * inverse, inverse)


def norm_back(grad_normed, normal, inverse, gain):
    scaled = grad_normed * gain
    return inverse * (
        scaled
        - jnp.mean(scaled, -1, keepdims=True)
        - normal * jnp.mean(scaled * normal, -1, keepdims=True)
    )


def gelu_value(values):
    return 0.5 * values * (1.0 + jax.scipy.special.erf(values * root_half))


def gelu_slope(values):
    return (
        0.5 * (1.0 + jax.scipy.special.erf(values * root_half))
        + values * jnp.exp(-0.5 * values * values) * inv_root_two_pi
    )


def layer_forward(residual, vectors, matrices):
    gain_one, bias_one, gain_two, bias_two, bias_query, bias_value, bias_out, bias_down, bias_up = (
        vectors
    )
    w_qkv, w_out, w_up, w_down = matrices
    images_here = residual.shape[0] // SEQ
    normal_one, inverse_one = norm_parts(residual)
    normed_one = (normal_one * gain_one + bias_one).astype(jnp.bfloat16)
    bias_all = jnp.concatenate([bias_query, jnp.zeros_like(bias_query), bias_value])
    qkv = (jnp.dot(normed_one, w_qkv, preferred_element_type=jnp.float32) + bias_all).astype(
        jnp.bfloat16
    )
    split_heads = qkv.reshape(images_here, SEQ, 3, HEADS, HEAD)
    queries = split_heads[:, :, 0]
    keys_part = split_heads[:, :, 1]
    values_part = split_heads[:, :, 2]
    scores = jnp.einsum(
        "bqhe,bkhe->bhqk", queries, keys_part, preferred_element_type=jnp.float32
    ) * HEAD ** (-0.5)
    exponent = jnp.exp(scores - jnp.max(scores, -1, keepdims=True))
    attn_probs = exponent / jnp.sum(exponent, -1, keepdims=True)
    probs_low = attn_probs.astype(jnp.bfloat16)
    attended = jnp.einsum(
        "bhqk,bkhe->bqhe", probs_low, values_part, preferred_element_type=jnp.float32
    )
    attended = attended.astype(jnp.bfloat16).reshape(-1, D)
    state_mid = residual + jnp.dot(attended, w_out, preferred_element_type=jnp.float32) + bias_out
    normal_two, inverse_two = norm_parts(state_mid)
    normed_two = (normal_two * gain_two + bias_two).astype(jnp.bfloat16)
    up_value = jnp.dot(normed_two, w_up, preferred_element_type=jnp.float32) + bias_up
    active = gelu_value(up_value).astype(jnp.bfloat16)
    state_out = state_mid + jnp.dot(active, w_down, preferred_element_type=jnp.float32) + bias_down
    saved = (
        normal_one,
        inverse_one,
        normed_one,
        queries,
        keys_part,
        values_part,
        attn_probs,
        probs_low,
        attended,
        normal_two,
        inverse_two,
        normed_two,
        up_value,
        active,
    )
    return (state_out, saved)


def layer_backward(images_here, saved, vectors, matrices, grad_out):
    gain_one, bias_one, gain_two, bias_two, bias_query, bias_value, bias_out, bias_down, bias_up = (
        vectors
    )
    w_qkv, w_out, w_up, w_down = matrices
    (
        normal_one,
        inverse_one,
        normed_one,
        queries,
        keys_part,
        values_part,
        attn_probs,
        probs_low,
        attended,
        normal_two,
        inverse_two,
        normed_two,
        up_value,
        active,
    ) = saved
    grad_bias_down = jnp.sum(grad_out, 0)
    grad_low = grad_out.astype(jnp.bfloat16)
    grad_w_down = contract_rows(active, grad_low)
    grad_up = contract_last(grad_low, w_down) * gelu_slope(up_value)
    grad_bias_up = jnp.sum(grad_up, 0)
    grad_up_low = grad_up.astype(jnp.bfloat16)
    grad_w_up = contract_rows(normed_two, grad_up_low)
    grad_normed_two = contract_last(grad_up_low, w_up)
    grad_gain_two = jnp.sum(grad_normed_two * normal_two, 0)
    grad_bias_two = jnp.sum(grad_normed_two, 0)
    grad_mid = grad_out + norm_back(grad_normed_two, normal_two, inverse_two, gain_two)
    grad_bias_out = jnp.sum(grad_mid, 0)
    grad_mid_low = grad_mid.astype(jnp.bfloat16)
    grad_w_out = contract_rows(attended, grad_mid_low)
    grad_attended = (
        contract_last(grad_mid_low, w_out)
        .astype(jnp.bfloat16)
        .reshape(images_here, SEQ, HEADS, HEAD)
    )
    grad_probs = jnp.einsum(
        "bqhe,bkhe->bhqk", grad_attended, values_part, preferred_element_type=jnp.float32
    )
    grad_values = jnp.einsum(
        "bhqk,bqhe->bkhe", probs_low, grad_attended, preferred_element_type=jnp.float32
    )
    grad_scores = attn_probs * (grad_probs - jnp.sum(grad_probs * attn_probs, -1, keepdims=True))
    grad_scores_low = (grad_scores * HEAD ** (-0.5)).astype(jnp.bfloat16)
    grad_queries = jnp.einsum(
        "bhqk,bkhe->bqhe", grad_scores_low, keys_part, preferred_element_type=jnp.float32
    )
    grad_keys = jnp.einsum(
        "bhqk,bqhe->bkhe", grad_scores_low, queries, preferred_element_type=jnp.float32
    )
    grad_qkv = jnp.stack([grad_queries, grad_keys, grad_values], 2).reshape(-1, 3 * D)
    grad_bias_query = jnp.sum(grad_qkv[:, :D], 0)
    grad_bias_value = jnp.sum(grad_qkv[:, 2 * D :], 0)
    grad_qkv_low = grad_qkv.astype(jnp.bfloat16)
    grad_w_qkv = contract_rows(normed_one, grad_qkv_low)
    grad_normed_one = contract_last(grad_qkv_low, w_qkv)
    grad_gain_one = jnp.sum(grad_normed_one * normal_one, 0)
    grad_bias_one = jnp.sum(grad_normed_one, 0)
    grad_in = grad_mid + norm_back(grad_normed_one, normal_one, inverse_one, gain_one)
    grad_vectors = [
        grad_gain_one,
        grad_bias_one,
        grad_gain_two,
        grad_bias_two,
        grad_bias_query,
        grad_bias_value,
        grad_bias_out,
        grad_bias_down,
        grad_bias_up,
    ]
    grad_vec = jnp.concatenate(grad_vectors).reshape(ROW_VEC, LANES)
    return (grad_in, grad_vec, (grad_w_qkv, grad_w_out, grad_w_up, grad_w_down))


def nesterov(params, momentum, average, grads):
    momentum_new = 0.5 * momentum + grads
    params_new = params - step_rate * (grads + 0.5 * momentum_new)
    return (params_new, momentum_new, 0.5 * average + 0.5 * params_new)


def shards(
    images,
    labels,
    valid,
    layer_params,
    layer_momentum,
    layer_average,
    outer_params,
    outer_momentum,
    outer_average,
):
    devices = lax.axis_size("fsdp")
    me = lax.axis_index("fsdp")
    layer_rows = layer_params.shape[1] // LANES
    layer_padded = round_up(layer_rows + 3 * devices // LANES + 1, 16)
    outer_rows = outer_params.shape[0] // LANES
    outer_padded = round_up(outer_rows + 2, 16)

    valid_float = valid.astype(jnp.float32)
    count_row = jnp.pad(jnp.sum(valid_float).reshape(1), (0, LANES - 1)).reshape(1, LANES)
    outer_shard = jnp.pad(outer_params, (OUTER_SHIFT, LANES - OUTER_SHIFT)).reshape(-1, LANES)
    outer_shard = jnp.concatenate([outer_shard, count_row]).astype(jnp.bfloat16)
    outer_shard = jnp.pad(outer_shard, ((0, outer_padded - outer_rows - 2), (0, 0)))
    layer_shards = []
    for layer_index in range(LAYERS):
        shard = layer_params[layer_index].reshape(layer_rows, LANES).astype(jnp.bfloat16)
        layer_shards.append(jnp.pad(shard, ((0, layer_padded - layer_rows), (0, 0))))

    small, position, w_patch, w_head, counts = unpack_outer(
        gather_column(outer_shard, devices), outer_rows
    )
    small = small.reshape(-1)[OUTER_SHIFT:]
    cls_token, gain_final, bias_final, bias_patch, bias_head = split_flat(
        small, [D] * 4 + [CLASSES]
    )
    bias_head = jnp.pad(bias_head, (0, CLASS_PAD - CLASSES))
    image_count = counts[0, 0]

    images_here = images.shape[0]
    patch_rows = images.reshape(-1, PATCH_IN)
    embed = (jnp.dot(patch_rows, w_patch, preferred_element_type=jnp.float32) + bias_patch).reshape(
        images_here, PATCHES, D
    )
    leading = jnp.broadcast_to(cls_token, (images_here, 1, D))
    residual = (jnp.concatenate([leading, embed], 1) + position).reshape(-1, D)
    kept = []
    for layer_index in range(LAYERS):
        vec, *matrices = unpack_layer(
            gather_column(layer_shards[layer_index], devices), layer_rows
        )
        vectors = split_flat(vec.reshape(-1), [D] * 8 + [FF])
        residual, saved = layer_forward(residual, vectors, matrices)
        kept.append((saved, vectors, matrices))
    final_rows = residual.reshape(images_here, SEQ, D)[:, 0]
    normal_final, inverse_final = norm_parts(final_rows)
    normed_final = (normal_final * gain_final + bias_final).astype(jnp.bfloat16)
    logits = jnp.dot(normed_final, w_head, preferred_element_type=jnp.float32) + bias_head
    real = jnp.arange(CLASS_PAD, dtype=jnp.int32)[None, :] < CLASSES
    top_logit = jnp.max(jnp.where(real, logits, -jnp.inf), -1, keepdims=True)
    exponent = jnp.where(real, jnp.exp(jnp.minimum(logits - top_logit, 0.0)), 0.0)
    total_exp = jnp.sum(exponent, -1, keepdims=True)
    log_total = jnp.log(total_exp[:, 0]) + top_logit[:, 0]
    onehot = (labels[:, None] == jnp.arange(CLASS_PAD, dtype=jnp.int32)[None, :]).astype(
        jnp.float32
    )
    target = jnp.where(real, (1.0 - smooth) * onehot + smooth / CLASSES, 0.0)
    per_image = log_total - jnp.sum(target * logits, -1)
    loss_here = jnp.sum(valid_float * per_image)
    loss_high = loss_here.astype(jnp.bfloat16).astype(jnp.float32)
    loss_mid = (loss_here - loss_high).astype(jnp.bfloat16).astype(jnp.float32)
    loss_low = loss_here - loss_high - loss_mid
    spare = layer_padded - layer_rows
    place = jnp.arange(spare * LANES, dtype=jnp.int32)
    extra = jnp.where(place == 3 * me, loss_high, 0.0)
    extra = jnp.where(place == 3 * me + 1, loss_mid, extra)
    extra = jnp.where(place == 3 * me + 2, loss_low, extra)
    extra = extra.astype(jnp.bfloat16).reshape(spare, LANES)

    grad_scale = valid_float * (1.0 / image_count)
    grad_logits = (exponent / total_exp - target) * grad_scale[:, None]
    grad_bias_head = jnp.sum(grad_logits, 0)
    grad_logits_low = grad_logits.astype(jnp.bfloat16)
    grad_w_head = contract_rows(normed_final, grad_logits_low)
    grad_normed_final = contract_last(grad_logits_low, w_head)
    grad_gain_final = jnp.sum(grad_normed_final * normal_final, 0)
    grad_bias_final = jnp.sum(grad_normed_final, 0)
    grad_final = norm_back(grad_normed_final, normal_final, inverse_final, gain_final)
    grad_state = (
        jnp.zeros((images_here, SEQ, D), jnp.float32).at[:, 0].set(grad_final).reshape(-1, D)
    )
    layer_grads = [None] * LAYERS
    for layer_index in reversed(range(LAYERS)):
        saved, vectors, matrices = kept[layer_index]
        grad_state, grad_vec, grad_matrices = layer_backward(
            images_here, saved, vectors, matrices, grad_state
        )
        keep, send = pack_layer(grad_vec, grad_matrices, extra, layer_rows, layer_padded, devices)
        summed = scatter_sum(keep, send, devices)
        layer_grads[layer_index] = summed[:layer_rows].reshape(-1)
        if layer_index == LAYERS - 1:
            loss_sum = jnp.sum(summed[layer_rows:])
    grad_embed_state = grad_state.reshape(images_here, SEQ, D)
    grad_cls = jnp.sum(grad_embed_state[:, 0], 0)
    grad_position = jnp.sum(grad_embed_state, 0)
    grad_embed = grad_embed_state[:, 1:].reshape(-1, D)
    grad_bias_patch = jnp.sum(grad_embed, 0)
    grad_w_patch = contract_rows(patch_rows, grad_embed.astype(jnp.bfloat16))
    grad_small = jnp.concatenate(
        [
            jnp.zeros((OUTER_SHIFT,), jnp.float32),
            grad_cls,
            grad_gain_final,
            grad_bias_final,
            grad_bias_patch,
            grad_bias_head[:CLASSES],
        ]
    ).reshape(OROW_POS, LANES)
    keep, send = pack_outer(
        grad_small, grad_position, grad_w_patch, grad_w_head, outer_rows, outer_padded, devices
    )
    summed = scatter_sum(keep, send, devices)
    outer_grad = summed[: outer_rows + 1].reshape(-1)[OUTER_SHIFT : OUTER_SHIFT + outer_rows * LANES]
    layer_grad = jnp.stack(layer_grads)
    layer_new, layer_mom_new, layer_avg_new = nesterov(
        layer_params, layer_momentum, layer_average, layer_grad
    )
    outer_new, outer_mom_new, outer_avg_new = nesterov(
        outer_params, outer_momentum, outer_average, outer_grad
    )
    return (
        loss_sum,
        image_count,
        layer_new,
        layer_mom_new,
        layer_avg_new,
        outer_new,
        outer_mom_new,
        outer_avg_new,
    )


def solution(mesh):
    return jax.shard_map(
        shards,
        mesh=mesh,
        in_specs=(
            P("fsdp", None, None),
            P("fsdp"),
            P("fsdp"),
            P(None, "fsdp"),
            P(None, "fsdp"),
            P(None, "fsdp"),
            P("fsdp"),
            P("fsdp"),
            P("fsdp"),
        ),
        out_specs=(
            P(),
            P(),
            P(None, "fsdp"),
            P(None, "fsdp"),
            P(None, "fsdp"),
            P("fsdp"),
            P("fsdp"),
            P("fsdp"),
        ),
        check_vma=False,
    )
```

```python
import functools

import jax
import jax.numpy as jnp
import numpy as np
from jax import lax
from jax.experimental import pallas as pl
from jax.experimental.pallas import tpu as pltpu
from jax.sharding import PartitionSpec as P

D = 384
HEADS = 6
HEAD = 64
FF = 1536
CLASSES = 1000
CLASS_PAD = 1024
PATCH_IN = 768
PATCHES = 196
SEQ = 197
LAYERS = 3
LANES = 128
TOKENS = 208

eps_norm = 1e-06
smooth = 0.1
step_rate = 20.0
root_half = 0.7071067811865476
inv_root_two_pi = 0.3989422804014327

VMEM_LIMIT = 56 * 1024 * 1024

ROW_VEC = 36
ROW_QKV = ROW_VEC
ROW_OUT = ROW_QKV + 3 * D * D // LANES
ROW_UP = ROW_OUT + D * D // LANES
ROW_DOWN = ROW_UP + D * FF // LANES
ROW_END = ROW_DOWN + D * FF // LANES

OUTER_SHIFT = 24
SMALL_ROWS = 4 * D // LANES + CLASS_PAD // LANES
OROW_POS = (4 * D + CLASSES + OUTER_SHIFT) // LANES
OROW_PATCH = OROW_POS + SEQ * D // LANES
OROW_HEAD = OROW_PATCH + PATCH_IN * D // LANES


def round_up(value, unit):
    return (value + unit - 1) // unit * unit


def bits_of(devices):
    count = devices.bit_length() - 1
    assert 1 << count == devices
    return count


def slot_masks(devices):
    if devices == 32:
        first, second = [], []
        for slot in range(16):
            along_z = (slot & 3) * 8
            near, far = (slot >> 2) & 1, (slot >> 3) & 1
            first.append(along_z + near * 4 + far * 2)
            second.append(along_z + near * 2 + far * 4)
        return (first, second)
    plain = [2 * slot for slot in range(devices // 2)]
    return (plain, plain)


def swap(values, masks, devices):
    pairs = [(i, i ^ masks[i & 1]) for i in range(devices)]
    return lax.ppermute(values, "fsdp", pairs)


def gather_column(shard, devices):
    if devices == 32:
        column = jnp.stack([shard] + [swap(shard, (8 * k, 8 * k), devices) for k in (1, 2, 3)])
        column = jnp.concatenate([column, swap(column, (4, 2), devices)])
        column = jnp.concatenate([column, swap(column, (2, 4), devices)])
    else:
        column = shard[None]
        step = 2
        while step < devices:
            column = jnp.concatenate([column, swap(column, (step, step), devices)])
            step = step * 2
    return (column, swap(column, (1, 1), devices))


def scatter_sum(keep, send, devices):
    total = keep.astype(jnp.float32) + swap(send, (1, 1), devices).astype(jnp.float32)
    if devices == 32:
        low = total[8:].astype(jnp.bfloat16)
        total = total[:8] + swap(low, (2, 4), devices).astype(jnp.float32)
        low = total[4:].astype(jnp.bfloat16)
        total = total[:4] + swap(low, (4, 2), devices).astype(jnp.float32)
        low = total[1:].astype(jnp.bfloat16)
        parts = [swap(low[k - 1], (8 * k, 8 * k), devices).astype(jnp.float32) for k in (1, 2, 3)]
        return total[0] + ((parts[0] + parts[1]) + parts[2])
    while total.shape[0] > 1:
        half = total.shape[0] // 2
        low = total[half:].astype(jnp.bfloat16)
        total = total[:half] + swap(low, (2 * half, 2 * half), devices).astype(jnp.float32)
    return total[0]


def select_mask(core, masks, slot):
    first, second = masks[0][slot], masks[1][slot]
    if first == second:
        return first
    return jnp.where(core == 0, first, second)


def load_shards(mine_ref, theirs_ref, staged, sem, masks, half):
    me = lax.axis_index("fsdp")
    core = lax.rem(me, 2)
    copies = []
    for slot in range(half):
        own = jnp.bitwise_xor(me, select_mask(core, masks, slot))
        other = jnp.bitwise_xor(jnp.bitwise_xor(me, 1), select_mask(1 - core, masks, slot))
        copies.append(pltpu.make_async_copy(mine_ref.at[slot], staged.at[own], sem))
        copies.append(pltpu.make_async_copy(theirs_ref.at[slot], staged.at[other], sem))
    for copy in copies:
        copy.start()
    for copy in copies:
        copy.wait()


def store_shards(keep_ref, send_ref, staged, sem, masks, half):
    me = lax.axis_index("fsdp")
    core = lax.rem(me, 2)
    copies = []
    for slot in range(half):
        own = jnp.bitwise_xor(me, select_mask(core, masks, slot))
        other = jnp.bitwise_xor(jnp.bitwise_xor(me, 1), select_mask(1 - core, masks, slot))
        copies.append(pltpu.make_async_copy(staged.at[own], keep_ref.at[slot], sem))
        copies.append(pltpu.make_async_copy(staged.at[other], send_ref.at[slot], sem))
    for copy in copies:
        copy.start()
    for copy in copies:
        copy.wait()


def start_all(copies):
    for copy in copies:
        copy.start()


def wait_all(copies):
    for copy in copies:
        copy.wait()


def row_vector(ref, row, blocks):
    return jnp.concatenate([ref[row + i : row + i + 1, :] for i in range(blocks)], axis=1)


def put_vector(ref, row, vector):
    for i in range(vector.shape[1] // LANES):
        ref[row + i : row + i + 1, :] = vector[:, i * LANES : (i + 1) * LANES]


def take_matrix(flat, row, height, width):
    blocks = width // LANES
    return [flat[pl.ds(row + c, height, stride=blocks), :] for c in range(blocks)]


def put_block(flat, row, width, block, first_row, first_block):
    blocks = width // LANES
    height = block.shape[0]
    for c in range(block.shape[1] // LANES):
        place = row + first_row * blocks + first_block + c
        flat[pl.ds(place, height, stride=blocks), :] = block[:, c * LANES : (c + 1) * LANES]


def dot_plain(left, right):
    return jnp.dot(left, right, preferred_element_type=jnp.float32)


def contract_rows(left, right):
    return lax.dot_general(
        left, right, (((0,), (0,)), ((), ())), preferred_element_type=jnp.float32
    )


def contract_last(left, right):
    return lax.dot_general(
        left, right, (((1,), (1,)), ((), ())), preferred_element_type=jnp.float32
    )


def norm_parts(values):
    center = values - jnp.mean(values, -1, keepdims=True)
    inverse = lax.rsqrt(jnp.mean(center * center, -1, keepdims=True) + eps_norm)
    return (center * inverse, inverse)


def norm_back(grad_normed, normal, inverse, gain):
    scaled = grad_normed * gain
    return inverse * (
        scaled
        - jnp.mean(scaled, -1, keepdims=True)
        - normal * jnp.mean(scaled * normal, -1, keepdims=True)
    )


def gelu_parts(values):
    near = 1.0 / (1.0 + (0.3275911 * root_half) * jnp.abs(values))
    bell = jnp.exp(-0.5 * values * values)
    series = 1.061405429 * near - 1.453152027
    series = series * near + 1.421413741
    series = series * near - 0.284496736
    series = series * near + 0.254829592
    tail = 0.5 * series * near * bell
    below = jnp.where(values >= 0.0, 1.0 - tail, tail)
    return (values * below, below + values * bell * inv_root_two_pi)


def column_sum(values):
    return jnp.sum(values, 0, keepdims=True)


def forward_kernel(
    masks,
    half,
    rows,
    mine,
    theirs,
    state_ref,
    next_ref,
    vec_out,
    w_qkv_out,
    w_out_out,
    w_up_out,
    w_down_out,
    qkv_out,
    probs_out,
    attended_out,
    mid_out,
    active_out,
    slope_out,
    staged,
    flat,
    w_qkv,
    w_out,
    w_up,
    w_down,
    qkv,
    probs,
    attended,
    mid,
    active,
    slope,
    normed,
    load_sem,
    sems,
):
    load_shards(mine, theirs, staged, load_sem, masks, half)
    for shard in range(2 * half):
        flat[shard * rows : (shard + 1) * rows, :] = staged[shard, :rows, :].astype(jnp.float32)
    weights = (
        (w_qkv, w_qkv_out, ROW_QKV),
        (w_out, w_out_out, ROW_OUT),
        (w_up, w_up_out, ROW_UP),
        (w_down, w_down_out, ROW_DOWN),
    )
    copies = []

    def send(source, target):
        copy = pltpu.make_async_copy(source, target, sems.at[len(copies)])
        copy.start()
        copies.append(copy)

    vec_out[...] = flat[0:ROW_VEC, :]
    for ref, target, row in weights:
        for c, block in enumerate(take_matrix(flat, row, *ref.shape)):
            ref[:, c * LANES : (c + 1) * LANES] = block.astype(jnp.bfloat16)
        send(ref, target)

    blocks = D // LANES
    images_here = state_ref.shape[0] // TOKENS
    gain, bias = row_vector(flat, 0, blocks), row_vector(flat, 3, blocks)
    for image in range(images_here):
        place = slice(image * TOKENS, (image + 1) * TOKENS)
        normal, inverse = norm_parts(state_ref[place, :])
        normed[place, :] = (normal * gain + bias).astype(jnp.bfloat16)
    for part in range(3):
        columns = slice(part * D, (part + 1) * D)
        value = dot_plain(normed[...], w_qkv[:, columns])
        if part != 1:
            value = value + row_vector(flat, 12 if part == 0 else 15, blocks)
        qkv[:, columns] = value.astype(jnp.bfloat16)
    send(qkv, qkv_out)

    left_lane = lax.broadcasted_iota(jnp.int32, (TOKENS, LANES), 1) < HEAD
    real_key = lax.broadcasted_iota(jnp.int32, (TOKENS, TOKENS), 1) < SEQ
    for image in range(images_here):
        place = slice(image * TOKENS, (image + 1) * TOKENS)
        for pair in range(HEADS // 2):
            queries = qkv[place, pair * LANES : (pair + 1) * LANES]
            keys = qkv[place, D + pair * LANES : D + (pair + 1) * LANES]
            values = qkv[place, 2 * D + pair * LANES : 2 * D + (pair + 1) * LANES]
            results = []
            for side in range(2):
                own = left_lane if side == 0 else jnp.logical_not(left_lane)
                head_queries = jnp.where(own, queries, jnp.zeros_like(queries))
                scores = contract_last(head_queries, keys) * HEAD ** (-0.5)
                scores = jnp.where(real_key, scores, -1e30)
                exponent = jnp.exp(scores - jnp.max(scores, -1, keepdims=True))
                prob = exponent * (1.0 / jnp.sum(exponent, -1, keepdims=True))
                probs[image * HEADS + 2 * pair + side] = prob
                results.append(dot_plain(prob.astype(jnp.bfloat16), values))
            joined = jnp.where(left_lane, results[0], results[1])
            attended[place, pair * LANES : (pair + 1) * LANES] = joined.astype(jnp.bfloat16)
    send(probs, probs_out)
    send(attended, attended_out)

    bias_out = row_vector(flat, 18, blocks)
    gain, bias = row_vector(flat, 6, blocks), row_vector(flat, 9, blocks)
    for image in range(images_here):
        place = slice(image * TOKENS, (image + 1) * TOKENS)
        value = state_ref[place, :] + dot_plain(attended[place, :], w_out[...]) + bias_out
        mid[place, :] = value
        normal, inverse = norm_parts(value)
        normed[place, :] = (normal * gain + bias).astype(jnp.bfloat16)
    send(mid, mid_out)
    for part in range(FF // D):
        columns = slice(part * D, (part + 1) * D)
        bias_up = row_vector(flat, 24 + blocks * part, blocks)
        for image in range(images_here):
            place = slice(image * TOKENS, (image + 1) * TOKENS)
            up_value = dot_plain(normed[place, :], w_up[:, columns]) + bias_up
            act, slo = gelu_parts(up_value)
            active[place, columns] = act.astype(jnp.bfloat16)
            slope[place, columns] = slo
    send(active, active_out)
    send(slope, slope_out)
    bias_down = row_vector(flat, 21, blocks)
    for image in range(images_here):
        place = slice(image * TOKENS, (image + 1) * TOKENS)
        next_ref[place, :] = mid[place, :] + dot_plain(active[place, :], w_down[...]) + bias_down
    wait_all(copies)


def matrix_shapes():
    return [(D, 3 * D), (D, D), (D, FF), (FF, D)]


def saved_shapes(tokens_here):
    images_here = tokens_here // TOKENS
    return [
        jax.ShapeDtypeStruct((tokens_here, 3 * D), jnp.bfloat16),
        jax.ShapeDtypeStruct((images_here * HEADS, TOKENS, TOKENS), jnp.float32),
        jax.ShapeDtypeStruct((tokens_here, D), jnp.bfloat16),
        jax.ShapeDtypeStruct((tokens_here, D), jnp.float32),
        jax.ShapeDtypeStruct((tokens_here, FF), jnp.bfloat16),
        jax.ShapeDtypeStruct((tokens_here, FF), jnp.float32),
    ]


def layer_forward(pieces, state, rows):
    mine, theirs = pieces
    half, padded = mine.shape[0], mine.shape[1]
    kernel = functools.partial(forward_kernel, slot_masks(2 * half), half, rows)
    weights = [jax.ShapeDtypeStruct(shape, jnp.bfloat16) for shape in matrix_shapes()]
    large = weights + saved_shapes(state.shape[0])
    any_spec = pl.BlockSpec(memory_space=pl.ANY)
    vmem_spec = pl.BlockSpec(memory_space=pltpu.VMEM)
    outs = pl.pallas_call(
        kernel,
        out_shape=[
            jax.ShapeDtypeStruct(state.shape, jnp.float32),
            jax.ShapeDtypeStruct((ROW_VEC, LANES), jnp.float32),
        ]
        + large,
        in_specs=[any_spec, any_spec, vmem_spec],
        out_specs=[vmem_spec] * 2 + [any_spec] * len(large),
        scratch_shapes=[
            pltpu.VMEM((2 * half, padded, LANES), jnp.bfloat16),
            pltpu.VMEM((round_up(2 * half * rows, 8), LANES), jnp.float32),
        ]
        + [pltpu.VMEM(item.shape, item.dtype) for item in large]
        + [
            pltpu.VMEM(state.shape, jnp.bfloat16),
            pltpu.SemaphoreType.DMA,
            pltpu.SemaphoreType.DMA((len(large),)),
        ],
        compiler_params=pltpu.CompilerParams(vmem_limit_bytes=VMEM_LIMIT),
        name="layer_forward",
    )(mine, theirs, state)
    return (outs[0], outs[1], outs[2:6], outs[6:])


def backward_kernel(
    masks,
    half,
    rows,
    padded,
    grad_ref,
    state_ref,
    vec,
    extra,
    w_qkv_in,
    w_out_in,
    w_up_in,
    w_down_in,
    qkv_in,
    probs_in,
    attended_in,
    mid_in,
    active_in,
    slope_in,
    grad_in_ref,
    keep_ref,
    send_ref,
    w_qkv,
    w_out,
    w_up,
    w_down,
    qkv,
    probs,
    attended,
    mid,
    active,
    slope,
    staged,
    flat,
    grad_low,
    grad_up,
    grad_qkv,
    normed,
    store_sem,
    sems,
):
    pairs = (
        (active_in, active),
        (w_down_in, w_down),
        (slope_in, slope),
        (mid_in, mid),
        (w_up_in, w_up),
        (attended_in, attended),
        (w_out_in, w_out),
        (qkv_in, qkv),
        (probs_in, probs),
        (w_qkv_in, w_qkv),
    )
    copies = [
        pltpu.make_async_copy(source, target, sems.at[i]) for i, (source, target) in enumerate(pairs)
    ]
    start_all(copies)
    blocks = D // LANES
    images_here = grad_ref.shape[0] // TOKENS
    places = [slice(i * TOKENS, (i + 1) * TOKENS) for i in range(images_here)]
    flat[ROW_END:, :] = jnp.zeros((flat.shape[0] - ROW_END, LANES), jnp.float32)

    put_vector(flat, 21, column_sum(grad_ref[...]))
    grad_low[...] = grad_ref[...].astype(jnp.bfloat16)
    copies[0].wait()
    copies[1].wait()
    for part in range(FF // D):
        columns = slice(part * D, (part + 1) * D)
        block = contract_rows(active[:, columns], grad_low[...])
        put_block(flat, ROW_DOWN, D, block, part * D, 0)
    copies[2].wait()
    for part in range(FF // D):
        columns = slice(part * D, (part + 1) * D)
        total = 0.0
        for place in places:
            value = contract_last(grad_low[place, :], w_down[columns, :]) * slope[place, columns]
            total = total + column_sum(value)
            grad_up[place, columns] = value.astype(jnp.bfloat16)
        put_vector(flat, 24 + blocks * part, total)
    copies[3].wait()
    copies[4].wait()
    gain, bias = row_vector(vec, 6, blocks), row_vector(vec, 9, blocks)
    sums = [0.0, 0.0, 0.0]
    for place in places:
        normal, inverse = norm_parts(mid[place, :])
        normed[place, :] = (normal * gain + bias).astype(jnp.bfloat16)
        grad_normed = contract_last(grad_up[place, :], w_up[...])
        sums[0] = sums[0] + column_sum(grad_normed * normal)
        sums[1] = sums[1] + column_sum(grad_normed)
        value = grad_ref[place, :] + norm_back(grad_normed, normal, inverse, gain)
        sums[2] = sums[2] + column_sum(value)
        mid[place, :] = value
        grad_low[place, :] = value.astype(jnp.bfloat16)
    put_vector(flat, 6, sums[0])
    put_vector(flat, 9, sums[1])
    put_vector(flat, 18, sums[2])
    for part in range(FF // D):
        columns = slice(part * D, (part + 1) * D)
        block = contract_rows(normed[...], grad_up[:, columns])
        put_block(flat, ROW_UP, FF, block, 0, blocks * part)

    copies[5].wait()
    copies[6].wait()
    put_block(flat, ROW_OUT, D, contract_rows(attended[...], grad_low[...]), 0, 0)
    for place in places:
        attended[place, :] = contract_last(grad_low[place, :], w_out[...]).astype(jnp.bfloat16)
    copies[7].wait()
    copies[8].wait()
    left_lane = lax.broadcasted_iota(jnp.int32, (TOKENS, LANES), 1) < HEAD
    for pair in range(HEADS // 2):
        sum_query, sum_value = 0.0, 0.0
        for image, place in enumerate(places):
            spans = [slice(i * D + pair * LANES, i * D + (pair + 1) * LANES) for i in range(3)]
            queries, keys, values = [qkv[place, span] for span in spans]
            grad_here = attended[place, pair * LANES : (pair + 1) * LANES]
            results = []
            for side in range(2):
                own = left_lane if side == 0 else jnp.logical_not(left_lane)
                head_grad = jnp.where(own, grad_here, jnp.zeros_like(grad_here))
                prob = probs[image * HEADS + 2 * pair + side]
                grad_probs = contract_last(head_grad, values)
                grad_values = contract_rows(prob.astype(jnp.bfloat16), grad_here)
                inner = jnp.sum(grad_probs * prob, -1, keepdims=True)
                grad_scores = (prob * (grad_probs - inner) * HEAD ** (-0.5)).astype(jnp.bfloat16)
                grad_queries = dot_plain(grad_scores, keys)
                grad_keys = contract_rows(grad_scores, queries)
                results.append((grad_queries, grad_keys, grad_values))
            joined = [jnp.where(left_lane, results[0][i], results[1][i]) for i in range(3)]
            for i in range(3):
                grad_qkv[place, spans[i]] = joined[i].astype(jnp.bfloat16)
            sum_query = sum_query + column_sum(joined[0])
            sum_value = sum_value + column_sum(joined[2])
        put_vector(flat, 12 + pair, sum_query)
        put_vector(flat, 15 + pair, sum_value)
    copies[9].wait()
    gain, bias = row_vector(vec, 0, blocks), row_vector(vec, 3, blocks)
    sums = [0.0, 0.0]
    for place in places:
        normal, inverse = norm_parts(state_ref[place, :])
        normed[place, :] = (normal * gain + bias).astype(jnp.bfloat16)
        grad_normed = contract_last(grad_qkv[place, :], w_qkv[...])
        sums[0] = sums[0] + column_sum(grad_normed * normal)
        sums[1] = sums[1] + column_sum(grad_normed)
        grad_in_ref[place, :] = mid[place, :] + norm_back(grad_normed, normal, inverse, gain)
    put_vector(flat, 0, sums[0])
    put_vector(flat, 3, sums[1])
    for part in range(3):
        columns = slice(part * D, (part + 1) * D)
        block = contract_rows(normed[...], grad_qkv[:, columns])
        put_block(flat, ROW_QKV, 3 * D, block, 0, blocks * part)
    tail = extra[...]
    for shard in range(2 * half):
        staged[shard, :rows, :] = flat[shard * rows : (shard + 1) * rows, :].astype(jnp.bfloat16)
        staged[shard, rows:, :] = tail
    store_shards(keep_ref, send_ref, staged, store_sem, masks, half)


def layer_backward(grad_state, state, vec, weights, saved, extra, rows, padded, devices):
    half = devices // 2
    kernel = functools.partial(backward_kernel, slot_masks(devices), half, rows, padded)
    shape = jax.ShapeDtypeStruct((half, padded, LANES), jnp.bfloat16)
    large = list(weights) + list(saved)
    any_spec = pl.BlockSpec(memory_space=pl.ANY)
    vmem_spec = pl.BlockSpec(memory_space=pltpu.VMEM)
    return pl.pallas_call(
        kernel,
        out_shape=[jax.ShapeDtypeStruct(grad_state.shape, jnp.float32), shape, shape],
        in_specs=[vmem_spec] * 4 + [any_spec] * len(large),
        out_specs=[vmem_spec, any_spec, any_spec],
        scratch_shapes=[pltpu.VMEM(item.shape, item.dtype) for item in large]
        + [
            pltpu.VMEM((2 * half, padded, LANES), jnp.bfloat16),
            pltpu.VMEM((round_up(2 * half * rows, 8), LANES), jnp.float32),
            pltpu.VMEM(grad_state.shape, jnp.bfloat16),
            pltpu.VMEM((grad_state.shape[0], FF), jnp.bfloat16),
            pltpu.VMEM((grad_state.shape[0], 3 * D), jnp.bfloat16),
            pltpu.VMEM(grad_state.shape, jnp.bfloat16),
            pltpu.SemaphoreType.DMA,
            pltpu.SemaphoreType.DMA((len(large),)),
        ],
        compiler_params=pltpu.CompilerParams(vmem_limit_bytes=VMEM_LIMIT),
        name="layer_backward",
    )(grad_state, state, vec, extra, *large)


def embed_kernel(
    masks,
    half,
    rows,
    images,
    mine,
    theirs,
    state_ref,
    small_ref,
    head_ref,
    count_ref,
    staged,
    flat,
    head,
    patch,
    position,
    sem,
):
    load_shards(mine, theirs, staged, sem, masks, half)
    count = jnp.zeros((1, LANES), jnp.float32)
    for shard in range(2 * half):
        flat[shard * rows : (shard + 1) * rows, :] = staged[shard, :rows, :].astype(jnp.float32)
        tail = staged[shard, rows : rows + 2, :].astype(jnp.float32)
        count = count + tail[1:2]
        if shard + 1 < 2 * half:
            later = staged[shard + 1, 0:1, :].astype(jnp.float32)
            carry = tail[0:1] + later
        if shard > 0:
            flat[shard * rows : shard * rows + 1, :] = before
        before = carry
    count_ref[...] = count
    lane = lax.broadcasted_iota(jnp.int32, (24, LANES), 1)
    low = pltpu.roll(flat[0:24, :], LANES - OUTER_SHIFT, 1)
    later = pltpu.roll(flat[1:25, :], LANES - OUTER_SHIFT, 1)
    small = jnp.where(lane < LANES - OUTER_SHIFT, low, later)
    line = lax.broadcasted_iota(jnp.int32, (24, LANES), 0)
    past = (line - 4 * D // LANES) * LANES + lane >= CLASSES
    small_ref[...] = jnp.where(past, 0.0, small)
    blocks = D // LANES
    for c, block in enumerate(take_matrix(flat, OROW_POS, SEQ, D)):
        position[:SEQ, c * LANES : (c + 1) * LANES] = block
    for c, block in enumerate(take_matrix(flat, OROW_PATCH, PATCH_IN, D)):
        patch[:, c * LANES : (c + 1) * LANES] = block.astype(jnp.bfloat16)
    bias_patch = row_vector(small_ref, 3 * blocks, blocks)
    for image in range(images.shape[0]):
        base = image * TOKENS
        state_ref[base + SEQ : base + TOKENS, :] = jnp.zeros((TOKENS - SEQ, D), jnp.float32)
        state_ref[base : base + 1, :] = row_vector(small_ref, 0, blocks) + position[0:1, :]
        value = dot_plain(images[image], patch[...]) + bias_patch
        state_ref[base + 1 : base + SEQ, :] = value + position[1:SEQ, :]
    for p in range(16):
        shift, base = (CLASSES * p) % LANES, OROW_HEAD + (CLASSES * p) // LANES
        part = [flat[pl.ds(base + c, 24, stride=125), :] for c in range(9 if shift else 8)]
        if shift:
            part = [pltpu.roll(block, LANES - shift, 1) for block in part]
        for c in range(8):
            block = jnp.where(lane < LANES - shift, part[c], part[c + 1]) if shift else part[c]
            if c == 7:
                block = jnp.where(lane < CLASSES - 7 * LANES, block, 0.0)
            head[c, pl.ds(p, 24, stride=16), :] = block
    for c in range(8):
        head_ref[:, c * LANES : (c + 1) * LANES] = head[c].astype(jnp.bfloat16)


def embed_images(images, pieces, rows):
    mine, theirs = pieces
    half, padded = mine.shape[0], mine.shape[1]
    kernel = functools.partial(embed_kernel, slot_masks(2 * half), half, rows)
    any_spec = pl.BlockSpec(memory_space=pl.ANY)
    vmem_spec = pl.BlockSpec(memory_space=pltpu.VMEM)
    return pl.pallas_call(
        kernel,
        out_shape=[
            jax.ShapeDtypeStruct((images.shape[0] * TOKENS, D), jnp.float32),
            jax.ShapeDtypeStruct((24, LANES), jnp.float32),
            jax.ShapeDtypeStruct((D, CLASS_PAD), jnp.bfloat16),
            jax.ShapeDtypeStruct((1, LANES), jnp.float32),
        ],
        in_specs=[vmem_spec, any_spec, any_spec],
        out_specs=[vmem_spec] * 4,
        scratch_shapes=[
            pltpu.VMEM((2 * half, padded, LANES), jnp.bfloat16),
            pltpu.VMEM((round_up(2 * half * rows + 1, 8), LANES), jnp.float32),
            pltpu.VMEM((CLASS_PAD // LANES, D, LANES), jnp.float32),
            pltpu.VMEM((PATCH_IN, D), jnp.bfloat16),
            pltpu.VMEM((TOKENS, D), jnp.float32),
            pltpu.SemaphoreType.DMA,
        ],
        compiler_params=pltpu.CompilerParams(vmem_limit_bytes=VMEM_LIMIT),
        name="embed_images",
    )(images, mine, theirs)


def head_kernel(
    labels,
    valid,
    state_ref,
    small,
    w_head,
    count,
    extra_ref,
    grad_ref,
    normed_ref,
    logit_grad_ref,
    vec_ref,
    rows_in,
):
    blocks = D // LANES
    images_here = state_ref.shape[0] // TOKENS
    rows_in[...] = jnp.zeros(rows_in.shape, jnp.float32)
    for image in range(images_here):
        rows_in[image : image + 1, :] = state_ref[image * TOKENS : image * TOKENS + 1, :]
    normal, inverse = norm_parts(rows_in[...])
    gain, bias = row_vector(small, blocks, blocks), row_vector(small, 2 * blocks, blocks)
    normed_final = (normal * gain + bias).astype(jnp.bfloat16)
    bias_head = row_vector(small, 4 * blocks, CLASS_PAD // LANES)
    logits = dot_plain(normed_final, w_head[...]) + bias_head
    shape = logits.shape
    column = lax.broadcasted_iota(jnp.int32, shape, 1)
    line = lax.broadcasted_iota(jnp.int32, (shape[0], 1), 0)
    real = column < CLASSES
    label = jnp.zeros((shape[0], 1), jnp.int32)
    present = jnp.zeros((shape[0], 1), jnp.float32)
    for image in range(images_here):
        label = jnp.where(line == image, labels[image], label)
        present = jnp.where(line == image, valid[image].astype(jnp.float32), present)
    top_logit = jnp.max(jnp.where(real, logits, -1e30), -1, keepdims=True)
    exponent = jnp.where(real, jnp.exp(jnp.minimum(logits - top_logit, 0.0)), 0.0)
    total_exp = jnp.sum(exponent, -1, keepdims=True)
    log_total = jnp.log(total_exp) + top_logit
    target = jnp.where(column == label, 1.0 - smooth + smooth / CLASSES, smooth / CLASSES)
    target = jnp.where(real, target, 0.0)
    per_image = log_total - jnp.sum(target * logits, -1, keepdims=True)
    loss_here = jnp.sum(present * per_image, 0, keepdims=True)
    loss_high = loss_here.astype(jnp.bfloat16).astype(jnp.float32)
    loss_mid = (loss_here - loss_high).astype(jnp.bfloat16).astype(jnp.float32)
    loss_low = loss_here - loss_high - loss_mid
    me = lax.axis_index("fsdp")
    spare = extra_ref.shape
    place = lax.broadcasted_iota(jnp.int32, spare, 0) * LANES
    place = place + lax.broadcasted_iota(jnp.int32, spare, 1)
    extra = jnp.where(place == 3 * me, loss_high, 0.0)
    extra = jnp.where(place == 3 * me + 1, loss_mid, extra)
    extra_ref[...] = jnp.where(place == 3 * me + 2, loss_low, extra).astype(jnp.bfloat16)

    scale = present * (1.0 / count[0:1, 0:1])
    grad_logits = (exponent * (1.0 / total_exp) - target) * scale
    grad_logits_low = grad_logits.astype(jnp.bfloat16)
    grad_normed = contract_last(grad_logits_low, w_head[...])
    grad_final = norm_back(grad_normed, normal, inverse, gain)
    grad_ref[...] = jnp.zeros(grad_ref.shape, jnp.float32)
    for image in range(images_here):
        grad_ref[image * TOKENS : image * TOKENS + 1, :] = grad_final[image : image + 1, :]
    normed_ref[...] = jnp.where(line < images_here, normed_final, jnp.zeros_like(normed_final))
    logit_grad_ref[...] = grad_logits_low
    vec_ref[...] = jnp.zeros(vec_ref.shape, jnp.float32)
    put_vector(vec_ref, blocks, column_sum(grad_normed * normal))
    put_vector(vec_ref, 2 * blocks, column_sum(grad_normed))
    put_vector(vec_ref, 4 * blocks, column_sum(grad_logits))


def head_step(labels, valid, state, small, w_head, count, spare):
    smem_spec = pl.BlockSpec(memory_space=pltpu.SMEM)
    vmem_spec = pl.BlockSpec(memory_space=pltpu.VMEM)
    lines = 16
    return pl.pallas_call(
        head_kernel,
        out_shape=[
            jax.ShapeDtypeStruct((spare, LANES), jnp.bfloat16),
            jax.ShapeDtypeStruct(state.shape, jnp.float32),
            jax.ShapeDtypeStruct((lines, D), jnp.bfloat16),
            jax.ShapeDtypeStruct((lines, CLASS_PAD), jnp.bfloat16),
            jax.ShapeDtypeStruct((24, LANES), jnp.float32),
        ],
        in_specs=[smem_spec, smem_spec] + [vmem_spec] * 4,
        out_specs=[vmem_spec] * 5,
        scratch_shapes=[pltpu.VMEM((lines, D), jnp.float32)],
        compiler_params=pltpu.CompilerParams(vmem_limit_bytes=VMEM_LIMIT),
        name="head_step",
    )(labels, valid, state, small, w_head, count)


def outer_grad_kernel(
    masks,
    half,
    rows,
    padded,
    grad_ref,
    images,
    normed_final,
    logit_grad,
    vec,
    keep_ref,
    send_ref,
    staged,
    flat,
    head,
    small,
    sem,
):
    blocks = D // LANES
    images_here = images.shape[0]
    bases = [image * TOKENS for image in range(images_here)]
    small[...] = vec[...]
    token = sum(grad_ref[base : base + 1, :] for base in bases)
    put_vector(small, 0, token)
    total = sum(grad_ref[base : base + SEQ, :] for base in bases)
    put_block(flat, OROW_POS, D, total, 0, 0)
    put_vector(small, 3 * blocks, column_sum(total) - token)
    lane = lax.broadcasted_iota(jnp.int32, (24, LANES), 1)
    line = lax.broadcasted_iota(jnp.int32, (24, LANES), 0)
    moved = pltpu.roll(small[...], OUTER_SHIFT, 1)
    above = jnp.where(line == 0, 0.0, pltpu.roll(moved, 1, 0))
    moved = jnp.where(lane < OUTER_SHIFT, above, moved)
    flat[0:OROW_POS, :] = moved[0:OROW_POS]
    grads = [grad_ref[base + 1 : base + SEQ, :].astype(jnp.bfloat16) for base in bases]
    for part in range(PATCH_IN // D):
        columns = slice(part * D, (part + 1) * D)
        block = sum(contract_rows(images[i, :, columns], grads[i]) for i in range(images_here))
        put_block(flat, OROW_PATCH, D, block, part * D, 0)
    for c in range(8):
        head[c] = contract_rows(normed_final[...], logit_grad[:, c * LANES : (c + 1) * LANES])

    def block_of(p, c):
        return head[c, pl.ds(p, 24, stride=16), :]

    for i in range(125):
        p, start = LANES * i // CLASSES, LANES * i % CLASSES
        c, shift = start // LANES, start % LANES
        value = block_of(p, c)
        if shift:
            value = pltpu.roll(value, LANES - shift, 1)
            if c < 7:
                later = pltpu.roll(block_of(p, c + 1), LANES - shift, 1)
                value = jnp.where(lane < LANES - shift, value, later)
        here = CLASSES - start
        if here < LANES:
            value = jnp.where(lane < here, value, pltpu.roll(block_of(p + 1, 0), here, 1))
        flat[pl.ds(OROW_HEAD + i, 24, stride=125), :] = value
    end = OROW_HEAD + 24 * 125
    flat[end:, :] = jnp.zeros((flat.shape[0] - end, LANES), jnp.float32)
    for shard in range(2 * half):
        staged[shard, : rows + 1, :] = flat[shard * rows : (shard + 1) * rows + 1, :].astype(
            jnp.bfloat16
        )
    store_shards(keep_ref, send_ref, staged, sem, masks, half)


def outer_backward(grad_state, images, normed_final, logit_grad, vec, rows, padded, devices):
    half = devices // 2
    kernel = functools.partial(outer_grad_kernel, slot_masks(devices), half, rows, padded)
    shape = jax.ShapeDtypeStruct((half, padded, LANES), jnp.bfloat16)
    return pl.pallas_call(
        kernel,
        out_shape=[shape, shape],
        in_specs=[pl.BlockSpec(memory_space=pltpu.VMEM)] * 5,
        out_specs=[pl.BlockSpec(memory_space=pl.ANY)] * 2,
        scratch_shapes=[
            pltpu.VMEM((2 * half, padded, LANES), jnp.bfloat16),
            pltpu.VMEM((round_up(2 * half * rows + 1, 8), LANES), jnp.float32),
            pltpu.VMEM((CLASS_PAD // LANES, D, LANES), jnp.float32),
            pltpu.VMEM((24, LANES), jnp.float32),
            pltpu.SemaphoreType.DMA,
        ],
        compiler_params=pltpu.CompilerParams(vmem_limit_bytes=VMEM_LIMIT),
        name="outer_backward",
    )(grad_state, images, normed_final, logit_grad, vec)


def nesterov(params, momentum, average, grads):
    momentum_new = 0.5 * momentum + grads
    params_new = params - step_rate * (grads + 0.5 * momentum_new)
    return (params_new, momentum_new, 0.5 * average + 0.5 * params_new)


def shards(
    images,
    labels,
    valid,
    layer_params,
    layer_momentum,
    layer_average,
    outer_params,
    outer_momentum,
    outer_average,
):
    devices = lax.axis_size("fsdp")
    layer_rows = layer_params.shape[1] // LANES
    layer_padded = round_up(layer_rows + 3 * devices // LANES + 1, 16)
    outer_rows = outer_params.shape[0] // LANES
    outer_padded = round_up(outer_rows + 2, 16)

    count_row = jnp.pad(jnp.sum(valid).astype(jnp.float32).reshape(1), (0, LANES - 1)).reshape(1, LANES)
    outer_shard = jnp.pad(outer_params, (OUTER_SHIFT, LANES - OUTER_SHIFT)).reshape(-1, LANES)
    outer_shard = jnp.concatenate([outer_shard, count_row]).astype(jnp.bfloat16)
    outer_shard = jnp.pad(outer_shard, ((0, outer_padded - outer_rows - 2), (0, 0)))
    layer_shards = []
    for layer_index in range(LAYERS):
        shard = layer_params[layer_index].reshape(layer_rows, LANES).astype(jnp.bfloat16)
        layer_shards.append(jnp.pad(shard, ((0, layer_padded - layer_rows), (0, 0))))

    state, small, w_head, counts = embed_images(
        images, gather_column(outer_shard, devices), outer_rows
    )
    image_count = counts[0, 0]
    kept = []
    for layer_index in range(LAYERS):
        pieces = gather_column(layer_shards[layer_index], devices)
        state_next, vec, weights, saved = layer_forward(pieces, state, layer_rows)
        kept.append((state, vec, weights, saved))
        state = state_next
    extra, grad_state, normed_final, logit_grad, vec_grad = head_step(
        labels, valid, state, small, w_head, counts, layer_padded - layer_rows
    )
    layer_grads = [None] * LAYERS
    for layer_index in reversed(range(LAYERS)):
        state, vec, weights, saved = kept[layer_index]
        grad_state, keep, send = layer_backward(
            grad_state, state, vec, weights, saved, extra, layer_rows, layer_padded, devices
        )
        summed = scatter_sum(keep, send, devices)
        layer_grads[layer_index] = summed[:layer_rows].reshape(-1)
        if layer_index == LAYERS - 1:
            loss_sum = jnp.sum(summed[layer_rows:])
    keep, send = outer_backward(
        grad_state, images, normed_final, logit_grad, vec_grad, outer_rows, outer_padded, devices
    )
    summed = scatter_sum(keep, send, devices)
    outer_grad = summed[: outer_rows + 1].reshape(-1)[OUTER_SHIFT : OUTER_SHIFT + outer_rows * LANES]
    layer_grad = jnp.stack(layer_grads)
    layer_new, layer_mom_new, layer_avg_new = nesterov(
        layer_params, layer_momentum, layer_average, layer_grad
    )
    outer_new, outer_mom_new, outer_avg_new = nesterov(
        outer_params, outer_momentum, outer_average, outer_grad
    )
    return (
        loss_sum,
        image_count,
        layer_new,
        layer_mom_new,
        layer_avg_new,
        outer_new,
        outer_mom_new,
        outer_avg_new,
    )


def solution(mesh):
    return jax.shard_map(
        shards,
        mesh=mesh,
        in_specs=(
            P("fsdp", None, None),
            P("fsdp"),
            P("fsdp"),
            P(None, "fsdp"),
            P(None, "fsdp"),
            P(None, "fsdp"),
            P("fsdp"),
            P("fsdp"),
            P("fsdp"),
        ),
        out_specs=(
            P(),
            P(),
            P(None, "fsdp"),
            P(None, "fsdp"),
            P(None, "fsdp"),
            P("fsdp"),
            P("fsdp"),
            P("fsdp"),
        ),
        check_vma=False,
    )
```

```python
import functools

import jax
import jax.numpy as jnp
import numpy as np
from jax import lax
from jax.experimental import pallas as pl
from jax.experimental.pallas import tpu as pltpu
from jax.sharding import PartitionSpec as P

D = 384
HEADS = 6
HEAD = 64
FF = 1536
CLASSES = 1000
CLASS_PAD = 1024
PATCH_IN = 768
PATCHES = 196
SEQ = 197
LAYERS = 3
LANES = 128
TOKENS = 208

eps_norm = 1e-06
smooth = 0.1
step_rate = 20.0
root_half = 0.7071067811865476
inv_root_two_pi = 0.3989422804014327

VMEM_LIMIT = 26 * 1024 * 1024


def cost(microseconds):
    return pl.CostEstimate(
        flops=int(microseconds * 1e9), bytes_accessed=int(microseconds * 3.5e6), transcendentals=0
    )


ROW_VEC = 36
ROW_QKV = ROW_VEC
ROW_OUT = ROW_QKV + 3 * D * D // LANES
ROW_UP = ROW_OUT + D * D // LANES
ROW_DOWN = ROW_UP + D * FF // LANES
ROW_END = ROW_DOWN + D * FF // LANES

OUTER_SHIFT = 24
SMALL_ROWS = 4 * D // LANES + CLASS_PAD // LANES
OROW_POS = (4 * D + CLASSES + OUTER_SHIFT) // LANES
OROW_PATCH = OROW_POS + SEQ * D // LANES
OROW_HEAD = OROW_PATCH + PATCH_IN * D // LANES


def round_up(value, unit):
    return (value + unit - 1) // unit * unit


def bits_of(devices):
    count = devices.bit_length() - 1
    assert 1 << count == devices
    return count


def slot_masks(devices):
    if devices == 32:
        first, second = [], []
        for slot in range(16):
            along_z = (slot & 3) * 8
            near, far = (slot >> 2) & 1, (slot >> 3) & 1
            first.append(along_z + near * 4 + far * 2)
            second.append(along_z + near * 2 + far * 4)
        return (first, second)
    plain = [2 * slot for slot in range(devices // 2)]
    return (plain, plain)


def swap(values, masks, devices):
    pairs = [(i, i ^ masks[i & 1]) for i in range(devices)]
    return lax.ppermute(values, "fsdp", pairs)


def after(value, *earlier):
    return lax.optimization_barrier((value, earlier))[0]


class Gather:
    def __init__(self, devices):
        self.devices = devices
        self.parts = []

    def along_z(self, shard):
        if self.devices == 32:
            masks = [(8 * k, 8 * k) for k in (1, 2, 3)]
            self.column = jnp.stack([shard] + [swap(shard, mask, self.devices) for mask in masks])
        else:
            self.column = shard[None]
            for step in range(1, bits_of(self.devices) - 2):
                self.double((1 << step, 1 << step))
        return self.column

    def double(self, masks):
        self.column = jnp.concatenate([self.column, swap(self.column, masks, self.devices)])
        return self.column

    def near(self):
        top = self.devices // 4
        return self.double((4, 2) if self.devices == 32 else (top, top))

    def far(self):
        self.first = swap(self.column, (1, 1), self.devices)
        top = self.devices // 2
        self.last = swap(self.column, (2, 4) if self.devices == 32 else (top, top), self.devices)
        return self.last

    def across(self):
        second = swap(self.last, (1, 1), self.devices)
        return (self.column, self.last, self.first, second)


class Scatter:
    def __init__(self, keep, send, devices):
        self.devices = devices
        self.keep = keep
        self.send = send

    def across(self):
        other = swap(self.send, (1, 1), self.devices)
        self.total = self.keep.astype(jnp.float32) + other.astype(jnp.float32)
        return self.total

    def halve(self, masks):
        half = self.total.shape[0] // 2
        low = self.total[half:].astype(jnp.bfloat16)
        self.total = self.total[:half] + swap(low, masks, self.devices).astype(jnp.float32)
        return self.total

    def far(self):
        top = self.devices // 2
        return self.halve((2, 4) if self.devices == 32 else (top, top))

    def near(self):
        top = self.devices // 4
        return self.halve((4, 2) if self.devices == 32 else (top, top))

    def along_z(self):
        if self.devices == 32:
            low = self.total[1:].astype(jnp.bfloat16)
            parts = [swap(low[k - 1], (8 * k, 8 * k), self.devices) for k in (1, 2, 3)]
            parts = [part.astype(jnp.float32) for part in parts]
            return self.total[0] + ((parts[0] + parts[1]) + parts[2])
        for step in range(bits_of(self.devices) - 3, 0, -1):
            self.halve((1 << step, 1 << step))
        return self.total[0]


def select_mask(core, masks, slot):
    first, second = masks[0][slot], masks[1][slot]
    if first == second:
        return first
    return jnp.where(core == 0, first, second)


def owner_pairs(masks, half):
    me = lax.axis_index("fsdp")
    core = lax.rem(me, 2)
    other = jnp.bitwise_xor(me, 1)
    return [
        (
            jnp.bitwise_xor(me, select_mask(core, masks, slot)),
            jnp.bitwise_xor(other, select_mask(1 - core, masks, slot)),
        )
        for slot in range(half)
    ]


def load_shards(pieces, flat, masks, half, rows):
    quarter = half // 2
    for slot, owners in enumerate(owner_pairs(masks, half)):
        pair = (pieces[0], pieces[2]) if slot < quarter else (pieces[1], pieces[3])
        for piece, owner in zip(pair, owners):
            value = piece[slot % quarter, :rows, :].astype(jnp.float32)
            flat[pl.ds(owner * rows, rows), :] = value


def store_shards(keep_ref, send_ref, flat, masks, half, rows, stride):
    for slot, owners in enumerate(owner_pairs(masks, half)):
        for ref, owner in zip((keep_ref, send_ref), owners):
            ref[slot, :rows, :] = flat[pl.ds(owner * stride, rows), :].astype(jnp.bfloat16)


def row_vector(ref, row, blocks):
    return jnp.concatenate([ref[row + i : row + i + 1, :] for i in range(blocks)], axis=1)


def put_vector(ref, row, vector):
    for i in range(vector.shape[1] // LANES):
        ref[row + i : row + i + 1, :] = vector[:, i * LANES : (i + 1) * LANES]


def take_matrix(flat, row, height, width):
    blocks = width // LANES
    return [flat[pl.ds(row + c, height, stride=blocks), :] for c in range(blocks)]


def put_block(flat, row, width, block, first_row, first_block):
    blocks = width // LANES
    height = block.shape[0]
    for c in range(block.shape[1] // LANES):
        place = row + first_row * blocks + first_block + c
        flat[pl.ds(place, height, stride=blocks), :] = block[:, c * LANES : (c + 1) * LANES]


def dot_plain(left, right):
    return jnp.dot(left, right, preferred_element_type=jnp.float32)


def contract_rows(left, right):
    return lax.dot_general(
        left, right, (((0,), (0,)), ((), ())), preferred_element_type=jnp.float32
    )


def contract_last(left, right):
    return lax.dot_general(
        left, right, (((1,), (1,)), ((), ())), preferred_element_type=jnp.float32
    )


def norm_parts(values):
    center = values - jnp.mean(values, -1, keepdims=True)
    inverse = lax.rsqrt(jnp.mean(center * center, -1, keepdims=True) + eps_norm)
    return (center * inverse, inverse)


def norm_back(grad_normed, normal, inverse, gain):
    scaled = grad_normed * gain
    return inverse * (
        scaled
        - jnp.mean(scaled, -1, keepdims=True)
        - normal * jnp.mean(scaled * normal, -1, keepdims=True)
    )


def gelu_parts(values):
    near = 1.0 / (1.0 + (0.3275911 * root_half) * jnp.abs(values))
    bell = jnp.exp(-0.5 * values * values)
    series = 1.061405429 * near - 1.453152027
    series = series * near + 1.421413741
    series = series * near - 0.284496736
    series = series * near + 0.254829592
    tail = 0.5 * series * near * bell
    below = jnp.where(values >= 0.0, 1.0 - tail, tail)
    return (values * below, below + values * bell * inv_root_two_pi)


def column_sum(values):
    return jnp.sum(values, 0, keepdims=True)


def unpack_kernel(
    masks,
    half,
    rows,
    own_first,
    own_last,
    other_first,
    other_last,
    vec,
    w_qkv,
    w_out,
    w_up,
    w_down,
    flat,
):
    load_shards((own_first, own_last, other_first, other_last), flat, masks, half, rows)
    vec[...] = flat[0:ROW_VEC, :]
    for ref, row in ((w_qkv, ROW_QKV), (w_out, ROW_OUT), (w_up, ROW_UP), (w_down, ROW_DOWN)):
        for c, block in enumerate(take_matrix(flat, row, *ref.shape)):
            ref[:, c * LANES : (c + 1) * LANES] = block.astype(jnp.bfloat16)


def call_kernel(kernel, name, microseconds, outs, scratch, *args, smem=0):
    spaces = [pltpu.SMEM] * smem + [pltpu.VMEM] * (len(args) - smem)
    return pl.pallas_call(
        kernel,
        out_shape=[jax.ShapeDtypeStruct(shape, kind) for shape, kind in outs],
        in_specs=[pl.BlockSpec(memory_space=space) for space in spaces],
        out_specs=[pl.BlockSpec(memory_space=pltpu.VMEM)] * len(outs),
        scratch_shapes=[pltpu.VMEM(shape, kind) for shape, kind in scratch],
        compiler_params=pltpu.CompilerParams(vmem_limit_bytes=VMEM_LIMIT),
        cost_estimate=cost(microseconds),
        name=name,
    )(*args)


LOW = jnp.bfloat16
WIDE = jnp.float32
MATRICES = [(D, 3 * D), (D, D), (D, FF), (FF, D)]


def layer_unpack(pieces, rows):
    half = 2 * pieces[0].shape[0]
    kernel = functools.partial(unpack_kernel, slot_masks(2 * half), half, rows)
    outs = [((ROW_VEC, LANES), WIDE)] + [(shape, LOW) for shape in MATRICES]
    scratch = [((round_up(2 * half * rows, 8), LANES), WIDE)]
    vec, *weights = call_kernel(kernel, "layer_unpack", 3, outs, scratch, *pieces)
    return (vec, weights)


def forward_kernel(
    state_ref,
    vec,
    w_qkv,
    w_out,
    w_up,
    w_down,
    next_ref,
    qkv,
    probs,
    attended,
    mid,
    active,
    slope,
    normed,
):
    blocks = D // LANES
    images_here = state_ref.shape[0] // TOKENS
    gain, bias = row_vector(vec, 0, blocks), row_vector(vec, 3, blocks)
    for image in range(images_here):
        place = slice(image * TOKENS, (image + 1) * TOKENS)
        normal, inverse = norm_parts(state_ref[place, :])
        normed[place, :] = (normal * gain + bias).astype(jnp.bfloat16)
    for part in range(3):
        columns = slice(part * D, (part + 1) * D)
        value = dot_plain(normed[...], w_qkv[:, columns])
        if part != 1:
            value = value + row_vector(vec, 12 if part == 0 else 15, blocks)
        qkv[:, columns] = value.astype(jnp.bfloat16)

    left_lane = lax.broadcasted_iota(jnp.int32, (TOKENS, LANES), 1) < HEAD
    real_key = lax.broadcasted_iota(jnp.int32, (TOKENS, TOKENS), 1) < SEQ
    for image in range(images_here):
        place = slice(image * TOKENS, (image + 1) * TOKENS)
        for pair in range(HEADS // 2):
            queries = qkv[place, pair * LANES : (pair + 1) * LANES]
            keys = qkv[place, D + pair * LANES : D + (pair + 1) * LANES]
            values = qkv[place, 2 * D + pair * LANES : 2 * D + (pair + 1) * LANES]
            results = []
            for side in range(2):
                own = left_lane if side == 0 else jnp.logical_not(left_lane)
                head_queries = jnp.where(own, queries, jnp.zeros_like(queries))
                scores = contract_last(head_queries, keys) * HEAD ** (-0.5)
                scores = jnp.where(real_key, scores, -1e30)
                exponent = jnp.exp(scores - jnp.max(scores, -1, keepdims=True))
                prob = exponent * (1.0 / jnp.sum(exponent, -1, keepdims=True))
                probs[image * HEADS + 2 * pair + side] = prob
                results.append(dot_plain(prob.astype(jnp.bfloat16), values))
            joined = jnp.where(left_lane, results[0], results[1])
            attended[place, pair * LANES : (pair + 1) * LANES] = joined.astype(jnp.bfloat16)

    bias_out = row_vector(vec, 18, blocks)
    gain, bias = row_vector(vec, 6, blocks), row_vector(vec, 9, blocks)
    for image in range(images_here):
        place = slice(image * TOKENS, (image + 1) * TOKENS)
        value = state_ref[place, :] + dot_plain(attended[place, :], w_out[...]) + bias_out
        mid[place, :] = value
        normal, inverse = norm_parts(value)
        normed[place, :] = (normal * gain + bias).astype(jnp.bfloat16)
    for part in range(FF // D):
        columns = slice(part * D, (part + 1) * D)
        bias_up = row_vector(vec, 24 + blocks * part, blocks)
        for image in range(images_here):
            place = slice(image * TOKENS, (image + 1) * TOKENS)
            up_value = dot_plain(normed[place, :], w_up[:, columns]) + bias_up
            act, slo = gelu_parts(up_value)
            active[place, columns] = act.astype(jnp.bfloat16)
            slope[place, columns] = slo
    bias_down = row_vector(vec, 21, blocks)
    for image in range(images_here):
        place = slice(image * TOKENS, (image + 1) * TOKENS)
        next_ref[place, :] = mid[place, :] + dot_plain(active[place, :], w_down[...]) + bias_down


def layer_forward(state, vec, weights):
    tokens_here = state.shape[0]
    images_here = tokens_here // TOKENS
    outs = [
        (state.shape, WIDE),
        ((tokens_here, 3 * D), LOW),
        ((images_here * HEADS, TOKENS, TOKENS), WIDE),
        ((tokens_here, D), LOW),
        ((tokens_here, D), WIDE),
        ((tokens_here, FF), LOW),
        ((tokens_here, FF), WIDE),
    ]
    scratch = [(state.shape, LOW)]
    state_next, *saved = call_kernel(
        forward_kernel, "layer_forward", 9, outs, scratch, state, vec, *weights
    )
    return (state_next, saved)


def backward_kernel(
    grad_ref,
    state_ref,
    vec,
    w_qkv,
    w_out,
    w_up,
    w_down,
    qkv,
    probs,
    mid,
    slope,
    grad_in_ref,
    sums_ref,
    grad_up,
    normed_two,
    grad_low,
    grad_qkv,
    normed_one,
    attended,
    grad_mid,
):
    blocks = D // LANES
    images_here = grad_ref.shape[0] // TOKENS
    places = [slice(i * TOKENS, (i + 1) * TOKENS) for i in range(images_here)]
    put_vector(sums_ref, 21, column_sum(grad_ref[...]))
    grad_low[...] = grad_ref[...].astype(jnp.bfloat16)
    for part in range(FF // D):
        columns = slice(part * D, (part + 1) * D)
        total = 0.0
        for place in places:
            value = contract_last(grad_low[place, :], w_down[columns, :]) * slope[place, columns]
            total = total + column_sum(value)
            grad_up[place, columns] = value.astype(jnp.bfloat16)
        put_vector(sums_ref, 24 + blocks * part, total)
    gain, bias = row_vector(vec, 6, blocks), row_vector(vec, 9, blocks)
    sums = [0.0, 0.0, 0.0]
    for place in places:
        normal, inverse = norm_parts(mid[place, :])
        normed_two[place, :] = (normal * gain + bias).astype(jnp.bfloat16)
        grad_normed = contract_last(grad_up[place, :], w_up[...])
        sums[0] = sums[0] + column_sum(grad_normed * normal)
        sums[1] = sums[1] + column_sum(grad_normed)
        value = grad_ref[place, :] + norm_back(grad_normed, normal, inverse, gain)
        sums[2] = sums[2] + column_sum(value)
        grad_mid[place, :] = value
        grad_low[place, :] = value.astype(jnp.bfloat16)
    put_vector(sums_ref, 6, sums[0])
    put_vector(sums_ref, 9, sums[1])
    put_vector(sums_ref, 18, sums[2])
    for place in places:
        attended[place, :] = contract_last(grad_low[place, :], w_out[...]).astype(jnp.bfloat16)
    left_lane = lax.broadcasted_iota(jnp.int32, (TOKENS, LANES), 1) < HEAD
    for pair in range(HEADS // 2):
        sum_query, sum_value = 0.0, 0.0
        for image, place in enumerate(places):
            spans = [slice(i * D + pair * LANES, i * D + (pair + 1) * LANES) for i in range(3)]
            queries, keys, values = [qkv[place, span] for span in spans]
            grad_here = attended[place, pair * LANES : (pair + 1) * LANES]
            results = []
            for side in range(2):
                own = left_lane if side == 0 else jnp.logical_not(left_lane)
                head_grad = jnp.where(own, grad_here, jnp.zeros_like(grad_here))
                prob = probs[image * HEADS + 2 * pair + side]
                grad_probs = contract_last(head_grad, values)
                grad_values = contract_rows(prob.astype(jnp.bfloat16), grad_here)
                inner = jnp.sum(grad_probs * prob, -1, keepdims=True)
                grad_scores = (prob * (grad_probs - inner) * HEAD ** (-0.5)).astype(jnp.bfloat16)
                grad_queries = dot_plain(grad_scores, keys)
                grad_keys = contract_rows(grad_scores, queries)
                results.append((grad_queries, grad_keys, grad_values))
            joined = [jnp.where(left_lane, results[0][i], results[1][i]) for i in range(3)]
            for i in range(3):
                grad_qkv[place, spans[i]] = joined[i].astype(jnp.bfloat16)
            sum_query = sum_query + column_sum(joined[0])
            sum_value = sum_value + column_sum(joined[2])
        put_vector(sums_ref, 12 + pair, sum_query)
        put_vector(sums_ref, 15 + pair, sum_value)
    gain, bias = row_vector(vec, 0, blocks), row_vector(vec, 3, blocks)
    sums = [0.0, 0.0]
    for place in places:
        normal, inverse = norm_parts(state_ref[place, :])
        normed_one[place, :] = (normal * gain + bias).astype(jnp.bfloat16)
        grad_normed = contract_last(grad_qkv[place, :], w_qkv[...])
        sums[0] = sums[0] + column_sum(grad_normed * normal)
        sums[1] = sums[1] + column_sum(grad_normed)
        grad_in_ref[place, :] = grad_mid[place, :] + norm_back(grad_normed, normal, inverse, gain)
    put_vector(sums_ref, 0, sums[0])
    put_vector(sums_ref, 3, sums[1])


def layer_backward(grad_state, state, vec, weights, saved):
    qkv, probs, attended, mid, active, slope = saved
    tokens_here = grad_state.shape[0]
    outs = [(grad_state.shape, WIDE), ((ROW_VEC, LANES), WIDE)]
    outs = outs + [((tokens_here, width), LOW) for width in (FF, D, D, 3 * D, D)]
    scratch = [(grad_state.shape, LOW), (grad_state.shape, WIDE)]
    args = [grad_state, state, vec, *weights, qkv, probs, mid, slope]
    outs = call_kernel(backward_kernel, "layer_backward", 9, outs, scratch, *args)
    grad_in, sums, up_low, normed_two, mid_low, qkv_low, normed_one = outs
    factors = (active, normed_two, up_low, attended, mid_low, normed_one, qkv_low)
    return (grad_in, (sums, grad_state, *factors))


def weight_grad_kernel(
    masks,
    half,
    rows,
    extra,
    sums_ref,
    grad_ref,
    active,
    normed_two,
    grad_up,
    attended,
    mid_low,
    normed_one,
    grad_qkv,
    keep_ref,
    send_ref,
    grad_low,
    flat,
):
    blocks = D // LANES
    flat[0:ROW_VEC, :] = sums_ref[...]
    flat[ROW_END:, :] = jnp.zeros((flat.shape[0] - ROW_END, LANES), jnp.float32)
    grad_low[...] = grad_ref[...].astype(jnp.bfloat16)
    for part in range(FF // D):
        columns = slice(part * D, (part + 1) * D)
        block = contract_rows(active[:, columns], grad_low[...])
        put_block(flat, ROW_DOWN, D, block, part * D, 0)
    for part in range(FF // D):
        columns = slice(part * D, (part + 1) * D)
        block = contract_rows(normed_two[...], grad_up[:, columns])
        put_block(flat, ROW_UP, FF, block, 0, blocks * part)
    put_block(flat, ROW_OUT, D, contract_rows(attended[...], mid_low[...]), 0, 0)
    for part in range(3):
        columns = slice(part * D, (part + 1) * D)
        block = contract_rows(normed_one[...], grad_qkv[:, columns])
        put_block(flat, ROW_QKV, 3 * D, block, 0, blocks * part)
    store_shards(keep_ref, send_ref, flat, masks, half, rows, rows)
    tail = extra[...]
    for slot in range(half):
        keep_ref[slot, rows:, :] = tail
        send_ref[slot, rows:, :] = tail


def weight_grads(factors, extra, rows, padded, devices):
    half = devices // 2
    kernel = functools.partial(weight_grad_kernel, slot_masks(devices), half, rows)
    outs = [((half, padded, LANES), LOW)] * 2
    scratch = [(factors[1].shape, LOW), ((round_up(2 * half * rows, 8), LANES), WIDE)]
    keep, send = call_kernel(kernel, "weight_grads", 4, outs, scratch, extra, *factors)
    return Scatter(keep, send, devices)


def embed_kernel(
    masks,
    half,
    rows,
    images,
    own_first,
    own_last,
    other_first,
    other_last,
    state_ref,
    small_ref,
    head_ref,
    count_ref,
    flat,
    head,
    patch,
    position,
):
    pieces = (own_first, own_last, other_first, other_last)
    quarter = half // 2
    count = jnp.zeros((1, LANES), jnp.float32)
    for shard in range(2 * half + 1):
        flat[shard * rows : shard * rows + 1, :] = jnp.zeros((1, LANES), jnp.float32)
    for slot, owners in enumerate(owner_pairs(masks, half)):
        pair = (pieces[0], pieces[2]) if slot < quarter else (pieces[1], pieces[3])
        for piece, owner in zip(pair, owners):
            value = piece[slot % quarter, : rows + 2, :].astype(jnp.float32)
            flat[pl.ds(owner * rows + 1, rows - 1), :] = value[1:rows]
            flat[pl.ds(owner * rows, 1), :] += value[0:1]
            flat[pl.ds((owner + 1) * rows, 1), :] += value[rows : rows + 1]
            count = count + value[rows + 1 : rows + 2]
    count_ref[...] = count
    lane = lax.broadcasted_iota(jnp.int32, (24, LANES), 1)
    low = pltpu.roll(flat[0:24, :], LANES - OUTER_SHIFT, 1)
    later = pltpu.roll(flat[1:25, :], LANES - OUTER_SHIFT, 1)
    small = jnp.where(lane < LANES - OUTER_SHIFT, low, later)
    line = lax.broadcasted_iota(jnp.int32, (24, LANES), 0)
    past = (line - 4 * D // LANES) * LANES + lane >= CLASSES
    small_ref[...] = jnp.where(past, 0.0, small)
    blocks = D // LANES
    for c, block in enumerate(take_matrix(flat, OROW_POS, SEQ, D)):
        position[:SEQ, c * LANES : (c + 1) * LANES] = block
    for c, block in enumerate(take_matrix(flat, OROW_PATCH, PATCH_IN, D)):
        patch[:, c * LANES : (c + 1) * LANES] = block.astype(jnp.bfloat16)
    bias_patch = row_vector(small_ref, 3 * blocks, blocks)
    for image in range(images.shape[0]):
        base = image * TOKENS
        state_ref[base + SEQ : base + TOKENS, :] = jnp.zeros((TOKENS - SEQ, D), jnp.float32)
        state_ref[base : base + 1, :] = row_vector(small_ref, 0, blocks) + position[0:1, :]
        value = dot_plain(images[image], patch[...]) + bias_patch
        state_ref[base + 1 : base + SEQ, :] = value + position[1:SEQ, :]
    for p in range(16):
        shift, base = (CLASSES * p) % LANES, OROW_HEAD + (CLASSES * p) // LANES
        part = [flat[pl.ds(base + c, 24, stride=125), :] for c in range(9 if shift else 8)]
        if shift:
            part = [pltpu.roll(block, LANES - shift, 1) for block in part]
        for c in range(8):
            block = jnp.where(lane < LANES - shift, part[c], part[c + 1]) if shift else part[c]
            if c == 7:
                block = jnp.where(lane < CLASSES - 7 * LANES, block, 0.0)
            head[c, pl.ds(p, 24, stride=16), :] = block
    for c in range(8):
        head_ref[:, c * LANES : (c + 1) * LANES] = head[c].astype(jnp.bfloat16)


def embed_images(images, pieces, rows):
    half = 2 * pieces[0].shape[0]
    kernel = functools.partial(embed_kernel, slot_masks(2 * half), half, rows)
    outs = [
        ((images.shape[0] * TOKENS, D), WIDE),
        ((24, LANES), WIDE),
        ((D, CLASS_PAD), LOW),
        ((1, LANES), WIDE),
    ]
    scratch = [
        ((round_up(2 * half * rows + 1, 8), LANES), WIDE),
        ((CLASS_PAD // LANES, D, LANES), WIDE),
        ((PATCH_IN, D), LOW),
        ((TOKENS, D), WIDE),
    ]
    return call_kernel(kernel, "embed_images", 4, outs, scratch, images, *pieces)


def head_kernel(
    labels,
    valid,
    state_ref,
    small,
    w_head,
    count,
    extra_ref,
    grad_ref,
    normed_ref,
    logit_grad_ref,
    vec_ref,
    rows_in,
):
    blocks = D // LANES
    images_here = state_ref.shape[0] // TOKENS
    rows_in[...] = jnp.zeros(rows_in.shape, jnp.float32)
    for image in range(images_here):
        rows_in[image : image + 1, :] = state_ref[image * TOKENS : image * TOKENS + 1, :]
    normal, inverse = norm_parts(rows_in[...])
    gain, bias = row_vector(small, blocks, blocks), row_vector(small, 2 * blocks, blocks)
    normed_final = (normal * gain + bias).astype(jnp.bfloat16)
    bias_head = row_vector(small, 4 * blocks, CLASS_PAD // LANES)
    logits = dot_plain(normed_final, w_head[...]) + bias_head
    shape = logits.shape
    column = lax.broadcasted_iota(jnp.int32, shape, 1)
    line = lax.broadcasted_iota(jnp.int32, (shape[0], 1), 0)
    real = column < CLASSES
    label = jnp.zeros((shape[0], 1), jnp.int32)
    present = jnp.zeros((shape[0], 1), jnp.float32)
    for image in range(images_here):
        label = jnp.where(line == image, labels[image], label)
        present = jnp.where(line == image, valid[image].astype(jnp.float32), present)
    top_logit = jnp.max(jnp.where(real, logits, -1e30), -1, keepdims=True)
    exponent = jnp.where(real, jnp.exp(jnp.minimum(logits - top_logit, 0.0)), 0.0)
    total_exp = jnp.sum(exponent, -1, keepdims=True)
    log_total = jnp.log(total_exp) + top_logit
    target = jnp.where(column == label, 1.0 - smooth + smooth / CLASSES, smooth / CLASSES)
    target = jnp.where(real, target, 0.0)
    per_image = log_total - jnp.sum(target * logits, -1, keepdims=True)
    loss_here = jnp.sum(present * per_image, 0, keepdims=True)
    loss_high = loss_here.astype(jnp.bfloat16).astype(jnp.float32)
    loss_mid = (loss_here - loss_high).astype(jnp.bfloat16).astype(jnp.float32)
    loss_low = loss_here - loss_high - loss_mid
    me = lax.axis_index("fsdp")
    spare = extra_ref.shape
    place = lax.broadcasted_iota(jnp.int32, spare, 0) * LANES
    place = place + lax.broadcasted_iota(jnp.int32, spare, 1)
    extra = jnp.where(place == 3 * me, loss_high, 0.0)
    extra = jnp.where(place == 3 * me + 1, loss_mid, extra)
    extra_ref[...] = jnp.where(place == 3 * me + 2, loss_low, extra).astype(jnp.bfloat16)

    scale = present * (1.0 / count[0:1, 0:1])
    grad_logits = (exponent * (1.0 / total_exp) - target) * scale
    grad_logits_low = grad_logits.astype(jnp.bfloat16)
    grad_normed = contract_last(grad_logits_low, w_head[...])
    grad_final = norm_back(grad_normed, normal, inverse, gain)
    grad_ref[...] = jnp.zeros(grad_ref.shape, jnp.float32)
    for image in range(images_here):
        grad_ref[image * TOKENS : image * TOKENS + 1, :] = grad_final[image : image + 1, :]
    normed_ref[...] = jnp.where(line < images_here, normed_final, jnp.zeros_like(normed_final))
    logit_grad_ref[...] = grad_logits_low
    vec_ref[...] = jnp.zeros(vec_ref.shape, jnp.float32)
    put_vector(vec_ref, blocks, column_sum(grad_normed * normal))
    put_vector(vec_ref, 2 * blocks, column_sum(grad_normed))
    put_vector(vec_ref, 4 * blocks, column_sum(grad_logits))


def head_step(labels, valid, state, small, w_head, count, spare):
    lines = 16
    outs = [
        ((spare, LANES), LOW),
        (state.shape, WIDE),
        ((lines, D), LOW),
        ((lines, CLASS_PAD), LOW),
        ((24, LANES), WIDE),
    ]
    args = (labels, valid, state, small, w_head, count)
    return call_kernel(head_kernel, "head_step", 2, outs, [((lines, D), WIDE)], *args, smem=2)


def outer_grad_kernel(
    masks,
    half,
    rows,
    grad_ref,
    images,
    normed_final,
    logit_grad,
    vec,
    keep_ref,
    send_ref,
    flat,
    head,
    small,
):
    blocks = D // LANES
    images_here = images.shape[0]
    bases = [image * TOKENS for image in range(images_here)]
    small[...] = vec[...]
    token = sum(grad_ref[base : base + 1, :] for base in bases)
    put_vector(small, 0, token)
    total = sum(grad_ref[base : base + SEQ, :] for base in bases)
    put_block(flat, OROW_POS, D, total, 0, 0)
    put_vector(small, 3 * blocks, column_sum(total) - token)
    lane = lax.broadcasted_iota(jnp.int32, (24, LANES), 1)
    line = lax.broadcasted_iota(jnp.int32, (24, LANES), 0)
    moved = pltpu.roll(small[...], OUTER_SHIFT, 1)
    above = jnp.where(line == 0, 0.0, pltpu.roll(moved, 1, 0))
    moved = jnp.where(lane < OUTER_SHIFT, above, moved)
    flat[0:OROW_POS, :] = moved[0:OROW_POS]
    grads = [grad_ref[base + 1 : base + SEQ, :].astype(jnp.bfloat16) for base in bases]
    for part in range(PATCH_IN // D):
        columns = slice(part * D, (part + 1) * D)
        block = sum(contract_rows(images[i, :, columns], grads[i]) for i in range(images_here))
        put_block(flat, OROW_PATCH, D, block, part * D, 0)
    for c in range(8):
        head[c] = contract_rows(normed_final[...], logit_grad[:, c * LANES : (c + 1) * LANES])

    def block_of(p, c):
        return head[c, pl.ds(p, 24, stride=16), :]

    for i in range(125):
        p, start = LANES * i // CLASSES, LANES * i % CLASSES
        c, shift = start // LANES, start % LANES
        value = block_of(p, c)
        if shift:
            value = pltpu.roll(value, LANES - shift, 1)
            if c < 7:
                later = pltpu.roll(block_of(p, c + 1), LANES - shift, 1)
                value = jnp.where(lane < LANES - shift, value, later)
        here = CLASSES - start
        if here < LANES:
            value = jnp.where(lane < here, value, pltpu.roll(block_of(p + 1, 0), here, 1))
        flat[pl.ds(OROW_HEAD + i, 24, stride=125), :] = value
    end = OROW_HEAD + 24 * 125
    flat[end:, :] = jnp.zeros((flat.shape[0] - end, LANES), jnp.float32)
    store_shards(keep_ref, send_ref, flat, masks, half, rows + 1, rows)


def outer_backward(grad_state, images, normed_final, logit_grad, vec, rows, padded, devices):
    half = devices // 2
    kernel = functools.partial(outer_grad_kernel, slot_masks(devices), half, rows)
    outs = [((half, padded, LANES), LOW)] * 2
    scratch = [
        ((round_up(2 * half * rows + 1, 8), LANES), WIDE),
        ((CLASS_PAD // LANES, D, LANES), WIDE),
        ((24, LANES), WIDE),
    ]
    args = (grad_state, images, normed_final, logit_grad, vec)
    keep, send = call_kernel(kernel, "outer_backward", 4, outs, scratch, *args)
    return Scatter(keep, send, devices)


def nesterov(params, momentum, average, grads):
    momentum_new = 0.5 * momentum + grads
    params_new = params - step_rate * (grads + 0.5 * momentum_new)
    return (params_new, momentum_new, 0.5 * average + 0.5 * params_new)


def shards(
    images,
    labels,
    valid,
    layer_params,
    layer_momentum,
    layer_average,
    outer_params,
    outer_momentum,
    outer_average,
):
    devices = lax.axis_size("fsdp")
    layer_rows = layer_params.shape[1] // LANES
    layer_padded = round_up(layer_rows + 3 * devices // LANES + 1, 16)
    outer_rows = outer_params.shape[0] // LANES
    outer_padded = round_up(outer_rows + 2, 16)

    count_row = jnp.pad(jnp.sum(valid).astype(jnp.float32).reshape(1), (0, LANES - 1)).reshape(1, LANES)
    outer_shard = jnp.pad(outer_params, (OUTER_SHIFT, LANES - OUTER_SHIFT)).reshape(-1, LANES)
    outer_shard = jnp.concatenate([outer_shard, count_row]).astype(jnp.bfloat16)
    outer_shard = jnp.pad(outer_shard, ((0, outer_padded - outer_rows - 2), (0, 0)))
    layer_shards = []
    for layer_index in range(LAYERS):
        shard = layer_params[layer_index].reshape(layer_rows, LANES).astype(jnp.bfloat16)
        layer_shards.append(jnp.pad(shard, ((0, layer_padded - layer_rows), (0, 0))))

    outer, *layers = [Gather(devices) for _ in range(1 + LAYERS)]
    outer.along_z(outer_shard)
    layers[0].along_z(layer_shards[0])
    outer.near()
    outer.far()
    layers[0].column = after(layers[0].column, outer.column)
    layers[0].near()
    outer_pieces = outer.across()
    layers[0].column = after(layers[0].column, outer_pieces[1])
    layers[0].far()
    layers[1].along_z(after(layer_shards[1], layers[0].column))
    state, small, w_head, counts = embed_images(images, outer_pieces, outer_rows)
    image_count = counts[0, 0]
    layers[0].last = after(layers[0].last, state)
    pieces = layers[0].across()
    layers[1].column = after(layers[1].column, layers[0].last)
    layers[1].near()
    layers[2].along_z(after(layer_shards[2], layers[1].column, pieces[1]))
    kept = []
    for layer_index in range(LAYERS):
        vec, weights = layer_unpack(pieces, layer_rows)
        if layer_index + 1 < LAYERS:
            ahead = layers[layer_index + 1]
            ahead.column = after(ahead.column, vec)
            ahead.far()
            if layer_index + 2 < LAYERS:
                later = layers[layer_index + 2]
                later.column = after(later.column, vec, ahead.column)
                later.near()
            state = after(state, ahead.column)
        state_next, saved = layer_forward(state, vec, weights)
        kept.append((state, vec, weights, saved))
        state = state_next
        if layer_index + 1 < LAYERS:
            ahead.last = after(ahead.last, state)
            pieces = ahead.across()
    extra, grad_state, normed_final, logit_grad, vec_grad = head_step(
        labels, valid, state, small, w_head, counts, layer_padded - layer_rows
    )

    def backward(layer_index, grad_state):
        return layer_backward(grad_state, *kept[layer_index])

    def packed(factors):
        return weight_grads(factors, extra, layer_rows, layer_padded, devices)

    sums = [None] * LAYERS
    grad_state, rest = backward(2, grad_state)
    sums[2] = packed(rest)
    sums[2].across()
    grad_state = after(grad_state, sums[2].send)
    grad_state, (first, *rest) = backward(1, grad_state)
    sums[2].total = after(sums[2].total, grad_state)
    first = after(first, sums[2].total)
    sums[2].far()
    sums[1] = packed((first, *rest))
    grad_state = after(grad_state, sums[2].total, sums[1].send)
    sums[2].near()
    sums[1].across()
    grad_state, (first, *rest) = backward(0, grad_state)
    sums[1].total = after(sums[1].total, grad_state)
    first = after(first, sums[2].total, sums[1].total)
    layer_sum_two = sums[2].along_z()
    sums[1].far()
    sums[0] = packed((first, *rest))
    grad_state = after(grad_state, layer_sum_two, sums[1].total, sums[0].send)
    sums[1].near()
    sums[0].across()
    outer_sum = outer_backward(
        grad_state, images, normed_final, logit_grad, vec_grad, outer_rows, outer_padded, devices
    )
    sums[0].total = after(sums[0].total, outer_sum.send)
    sums[0].far()
    outer_sum.across()
    layer_sum_one = sums[1].along_z()
    outer_sum.total = after(outer_sum.total, layer_sum_one)
    outer_sum.far()
    sums[0].near()
    outer_sum.total = after(outer_sum.total, sums[0].total)
    outer_sum.near()
    layer_summed = [sums[0].along_z(), layer_sum_one, layer_sum_two]
    outer_summed = outer_sum.along_z()
    loss_sum = jnp.sum(layer_summed[2][layer_rows:])
    layer_grads = [summed[:layer_rows].reshape(-1) for summed in layer_summed]
    outer_grad = outer_summed[: outer_rows + 1].reshape(-1)
    outer_grad = outer_grad[OUTER_SHIFT : OUTER_SHIFT + outer_rows * LANES]
    layer_grad = jnp.stack(layer_grads)
    layer_new, layer_mom_new, layer_avg_new = nesterov(
        layer_params, layer_momentum, layer_average, layer_grad
    )
    outer_new, outer_mom_new, outer_avg_new = nesterov(
        outer_params, outer_momentum, outer_average, outer_grad
    )
    return (
        loss_sum,
        image_count,
        layer_new,
        layer_mom_new,
        layer_avg_new,
        outer_new,
        outer_mom_new,
        outer_avg_new,
    )


def solution(mesh):
    return jax.shard_map(
        shards,
        mesh=mesh,
        in_specs=(
            P("fsdp", None, None),
            P("fsdp"),
            P("fsdp"),
            P(None, "fsdp"),
            P(None, "fsdp"),
            P(None, "fsdp"),
            P("fsdp"),
            P("fsdp"),
            P("fsdp"),
        ),
        out_specs=(
            P(),
            P(),
            P(None, "fsdp"),
            P(None, "fsdp"),
            P(None, "fsdp"),
            P("fsdp"),
            P("fsdp"),
            P("fsdp"),
        ),
        check_vma=False,
    )
```

```python
import functools

import jax
import jax.numpy as jnp
import numpy as np
from jax import lax
from jax.experimental import pallas as pl
from jax.experimental.pallas import tpu as pltpu
from jax.sharding import PartitionSpec as P

D = 384
HEADS = 6
HEAD = 64
FF = 1536
CLASSES = 1000
CLASS_PAD = 1024
PATCH_IN = 768
PATCHES = 196
SEQ = 197
LAYERS = 3
LANES = 128
TOKENS = 208

eps_norm = 1e-06
smooth = 0.1
step_rate = 20.0
root_half = 0.7071067811865476
inv_root_two_pi = 0.3989422804014327

MIB = 1024 * 1024


def cost(microseconds):
    return pl.CostEstimate(
        flops=int(microseconds * 1e9), bytes_accessed=int(microseconds * 3.5e6), transcendentals=0
    )


ROW_VEC = 36
ROW_QKV = ROW_VEC
ROW_OUT = ROW_QKV + 3 * D * D // LANES
ROW_UP = ROW_OUT + D * D // LANES
ROW_DOWN = ROW_UP + D * FF // LANES
ROW_END = ROW_DOWN + D * FF // LANES

OUTER_SHIFT = 24
SMALL_ROWS = 4 * D // LANES + CLASS_PAD // LANES
OROW_POS = (4 * D + CLASSES + OUTER_SHIFT) // LANES
OROW_PATCH = OROW_POS + SEQ * D // LANES
OROW_HEAD = OROW_PATCH + PATCH_IN * D // LANES


def round_up(value, unit):
    return (value + unit - 1) // unit * unit


def bits_of(devices):
    count = devices.bit_length() - 1
    assert 1 << count == devices
    return count


def steps_of(plan, devices):
    if devices != 32:
        return [[(1 << bit, 1 << bit)] for bit in range(1, bits_of(devices))]
    kinds = {"z": [(8, 8), (16, 16), (24, 24)], "near": [(4, 2)], "far": [(2, 4)]}
    return [kinds[name] for name in plan]


Z_FIRST = ("z", "near", "far")
Z_SECOND = ("near", "z", "far")
LAST_PLAN = Z_FIRST


def slot_masks(plan, devices):
    masks = [(0, 0)]
    for partners in steps_of(plan, devices):
        masks = masks + [(a ^ p, b ^ q) for p, q in partners for a, b in masks]
    return tuple(zip(*masks))


def swap(values, masks, devices):
    pairs = [(i, i ^ masks[i & 1]) for i in range(devices)]
    return lax.ppermute(values, "fsdp", pairs)


def fence_kernel(token, out):
    out[...] = token[...]


class Order:
    def __init__(self, value):
        self.token = jnp.zeros((8, LANES), jnp.float32)
        self.latest = value

    def begin(self, value):
        value, self.latest, self.token = lax.optimization_barrier(
            (value, self.latest, self.token)
        )
        return value

    def end(self, value):
        self.latest = value
        return value

    def fence(self, microseconds=0.5):
        self.begin(())
        self.token = pl.pallas_call(
            fence_kernel,
            out_shape=jax.ShapeDtypeStruct((8, LANES), jnp.float32),
            in_specs=[pl.BlockSpec(memory_space=pltpu.VMEM)],
            out_specs=pl.BlockSpec(memory_space=pltpu.VMEM),
            compiler_params=pltpu.CompilerParams(vmem_limit_bytes=MIB),
            cost_estimate=cost(microseconds),
            name="fence",
        )(self.token)


class Gather:
    def __init__(self, shard, plan, devices, order):
        self.devices = devices
        self.order = order
        self.steps = steps_of(plan, devices)
        self.column = shard[None]

    def start(self):
        while len(self.steps) > 3:
            self.exchange()
            self.take()
        self.exchange()

    def exchange(self):
        self.column = self.order.begin(self.column)
        partners = self.steps.pop(0) if self.steps else [(1, 1)]
        self.arriving = [swap(self.column, masks, self.devices) for masks in partners]

    def take(self):
        first, *rest = self.arriving
        self.column = jnp.concatenate([self.column, self.order.begin(first)] + rest)
        self.order.end(self.column)

    def take_across(self):
        return (self.column, self.order.end(self.order.begin(self.arriving[0])))


class Scatter:
    def __init__(self, keep, send, plan, devices, order):
        self.devices = devices
        self.order = order
        self.steps = [[(1, 1)]] + steps_of(plan, devices)[::-1]
        self.total = keep
        self.low = [send]
        self.starts = 0

    def start(self):
        self.exchange()
        self.starts = self.starts + 1
        while self.starts == 4 and self.steps:
            self.take()
            self.exchange()

    def exchange(self):
        partners = self.steps.pop(0)
        low = self.order.begin(self.low)
        self.arriving = [swap(part, masks, self.devices) for part, masks in zip(low, partners)]

    def take(self):
        first, *rest = self.arriving
        parts = [part.astype(jnp.float32) for part in [self.order.begin(first)] + rest]
        total = self.total.astype(jnp.float32)
        if len(parts) == 3:
            total = total + ((parts[0] + parts[1]) + parts[2])
        else:
            total = total + parts[0]
        if not self.steps:
            self.total = self.order.end(total[0])
            return
        groups = 1 + len(self.steps[0])
        size = total.shape[0] // groups
        self.total = total[:size]
        sent = total[size:].astype(jnp.bfloat16)
        self.low = [sent[i * size : (i + 1) * size] for i in range(groups - 1)]
        self.order.end(sent)


def select_mask(core, masks, slot):
    first, second = masks[0][slot], masks[1][slot]
    if first == second:
        return first
    return jnp.where(core == 0, first, second)


def owner_pairs(masks, half):
    me = lax.axis_index("fsdp")
    core = lax.rem(me, 2)
    other = jnp.bitwise_xor(me, 1)
    return [
        (
            jnp.bitwise_xor(me, select_mask(core, masks, slot)),
            jnp.bitwise_xor(other, select_mask(1 - core, masks, slot)),
        )
        for slot in range(half)
    ]


def load_shards(pieces, flat, masks, half, base, rows):
    for slot, owners in enumerate(owner_pairs(masks, half)):
        for piece, owner in zip(pieces, owners):
            value = piece[slot, base : base + rows, :].astype(jnp.float32)
            flat[pl.ds(owner * rows, rows), :] = value


def store_shards(keep_ref, send_ref, flat, masks, half, rows, stride):
    for slot, owners in enumerate(owner_pairs(masks, half)):
        for ref, owner in zip((keep_ref, send_ref), owners):
            ref[slot, :rows, :] = flat[pl.ds(owner * stride, rows), :].astype(jnp.bfloat16)


def row_vector(ref, row, blocks):
    return jnp.concatenate([ref[row + i : row + i + 1, :] for i in range(blocks)], axis=1)


def put_vector(ref, row, vector):
    for i in range(vector.shape[1] // LANES):
        ref[row + i : row + i + 1, :] = vector[:, i * LANES : (i + 1) * LANES]


def take_matrix(flat, row, height, width):
    blocks = width // LANES
    return [flat[pl.ds(row + c, height, stride=blocks), :] for c in range(blocks)]


def put_block(flat, row, width, block, first_row, first_block):
    blocks = width // LANES
    height = block.shape[0]
    for c in range(block.shape[1] // LANES):
        place = row + first_row * blocks + first_block + c
        flat[pl.ds(place, height, stride=blocks), :] = block[:, c * LANES : (c + 1) * LANES]


def dot_plain(left, right):
    return jnp.dot(left, right, preferred_element_type=jnp.float32)


def contract_rows(left, right):
    return lax.dot_general(
        left, right, (((0,), (0,)), ((), ())), preferred_element_type=jnp.float32
    )


def contract_last(left, right):
    return lax.dot_general(
        left, right, (((1,), (1,)), ((), ())), preferred_element_type=jnp.float32
    )


def norm_parts(values):
    center = values - jnp.mean(values, -1, keepdims=True)
    inverse = lax.rsqrt(jnp.mean(center * center, -1, keepdims=True) + eps_norm)
    return (center * inverse, inverse)


def norm_back(grad_normed, normal, inverse, gain):
    scaled = grad_normed * gain
    return inverse * (
        scaled
        - jnp.mean(scaled, -1, keepdims=True)
        - normal * jnp.mean(scaled * normal, -1, keepdims=True)
    )


def gelu_parts(values):
    near = 1.0 / (1.0 + (0.3275911 * root_half) * jnp.abs(values))
    bell = jnp.exp(-0.5 * values * values)
    series = 1.061405429 * near - 1.453152027
    series = series * near + 1.421413741
    series = series * near - 0.284496736
    series = series * near + 0.254829592
    tail = 0.5 * series * near * bell
    below = jnp.where(values >= 0.0, 1.0 - tail, tail)
    return (values * below, below + values * bell * inv_root_two_pi)


def column_sum(values):
    return jnp.sum(values, 0, keepdims=True)


def unpack_kernel(
    masks,
    half,
    base,
    rows,
    count_row,
    mine,
    theirs,
    vec,
    count_ref,
    w_qkv,
    w_out,
    w_up,
    w_down,
    flat,
):
    pieces = (mine, theirs)
    load_shards(pieces, flat, masks, half, base, rows)
    vec[...] = flat[0:ROW_VEC, :]
    count = jnp.zeros((1, LANES), jnp.float32)
    for slot in range(half):
        for piece in pieces:
            count = count + piece[slot, count_row : count_row + 1, :].astype(jnp.float32)
    count_ref[...] = count
    for ref, row in ((w_qkv, ROW_QKV), (w_out, ROW_OUT), (w_up, ROW_UP), (w_down, ROW_DOWN)):
        for c, block in enumerate(take_matrix(flat, row, *ref.shape)):
            ref[:, c * LANES : (c + 1) * LANES] = block.astype(jnp.bfloat16)


def call_kernel(kernel, name, microseconds, megabytes, outs, scratch, *args, smem=0):
    spaces = [pltpu.SMEM] * smem + [pltpu.VMEM] * (len(args) - smem)
    return pl.pallas_call(
        kernel,
        out_shape=[jax.ShapeDtypeStruct(shape, kind) for shape, kind in outs],
        in_specs=[pl.BlockSpec(memory_space=space) for space in spaces],
        out_specs=[pl.BlockSpec(memory_space=pltpu.VMEM)] * len(outs),
        scratch_shapes=[pltpu.VMEM(shape, kind) for shape, kind in scratch],
        compiler_params=pltpu.CompilerParams(vmem_limit_bytes=megabytes * MIB),
        cost_estimate=cost(0.5),
        name=name,
    )(*args)


LOW = jnp.bfloat16
WIDE = jnp.float32
MATRICES = [(D, 3 * D), (D, D), (D, FF), (FF, D)]


def layer_unpack(pieces, plan, base, rows):
    half = pieces[0].shape[0]
    kernel = functools.partial(
        unpack_kernel, slot_masks(plan, 2 * half), half, base, rows, base + rows
    )
    outs = [((ROW_VEC, LANES), WIDE), ((1, LANES), WIDE)] + [(shape, LOW) for shape in MATRICES]
    scratch = [((round_up(2 * half * rows, 8), LANES), WIDE)]
    vec, count, *weights = call_kernel(kernel, "layer_unpack", 3, 10, outs, scratch, *pieces)
    return (vec, weights, count)


def forward_kernel(
    state_ref,
    vec,
    w_qkv,
    w_out,
    w_up,
    w_down,
    next_ref,
    qkv,
    probs,
    attended,
    mid,
    active,
    slope,
    normed,
):
    blocks = D // LANES
    images_here = state_ref.shape[0] // TOKENS
    gain, bias = row_vector(vec, 0, blocks), row_vector(vec, 3, blocks)
    for image in range(images_here):
        place = slice(image * TOKENS, (image + 1) * TOKENS)
        normal, inverse = norm_parts(state_ref[place, :])
        normed[place, :] = (normal * gain + bias).astype(jnp.bfloat16)
    for part in range(3):
        columns = slice(part * D, (part + 1) * D)
        value = dot_plain(normed[...], w_qkv[:, columns])
        if part != 1:
            value = value + row_vector(vec, 12 if part == 0 else 15, blocks)
        qkv[:, columns] = value.astype(jnp.bfloat16)

    left_lane = lax.broadcasted_iota(jnp.int32, (TOKENS, LANES), 1) < HEAD
    real_key = lax.broadcasted_iota(jnp.int32, (TOKENS, TOKENS), 1) < SEQ
    for image in range(images_here):
        place = slice(image * TOKENS, (image + 1) * TOKENS)
        for pair in range(HEADS // 2):
            queries = qkv[place, pair * LANES : (pair + 1) * LANES]
            keys = qkv[place, D + pair * LANES : D + (pair + 1) * LANES]
            values = qkv[place, 2 * D + pair * LANES : 2 * D + (pair + 1) * LANES]
            results = []
            for side in range(2):
                own = left_lane if side == 0 else jnp.logical_not(left_lane)
                head_queries = jnp.where(own, queries, jnp.zeros_like(queries))
                scores = contract_last(head_queries, keys) * HEAD ** (-0.5)
                scores = jnp.where(real_key, scores, -1e30)
                exponent = jnp.exp(scores - jnp.max(scores, -1, keepdims=True))
                prob = exponent * (1.0 / jnp.sum(exponent, -1, keepdims=True))
                probs[image * HEADS + 2 * pair + side] = prob
                results.append(dot_plain(prob.astype(jnp.bfloat16), values))
            joined = jnp.where(left_lane, results[0], results[1])
            attended[place, pair * LANES : (pair + 1) * LANES] = joined.astype(jnp.bfloat16)

    bias_out = row_vector(vec, 18, blocks)
    gain, bias = row_vector(vec, 6, blocks), row_vector(vec, 9, blocks)
    for image in range(images_here):
        place = slice(image * TOKENS, (image + 1) * TOKENS)
        value = state_ref[place, :] + dot_plain(attended[place, :], w_out[...]) + bias_out
        mid[place, :] = value
        normal, inverse = norm_parts(value)
        normed[place, :] = (normal * gain + bias).astype(jnp.bfloat16)
    for part in range(FF // D):
        columns = slice(part * D, (part + 1) * D)
        bias_up = row_vector(vec, 24 + blocks * part, blocks)
        for image in range(images_here):
            place = slice(image * TOKENS, (image + 1) * TOKENS)
            up_value = dot_plain(normed[place, :], w_up[:, columns]) + bias_up
            act, slo = gelu_parts(up_value)
            active[place, columns] = act.astype(jnp.bfloat16)
            slope[place, columns] = slo
    bias_down = row_vector(vec, 21, blocks)
    for image in range(images_here):
        place = slice(image * TOKENS, (image + 1) * TOKENS)
        next_ref[place, :] = mid[place, :] + dot_plain(active[place, :], w_down[...]) + bias_down


def layer_forward(state, vec, weights):
    tokens_here = state.shape[0]
    images_here = tokens_here // TOKENS
    outs = [
        (state.shape, WIDE),
        ((tokens_here, 3 * D), LOW),
        ((images_here * HEADS, TOKENS, TOKENS), WIDE),
        ((tokens_here, D), LOW),
        ((tokens_here, D), WIDE),
        ((tokens_here, FF), LOW),
        ((tokens_here, FF), WIDE),
    ]
    scratch = [(state.shape, LOW)]
    state_next, *saved = call_kernel(
        forward_kernel, "layer_forward", 7, 8, outs, scratch, state, vec, *weights
    )
    return (state_next, saved)


def backward_kernel(
    grad_ref,
    state_ref,
    vec,
    w_qkv,
    w_out,
    w_up,
    w_down,
    qkv,
    probs,
    mid,
    slope,
    grad_in_ref,
    sums_ref,
    grad_up,
    normed_two,
    grad_low,
    grad_qkv,
    normed_one,
    attended,
    grad_mid,
):
    blocks = D // LANES
    images_here = grad_ref.shape[0] // TOKENS
    places = [slice(i * TOKENS, (i + 1) * TOKENS) for i in range(images_here)]
    put_vector(sums_ref, 21, column_sum(grad_ref[...]))
    grad_low[...] = grad_ref[...].astype(jnp.bfloat16)
    for part in range(FF // D):
        columns = slice(part * D, (part + 1) * D)
        total = 0.0
        for place in places:
            value = contract_last(grad_low[place, :], w_down[columns, :]) * slope[place, columns]
            total = total + column_sum(value)
            grad_up[place, columns] = value.astype(jnp.bfloat16)
        put_vector(sums_ref, 24 + blocks * part, total)
    gain, bias = row_vector(vec, 6, blocks), row_vector(vec, 9, blocks)
    sums = [0.0, 0.0, 0.0]
    for place in places:
        normal, inverse = norm_parts(mid[place, :])
        normed_two[place, :] = (normal * gain + bias).astype(jnp.bfloat16)
        grad_normed = contract_last(grad_up[place, :], w_up[...])
        sums[0] = sums[0] + column_sum(grad_normed * normal)
        sums[1] = sums[1] + column_sum(grad_normed)
        value = grad_ref[place, :] + norm_back(grad_normed, normal, inverse, gain)
        sums[2] = sums[2] + column_sum(value)
        grad_mid[place, :] = value
        grad_low[place, :] = value.astype(jnp.bfloat16)
    put_vector(sums_ref, 6, sums[0])
    put_vector(sums_ref, 9, sums[1])
    put_vector(sums_ref, 18, sums[2])
    for place in places:
        attended[place, :] = contract_last(grad_low[place, :], w_out[...]).astype(jnp.bfloat16)
    left_lane = lax.broadcasted_iota(jnp.int32, (TOKENS, LANES), 1) < HEAD
    for pair in range(HEADS // 2):
        sum_query, sum_value = 0.0, 0.0
        for image, place in enumerate(places):
            spans = [slice(i * D + pair * LANES, i * D + (pair + 1) * LANES) for i in range(3)]
            queries, keys, values = [qkv[place, span] for span in spans]
            grad_here = attended[place, pair * LANES : (pair + 1) * LANES]
            results = []
            for side in range(2):
                own = left_lane if side == 0 else jnp.logical_not(left_lane)
                head_grad = jnp.where(own, grad_here, jnp.zeros_like(grad_here))
                prob = probs[image * HEADS + 2 * pair + side]
                grad_probs = contract_last(head_grad, values)
                grad_values = contract_rows(prob.astype(jnp.bfloat16), grad_here)
                inner = jnp.sum(grad_probs * prob, -1, keepdims=True)
                grad_scores = (prob * (grad_probs - inner) * HEAD ** (-0.5)).astype(jnp.bfloat16)
                grad_queries = dot_plain(grad_scores, keys)
                grad_keys = contract_rows(grad_scores, queries)
                results.append((grad_queries, grad_keys, grad_values))
            joined = [jnp.where(left_lane, results[0][i], results[1][i]) for i in range(3)]
            for i in range(3):
                grad_qkv[place, spans[i]] = joined[i].astype(jnp.bfloat16)
            sum_query = sum_query + column_sum(joined[0])
            sum_value = sum_value + column_sum(joined[2])
        put_vector(sums_ref, 12 + pair, sum_query)
        put_vector(sums_ref, 15 + pair, sum_value)
    gain, bias = row_vector(vec, 0, blocks), row_vector(vec, 3, blocks)
    sums = [0.0, 0.0]
    for place in places:
        normal, inverse = norm_parts(state_ref[place, :])
        normed_one[place, :] = (normal * gain + bias).astype(jnp.bfloat16)
        grad_normed = contract_last(grad_qkv[place, :], w_qkv[...])
        sums[0] = sums[0] + column_sum(grad_normed * normal)
        sums[1] = sums[1] + column_sum(grad_normed)
        grad_in_ref[place, :] = grad_mid[place, :] + norm_back(grad_normed, normal, inverse, gain)
    put_vector(sums_ref, 0, sums[0])
    put_vector(sums_ref, 3, sums[1])


def layer_backward(grad_state, state, vec, weights, saved):
    qkv, probs, attended, mid, active, slope = saved
    tokens_here = grad_state.shape[0]
    outs = [(grad_state.shape, WIDE), ((ROW_VEC, LANES), WIDE)]
    outs = outs + [((tokens_here, width), LOW) for width in (FF, D, D, 3 * D, D)]
    scratch = [(grad_state.shape, LOW), (grad_state.shape, WIDE)]
    args = [grad_state, state, vec, *weights, qkv, probs, mid, slope]
    outs = call_kernel(backward_kernel, "layer_backward", 7, 8, outs, scratch, *args)
    grad_in, sums, up_low, normed_two, mid_low, qkv_low, normed_one = outs
    factors = (active, normed_two, up_low, attended, mid_low, normed_one, qkv_low)
    return (grad_in, (sums, grad_state, *factors))


def weight_grad_kernel(
    masks,
    half,
    rows,
    extra,
    sums_ref,
    grad_ref,
    active,
    normed_two,
    grad_up,
    attended,
    mid_low,
    normed_one,
    grad_qkv,
    keep_ref,
    send_ref,
    grad_low,
    flat,
):
    blocks = D // LANES
    flat[0:ROW_VEC, :] = sums_ref[...]
    flat[ROW_END:, :] = jnp.zeros((flat.shape[0] - ROW_END, LANES), jnp.float32)
    grad_low[...] = grad_ref[...].astype(jnp.bfloat16)
    for part in range(FF // D):
        columns = slice(part * D, (part + 1) * D)
        block = contract_rows(active[:, columns], grad_low[...])
        put_block(flat, ROW_DOWN, D, block, part * D, 0)
    for part in range(FF // D):
        columns = slice(part * D, (part + 1) * D)
        block = contract_rows(normed_two[...], grad_up[:, columns])
        put_block(flat, ROW_UP, FF, block, 0, blocks * part)
    put_block(flat, ROW_OUT, D, contract_rows(attended[...], mid_low[...]), 0, 0)
    for part in range(3):
        columns = slice(part * D, (part + 1) * D)
        block = contract_rows(normed_one[...], grad_qkv[:, columns])
        put_block(flat, ROW_QKV, 3 * D, block, 0, blocks * part)
    store_shards(keep_ref, send_ref, flat, masks, half, rows, rows)
    tail = extra[...]
    for slot in range(half):
        keep_ref[slot, rows:, :] = tail
        send_ref[slot, rows:, :] = tail


def weight_grads(factors, extra, rows, padded, plan, devices, order):
    half = devices // 2
    kernel = functools.partial(weight_grad_kernel, slot_masks(plan, devices), half, rows)
    outs = [((half, padded, LANES), LOW)] * 2
    scratch = [(factors[1].shape, LOW), ((round_up(2 * half * rows, 8), LANES), WIDE)]
    keep, send = call_kernel(kernel, "weight_grads", 4, 10, outs, scratch, extra, *factors)
    order.end(send)
    return Scatter(keep, send, plan, devices, order)


def embed_kernel(
    masks,
    half,
    rows,
    images,
    mine,
    theirs,
    state_ref,
    small_ref,
    head_ref,
    flat,
    head,
    patch,
    position,
):
    pieces = (mine, theirs)
    for shard in range(2 * half + 1):
        flat[shard * rows : shard * rows + 1, :] = jnp.zeros((1, LANES), jnp.float32)
    for slot, owners in enumerate(owner_pairs(masks, half)):
        for piece, owner in zip(pieces, owners):
            value = piece[slot, : rows + 1, :].astype(jnp.float32)
            flat[pl.ds(owner * rows + 1, rows - 1), :] = value[1:rows]
            flat[pl.ds(owner * rows, 1), :] += value[0:1]
            flat[pl.ds((owner + 1) * rows, 1), :] += value[rows : rows + 1]
    lane = lax.broadcasted_iota(jnp.int32, (24, LANES), 1)
    low = pltpu.roll(flat[0:24, :], LANES - OUTER_SHIFT, 1)
    later = pltpu.roll(flat[1:25, :], LANES - OUTER_SHIFT, 1)
    small = jnp.where(lane < LANES - OUTER_SHIFT, low, later)
    line = lax.broadcasted_iota(jnp.int32, (24, LANES), 0)
    past = (line - 4 * D // LANES) * LANES + lane >= CLASSES
    small_ref[...] = jnp.where(past, 0.0, small)
    blocks = D // LANES
    for c, block in enumerate(take_matrix(flat, OROW_POS, SEQ, D)):
        position[:SEQ, c * LANES : (c + 1) * LANES] = block
    for c, block in enumerate(take_matrix(flat, OROW_PATCH, PATCH_IN, D)):
        patch[:, c * LANES : (c + 1) * LANES] = block.astype(jnp.bfloat16)
    bias_patch = row_vector(small_ref, 3 * blocks, blocks)
    for image in range(images.shape[0]):
        base = image * TOKENS
        state_ref[base + SEQ : base + TOKENS, :] = jnp.zeros((TOKENS - SEQ, D), jnp.float32)
        state_ref[base : base + 1, :] = row_vector(small_ref, 0, blocks) + position[0:1, :]
        value = dot_plain(images[image], patch[...]) + bias_patch
        state_ref[base + 1 : base + SEQ, :] = value + position[1:SEQ, :]
    for p in range(16):
        shift, base = (CLASSES * p) % LANES, OROW_HEAD + (CLASSES * p) // LANES
        part = [flat[pl.ds(base + c, 24, stride=125), :] for c in range(9 if shift else 8)]
        if shift:
            part = [pltpu.roll(block, LANES - shift, 1) for block in part]
        for c in range(8):
            block = jnp.where(lane < LANES - shift, part[c], part[c + 1]) if shift else part[c]
            if c == 7:
                block = jnp.where(lane < CLASSES - 7 * LANES, block, 0.0)
            head[c, pl.ds(p, 24, stride=16), :] = block
    for c in range(8):
        head_ref[:, c * LANES : (c + 1) * LANES] = head[c].astype(jnp.bfloat16)


def embed_images(images, pieces, plan, rows):
    half = pieces[0].shape[0]
    kernel = functools.partial(embed_kernel, slot_masks(plan, 2 * half), half, rows)
    outs = [
        ((images.shape[0] * TOKENS, D), WIDE),
        ((24, LANES), WIDE),
        ((D, CLASS_PAD), LOW),
    ]
    scratch = [
        ((round_up(2 * half * rows + 1, 8), LANES), WIDE),
        ((CLASS_PAD // LANES, D, LANES), WIDE),
        ((PATCH_IN, D), LOW),
        ((TOKENS, D), WIDE),
    ]
    return call_kernel(kernel, "embed_images", 2, 8, outs, scratch, images, *pieces)


def head_kernel(
    labels,
    valid,
    state_ref,
    small,
    w_head,
    count,
    extra_ref,
    grad_ref,
    normed_ref,
    logit_grad_ref,
    vec_ref,
    rows_in,
):
    blocks = D // LANES
    images_here = state_ref.shape[0] // TOKENS
    rows_in[...] = jnp.zeros(rows_in.shape, jnp.float32)
    for image in range(images_here):
        rows_in[image : image + 1, :] = state_ref[image * TOKENS : image * TOKENS + 1, :]
    normal, inverse = norm_parts(rows_in[...])
    gain, bias = row_vector(small, blocks, blocks), row_vector(small, 2 * blocks, blocks)
    normed_final = (normal * gain + bias).astype(jnp.bfloat16)
    bias_head = row_vector(small, 4 * blocks, CLASS_PAD // LANES)
    logits = dot_plain(normed_final, w_head[...]) + bias_head
    shape = logits.shape
    column = lax.broadcasted_iota(jnp.int32, shape, 1)
    line = lax.broadcasted_iota(jnp.int32, (shape[0], 1), 0)
    real = column < CLASSES
    label = jnp.zeros((shape[0], 1), jnp.int32)
    present = jnp.zeros((shape[0], 1), jnp.float32)
    for image in range(images_here):
        label = jnp.where(line == image, labels[image], label)
        present = jnp.where(line == image, valid[image].astype(jnp.float32), present)
    top_logit = jnp.max(jnp.where(real, logits, -1e30), -1, keepdims=True)
    exponent = jnp.where(real, jnp.exp(jnp.minimum(logits - top_logit, 0.0)), 0.0)
    total_exp = jnp.sum(exponent, -1, keepdims=True)
    log_total = jnp.log(total_exp) + top_logit
    target = jnp.where(column == label, 1.0 - smooth + smooth / CLASSES, smooth / CLASSES)
    target = jnp.where(real, target, 0.0)
    per_image = log_total - jnp.sum(target * logits, -1, keepdims=True)
    loss_here = jnp.sum(present * per_image, 0, keepdims=True)
    loss_high = loss_here.astype(jnp.bfloat16).astype(jnp.float32)
    loss_mid = (loss_here - loss_high).astype(jnp.bfloat16).astype(jnp.float32)
    loss_low = loss_here - loss_high - loss_mid
    me = lax.axis_index("fsdp")
    spare = extra_ref.shape
    place = lax.broadcasted_iota(jnp.int32, spare, 0) * LANES
    place = place + lax.broadcasted_iota(jnp.int32, spare, 1)
    extra = jnp.where(place == 3 * me, loss_high, 0.0)
    extra = jnp.where(place == 3 * me + 1, loss_mid, extra)
    extra_ref[...] = jnp.where(place == 3 * me + 2, loss_low, extra).astype(jnp.bfloat16)

    scale = present * (1.0 / count[0:1, 0:1])
    grad_logits = (exponent * (1.0 / total_exp) - target) * scale
    grad_logits_low = grad_logits.astype(jnp.bfloat16)
    grad_normed = contract_last(grad_logits_low, w_head[...])
    grad_final = norm_back(grad_normed, normal, inverse, gain)
    grad_ref[...] = jnp.zeros(grad_ref.shape, jnp.float32)
    for image in range(images_here):
        grad_ref[image * TOKENS : image * TOKENS + 1, :] = grad_final[image : image + 1, :]
    normed_ref[...] = jnp.where(line < images_here, normed_final, jnp.zeros_like(normed_final))
    logit_grad_ref[...] = grad_logits_low
    vec_ref[...] = jnp.zeros(vec_ref.shape, jnp.float32)
    put_vector(vec_ref, blocks, column_sum(grad_normed * normal))
    put_vector(vec_ref, 2 * blocks, column_sum(grad_normed))
    put_vector(vec_ref, 4 * blocks, column_sum(grad_logits))


def head_step(labels, valid, state, small, w_head, count, spare):
    lines = 16
    outs = [
        ((spare, LANES), LOW),
        (state.shape, WIDE),
        ((lines, D), LOW),
        ((lines, CLASS_PAD), LOW),
        ((24, LANES), WIDE),
    ]
    args = (labels, valid, state, small, w_head, count)
    return call_kernel(head_kernel, "head_step", 2, 4, outs, [((lines, D), WIDE)], *args, smem=2)


def outer_grad_kernel(
    masks,
    half,
    rows,
    grad_ref,
    images,
    normed_final,
    logit_grad,
    vec,
    keep_ref,
    send_ref,
    flat,
    head,
    small,
):
    blocks = D // LANES
    images_here = images.shape[0]
    bases = [image * TOKENS for image in range(images_here)]
    small[...] = vec[...]
    token = sum(grad_ref[base : base + 1, :] for base in bases)
    put_vector(small, 0, token)
    total = sum(grad_ref[base : base + SEQ, :] for base in bases)
    put_block(flat, OROW_POS, D, total, 0, 0)
    put_vector(small, 3 * blocks, column_sum(total) - token)
    lane = lax.broadcasted_iota(jnp.int32, (24, LANES), 1)
    line = lax.broadcasted_iota(jnp.int32, (24, LANES), 0)
    moved = pltpu.roll(small[...], OUTER_SHIFT, 1)
    above = jnp.where(line == 0, 0.0, pltpu.roll(moved, 1, 0))
    moved = jnp.where(lane < OUTER_SHIFT, above, moved)
    flat[0:OROW_POS, :] = moved[0:OROW_POS]
    grads = [grad_ref[base + 1 : base + SEQ, :].astype(jnp.bfloat16) for base in bases]
    for part in range(PATCH_IN // D):
        columns = slice(part * D, (part + 1) * D)
        block = sum(contract_rows(images[i, :, columns], grads[i]) for i in range(images_here))
        put_block(flat, OROW_PATCH, D, block, part * D, 0)
    for c in range(8):
        head[c] = contract_rows(normed_final[...], logit_grad[:, c * LANES : (c + 1) * LANES])

    def block_of(p, c):
        return head[c, pl.ds(p, 24, stride=16), :]

    for i in range(125):
        p, start = LANES * i // CLASSES, LANES * i % CLASSES
        c, shift = start // LANES, start % LANES
        value = block_of(p, c)
        if shift:
            value = pltpu.roll(value, LANES - shift, 1)
            if c < 7:
                later = pltpu.roll(block_of(p, c + 1), LANES - shift, 1)
                value = jnp.where(lane < LANES - shift, value, later)
        here = CLASSES - start
        if here < LANES:
            value = jnp.where(lane < here, value, pltpu.roll(block_of(p + 1, 0), here, 1))
        flat[pl.ds(OROW_HEAD + i, 24, stride=125), :] = value
    end = OROW_HEAD + 24 * 125
    flat[end:, :] = jnp.zeros((flat.shape[0] - end, LANES), jnp.float32)
    store_shards(keep_ref, send_ref, flat, masks, half, rows + 1, rows)


def outer_backward(
    grad_state, images, normed_final, logit_grad, vec, rows, padded, plan, devices, order
):
    half = devices // 2
    kernel = functools.partial(outer_grad_kernel, slot_masks(plan, devices), half, rows)
    outs = [((half, padded, LANES), LOW)] * 2
    scratch = [
        ((round_up(2 * half * rows + 1, 8), LANES), WIDE),
        ((CLASS_PAD // LANES, D, LANES), WIDE),
        ((24, LANES), WIDE),
    ]
    args = (grad_state, images, normed_final, logit_grad, vec)
    keep, send = call_kernel(kernel, "outer_backward", 2, 8, outs, scratch, *args)
    order.end(send)
    return Scatter(keep, send, plan, devices, order)


def nesterov(params, momentum, average, grads):
    momentum_new = 0.5 * momentum + grads
    params_new = params - step_rate * (grads + 0.5 * momentum_new)
    return (params_new, momentum_new, 0.5 * average + 0.5 * params_new)


def shards(
    images,
    labels,
    valid,
    layer_params,
    layer_momentum,
    layer_average,
    outer_params,
    outer_momentum,
    outer_average,
):
    devices = lax.axis_size("fsdp")
    layer_rows = layer_params.shape[1] // LANES
    layer_padded = round_up(layer_rows + 3 * devices // LANES + 1, 16)
    outer_rows = outer_params.shape[0] // LANES
    outer_padded = round_up(outer_rows + 1, 16)

    def layer_shard(params, layer_index, tail):
        shard = params[layer_index].reshape(layer_rows, LANES).astype(jnp.bfloat16)
        tail = jnp.pad(tail, ((0, layer_padded - layer_rows - 1), (0, 0)))
        return jnp.concatenate([shard, tail.astype(jnp.bfloat16)])

    outer_shard = jnp.pad(outer_params, (OUTER_SHIFT, LANES - OUTER_SHIFT)).reshape(-1, LANES)
    outer_shard = jnp.pad(outer_shard, ((0, outer_padded - outer_rows - 1), (0, 0)))
    outer_shard = outer_shard.astype(jnp.bfloat16)
    empty = jnp.zeros((1, LANES), jnp.float32)
    order = Order(outer_shard)
    outer = Gather(outer_shard, Z_FIRST, devices, order)
    outer.start()
    params_later, valid_later = order.begin((layer_params, valid))
    one = Gather(layer_shard(params_later, 0, empty), Z_FIRST, devices, order)
    order.end(one.column)
    order.fence()
    one.start()
    params_later, valid_later = order.begin((params_later, valid_later))
    count = jnp.sum(valid_later).astype(jnp.float32).reshape(1, 1)
    count_row = jnp.pad(count, ((0, 0), (0, LANES - 1)))
    two = Gather(layer_shard(params_later, 1, count_row), Z_FIRST, devices, order)
    three = Gather(layer_shard(params_later, 2, empty), LAST_PLAN, devices, order)
    order.end((two.column, three.column))
    order.fence()
    outer.take()
    outer.start()
    order.fence()
    outer.take()
    outer.start()
    order.fence(20)
    one.take()
    one.start()
    order.fence()
    two.start()
    order.fence()
    outer.take()
    one.take()
    one.start()
    order.fence(20)
    two.take()
    two.start()
    order.fence()
    three.start()
    outer.start()
    order.fence()
    pieces = outer.take_across()
    state, small, w_head = embed_images(images, pieces, Z_FIRST, outer_rows)
    order.end(state)
    one.take()
    two.take()
    two.start()
    three.take()
    three.start()
    one.start()
    order.fence()
    kept = []

    def forward(state, pieces, plan):
        vec, weights, counts = layer_unpack(pieces, plan, 0, layer_rows)
        state_next, saved = layer_forward(state, vec, weights)
        kept.append((state, vec, weights, saved))
        order.end(state_next)
        return (state_next, counts)

    state, unused = forward(state, one.take_across(), Z_FIRST)
    two.take()
    three.take()
    three.start()
    two.start()
    order.fence()
    state, image_counts = forward(state, two.take_across(), Z_FIRST)
    three.take()
    three.start()
    order.fence()
    state, unused = forward(state, three.take_across(), LAST_PLAN)
    image_count = image_counts[0, 0]
    extra, grad_state, normed_final, logit_grad, vec_grad = head_step(
        labels, valid, state, small, w_head, image_counts, layer_padded - layer_rows
    )

    def backward(layer_index, grad_state):
        grad_state, factors = layer_backward(order.begin(grad_state), *kept[layer_index])
        order.end(grad_state)
        return (grad_state, factors)

    def packed(factors):
        first, *rest = factors
        factors = (order.begin(first), *rest)
        return weight_grads(
            factors, extra, layer_rows, layer_padded, Z_FIRST, devices, order
        )

    def turn_back(layer_index, grad_state):
        grad_state, factors = backward(layer_index, grad_state)
        return (grad_state, packed(factors))

    grad_state, factors = backward(2, grad_state)
    three = packed(factors)
    three.start()
    order.fence()
    three.take()
    three.start()
    order.fence()
    grad_state, factors = backward(1, grad_state)
    two = packed(factors)
    three.take()
    three.start()
    two.start()
    order.fence()
    two.take()
    two.start()
    order.fence()
    grad_state, factors = backward(0, grad_state)
    three.take()
    three.start()
    order.fence()
    one = packed(factors)
    outer = outer_backward(
        order.begin(grad_state),
        images,
        normed_final,
        logit_grad,
        vec_grad,
        outer_rows,
        outer_padded,
        Z_FIRST,
        devices,
        order,
    )
    two.take()
    three.take()
    two.start()
    one.start()
    outer.start()
    order.fence()
    one.take()
    one.start()
    outer.take()
    two.take()
    two.start()
    order.fence()
    one.take()
    one.start()
    outer.start()
    order.fence()
    two.take()
    one.take()
    one.start()
    order.fence()
    outer.take()
    outer.start()
    order.fence()
    outer.take()
    outer.start()
    order.fence()
    one.take()
    outer.take()
    sums = (one, two, three)
    layer_summed = [item.total for item in sums]
    outer_summed = outer.total
    loss_sum = jnp.sum(layer_summed[2][layer_rows:]) + order.token[0, 0]
    layer_grads = [summed[:layer_rows].reshape(-1) for summed in layer_summed]
    outer_grad = outer_summed[: outer_rows + 1].reshape(-1)
    outer_grad = outer_grad[OUTER_SHIFT : OUTER_SHIFT + outer_rows * LANES]
    layer_grad = jnp.stack(layer_grads)
    layer_new, layer_mom_new, layer_avg_new = nesterov(
        layer_params, layer_momentum, layer_average, layer_grad
    )
    outer_new, outer_mom_new, outer_avg_new = nesterov(
        outer_params, outer_momentum, outer_average, outer_grad
    )
    return (
        loss_sum,
        image_count,
        layer_new,
        layer_mom_new,
        layer_avg_new,
        outer_new,
        outer_mom_new,
        outer_avg_new,
    )


def solution(mesh):
    return jax.shard_map(
        shards,
        mesh=mesh,
        in_specs=(
            P("fsdp", None, None),
            P("fsdp"),
            P("fsdp"),
            P(None, "fsdp"),
            P(None, "fsdp"),
            P(None, "fsdp"),
            P("fsdp"),
            P("fsdp"),
            P("fsdp"),
        ),
        out_specs=(
            P(),
            P(),
            P(None, "fsdp"),
            P(None, "fsdp"),
            P(None, "fsdp"),
            P("fsdp"),
            P("fsdp"),
            P("fsdp"),
        ),
        check_vma=False,
    )
```

```python
import functools

import jax
import jax.numpy as jnp
import numpy as np
from jax import lax
from jax.experimental import pallas as pl
from jax.experimental.pallas import tpu as pltpu
from jax.sharding import PartitionSpec as P

D = 384
HEADS = 6
HEAD = 64
FF = 1536
CLASSES = 1000
CLASS_PAD = 1024
PATCH_IN = 768
PATCHES = 196
SEQ = 197
LAYERS = 3
LANES = 128
TOKENS = 208

eps_norm = 1e-06
smooth = 0.1
step_rate = 20.0
root_half = 0.7071067811865476
inv_root_two_pi = 0.3989422804014327

MIB = 1024 * 1024


def cost(microseconds):
    return pl.CostEstimate(
        flops=int(microseconds * 1e9), bytes_accessed=int(microseconds * 3.5e6), transcendentals=0
    )


ROW_VEC = 36
ROW_QKV = ROW_VEC
ROW_OUT = ROW_QKV + 3 * D * D // LANES
ROW_UP = ROW_OUT + D * D // LANES
ROW_DOWN = ROW_UP + D * FF // LANES
ROW_END = ROW_DOWN + D * FF // LANES

OUTER_SHIFT = 24
SMALL_ROWS = 4 * D // LANES + CLASS_PAD // LANES
OROW_POS = (4 * D + CLASSES + OUTER_SHIFT) // LANES
OROW_PATCH = OROW_POS + SEQ * D // LANES
OROW_HEAD = OROW_PATCH + PATCH_IN * D // LANES


def round_up(value, unit):
    return (value + unit - 1) // unit * unit


def bits_of(devices):
    count = devices.bit_length() - 1
    assert 1 << count == devices
    return count


def steps_of(plan, devices):
    if devices != 32:
        return [[(1 << bit, 1 << bit)] for bit in range(1, bits_of(devices))]
    kinds = {
        "z": [(8, 8), (16, 16), (24, 24)],
        "z two": [(16, 16)],
        "z one": [(8, 8)],
        "near": [(4, 2)],
        "far": [(2, 4)],
    }
    return [kinds[name] for name in plan]


Z_FIRST = ("z", "near", "far")
Z_STEPS = ("z two", "z one", "near", "far")


def slot_masks(plan, devices):
    masks = [(0, 0)]
    for partners in steps_of(plan, devices):
        masks = masks + [(a ^ p, b ^ q) for p, q in partners for a, b in masks]
    return tuple(zip(*masks))


def swap(values, masks, devices):
    pairs = [(i, i ^ masks[i & 1]) for i in range(devices)]
    return lax.ppermute(values, "fsdp", pairs)


def fence_kernel(token, out):
    out[...] = token[...]


class Order:
    def __init__(self, value):
        self.token = jnp.zeros((8, LANES), jnp.float32)
        self.latest = value

    def begin(self, value):
        value, self.latest, self.token = lax.optimization_barrier(
            (value, self.latest, self.token)
        )
        return value

    def end(self, value):
        self.latest = value
        return value

    def fence(self, microseconds=0.01):
        self.begin(())
        self.token = pl.pallas_call(
            fence_kernel,
            out_shape=jax.ShapeDtypeStruct((8, LANES), jnp.float32),
            in_specs=[pl.BlockSpec(memory_space=pltpu.VMEM)],
            out_specs=pl.BlockSpec(memory_space=pltpu.VMEM),
            compiler_params=pltpu.CompilerParams(vmem_limit_bytes=MIB),
            cost_estimate=cost(microseconds),
            name="fence",
        )(self.token)


class Gather:
    def __init__(self, shard, plan, devices, order):
        self.devices = devices
        self.order = order
        self.steps = steps_of(plan, devices)
        self.column = shard[None]
        self.plan_length = len(plan)

    def start(self):
        while len(self.steps) > self.plan_length:
            self.exchange()
            self.take()
        self.exchange()

    def exchange(self):
        self.column = self.order.begin(self.column)
        partners = self.steps.pop(0) if self.steps else [(1, 1)]
        self.arriving = [swap(self.column, masks, self.devices) for masks in partners]

    def take(self):
        first, *rest = self.arriving
        self.column = jnp.concatenate([self.column, self.order.begin(first)] + rest)
        self.order.end(self.column)

    def take_across(self):
        return (self.column, self.order.end(self.order.begin(self.arriving[0])))


class Scatter:
    def __init__(self, keep, send, plan, devices, order):
        self.devices = devices
        self.order = order
        self.steps = [[(1, 1)]] + steps_of(plan, devices)[::-1]
        self.total = keep
        self.low = [send]
        self.starts = 0
        self.plan_length = len(plan)

    def start(self):
        self.exchange()
        self.starts = self.starts + 1
        while self.starts > self.plan_length and self.steps:
            self.take()
            self.exchange()

    def exchange(self):
        partners = self.steps.pop(0)
        low = self.order.begin(self.low)
        self.arriving = [swap(part, masks, self.devices) for part, masks in zip(low, partners)]

    def take(self):
        first, *rest = self.arriving
        parts = [part.astype(jnp.float32) for part in [self.order.begin(first)] + rest]
        total = self.total.astype(jnp.float32)
        if len(parts) == 3:
            total = total + ((parts[0] + parts[1]) + parts[2])
        else:
            total = total + parts[0]
        if not self.steps:
            self.total = self.order.end(total[0])
            return
        groups = 1 + len(self.steps[0])
        size = total.shape[0] // groups
        self.total = total[:size]
        sent = total[size:].astype(jnp.bfloat16)
        self.low = [sent[i * size : (i + 1) * size] for i in range(groups - 1)]
        self.order.end(sent)


def select_mask(core, masks, slot):
    first, second = masks[0][slot], masks[1][slot]
    if first == second:
        return first
    return jnp.where(core == 0, first, second)


def owner_pairs(masks, half):
    me = lax.axis_index("fsdp")
    core = lax.rem(me, 2)
    other = jnp.bitwise_xor(me, 1)
    return [
        (
            jnp.bitwise_xor(me, select_mask(core, masks, slot)),
            jnp.bitwise_xor(other, select_mask(1 - core, masks, slot)),
        )
        for slot in range(half)
    ]


def load_shards(pieces, flat, masks, half, base, rows):
    for slot, owners in enumerate(owner_pairs(masks, half)):
        for piece, owner in zip(pieces, owners):
            value = piece[slot, base : base + rows, :].astype(jnp.float32)
            flat[pl.ds(owner * rows, rows), :] = value


def store_shards(keep_ref, send_ref, flat, masks, half, rows, stride):
    for slot, owners in enumerate(owner_pairs(masks, half)):
        for ref, owner in zip((keep_ref, send_ref), owners):
            ref[slot, :rows, :] = flat[pl.ds(owner * stride, rows), :].astype(jnp.bfloat16)


def row_vector(ref, row, blocks):
    return jnp.concatenate([ref[row + i : row + i + 1, :] for i in range(blocks)], axis=1)


def put_vector(ref, row, vector):
    for i in range(vector.shape[1] // LANES):
        ref[row + i : row + i + 1, :] = vector[:, i * LANES : (i + 1) * LANES]


def take_matrix(flat, row, height, width):
    blocks = width // LANES
    return [flat[pl.ds(row + c, height, stride=blocks), :] for c in range(blocks)]


def put_block(flat, row, width, block, first_row, first_block):
    blocks = width // LANES
    height = block.shape[0]
    for c in range(block.shape[1] // LANES):
        place = row + first_row * blocks + first_block + c
        flat[pl.ds(place, height, stride=blocks), :] = block[:, c * LANES : (c + 1) * LANES]


def dot_plain(left, right):
    return jnp.dot(left, right, preferred_element_type=jnp.float32)


def contract_rows(left, right):
    return lax.dot_general(
        left, right, (((0,), (0,)), ((), ())), preferred_element_type=jnp.float32
    )


def contract_last(left, right):
    return lax.dot_general(
        left, right, (((1,), (1,)), ((), ())), preferred_element_type=jnp.float32
    )


def norm_parts(values):
    center = values - jnp.mean(values, -1, keepdims=True)
    inverse = lax.rsqrt(jnp.mean(center * center, -1, keepdims=True) + eps_norm)
    return (center * inverse, inverse)


def norm_back(grad_normed, normal, inverse, gain):
    scaled = grad_normed * gain
    return inverse * (
        scaled
        - jnp.mean(scaled, -1, keepdims=True)
        - normal * jnp.mean(scaled * normal, -1, keepdims=True)
    )


def gelu_parts(values):
    below = 0.5 * (1.0 + lax.erf(values * root_half))
    bell = jnp.exp(-0.5 * values * values)
    return (values * below, below + values * bell * inv_root_two_pi)


def column_sum(values):
    return jnp.sum(values, 0, keepdims=True)


def unpack_kernel(
    masks,
    half,
    base,
    rows,
    count_row,
    mine,
    theirs,
    vec,
    count_ref,
    w_qkv,
    w_out,
    w_up,
    w_down,
    flat,
):
    pieces = (mine, theirs)
    load_shards(pieces, flat, masks, half, base, rows)
    vec[...] = flat[0:ROW_VEC, :]
    count = jnp.zeros((1, LANES), jnp.float32)
    for slot in range(half):
        for piece in pieces:
            count = count + piece[slot, count_row : count_row + 1, :].astype(jnp.float32)
    count_ref[...] = count
    for ref, row in ((w_qkv, ROW_QKV), (w_out, ROW_OUT), (w_up, ROW_UP), (w_down, ROW_DOWN)):
        for c, block in enumerate(take_matrix(flat, row, *ref.shape)):
            ref[:, c * LANES : (c + 1) * LANES] = block.astype(jnp.bfloat16)


def call_kernel(kernel, name, microseconds, megabytes, outs, scratch, *args, smem=0):
    spaces = [pltpu.SMEM] * smem + [pltpu.VMEM] * (len(args) - smem)
    return pl.pallas_call(
        kernel,
        out_shape=[jax.ShapeDtypeStruct(shape, kind) for shape, kind in outs],
        in_specs=[pl.BlockSpec(memory_space=space) for space in spaces],
        out_specs=[pl.BlockSpec(memory_space=pltpu.VMEM)] * len(outs),
        scratch_shapes=[pltpu.VMEM(shape, kind) for shape, kind in scratch],
        compiler_params=pltpu.CompilerParams(vmem_limit_bytes=megabytes * MIB),
        cost_estimate=cost(0.01),
        name=name,
    )(*args)


LOW = jnp.bfloat16
WIDE = jnp.float32
MATRICES = [(D, 3 * D), (D, D), (D, FF), (FF, D)]


def layer_unpack(pieces, plan, base, rows):
    half = pieces[0].shape[0]
    kernel = functools.partial(
        unpack_kernel, slot_masks(plan, 2 * half), half, base, rows, base + rows
    )
    outs = [((ROW_VEC, LANES), WIDE), ((1, LANES), WIDE)] + [(shape, LOW) for shape in MATRICES]
    scratch = [((round_up(2 * half * rows, 8), LANES), WIDE)]
    vec, count, *weights = call_kernel(kernel, "layer_unpack", 3, 10, outs, scratch, *pieces)
    return (vec, weights, count)


def forward_kernel(
    state_ref,
    vec,
    w_qkv,
    w_out,
    w_up,
    w_down,
    next_ref,
    qkv,
    probs,
    attended,
    mid,
    active,
    slope,
    normed,
):
    blocks = D // LANES
    images_here = state_ref.shape[0] // TOKENS
    gain, bias = row_vector(vec, 0, blocks), row_vector(vec, 3, blocks)
    for image in range(images_here):
        place = slice(image * TOKENS, (image + 1) * TOKENS)
        normal, inverse = norm_parts(state_ref[place, :])
        normed[place, :] = (normal * gain + bias).astype(jnp.bfloat16)
    for part in range(3):
        columns = slice(part * D, (part + 1) * D)
        value = dot_plain(normed[...], w_qkv[:, columns])
        if part != 1:
            value = value + row_vector(vec, 12 if part == 0 else 15, blocks)
        qkv[:, columns] = value.astype(jnp.bfloat16)

    left_lane = lax.broadcasted_iota(jnp.int32, (TOKENS, LANES), 1) < HEAD
    real_key = lax.broadcasted_iota(jnp.int32, (TOKENS, TOKENS), 1) < SEQ
    for image in range(images_here):
        place = slice(image * TOKENS, (image + 1) * TOKENS)
        for pair in range(HEADS // 2):
            queries = qkv[place, pair * LANES : (pair + 1) * LANES]
            keys = qkv[place, D + pair * LANES : D + (pair + 1) * LANES]
            values = qkv[place, 2 * D + pair * LANES : 2 * D + (pair + 1) * LANES]
            results = []
            for side in range(2):
                own = left_lane if side == 0 else jnp.logical_not(left_lane)
                head_queries = jnp.where(own, queries, jnp.zeros_like(queries))
                scores = contract_last(head_queries, keys) * HEAD ** (-0.5)
                scores = jnp.where(real_key, scores, -1e30)
                exponent = jnp.exp(scores - jnp.max(scores, -1, keepdims=True))
                prob = exponent * (1.0 / jnp.sum(exponent, -1, keepdims=True))
                probs[image * HEADS + 2 * pair + side] = prob
                results.append(dot_plain(prob.astype(jnp.bfloat16), values))
            joined = jnp.where(left_lane, results[0], results[1])
            attended[place, pair * LANES : (pair + 1) * LANES] = joined.astype(jnp.bfloat16)

    bias_out = row_vector(vec, 18, blocks)
    gain, bias = row_vector(vec, 6, blocks), row_vector(vec, 9, blocks)
    for image in range(images_here):
        place = slice(image * TOKENS, (image + 1) * TOKENS)
        value = state_ref[place, :] + dot_plain(attended[place, :], w_out[...]) + bias_out
        mid[place, :] = value
        normal, inverse = norm_parts(value)
        normed[place, :] = (normal * gain + bias).astype(jnp.bfloat16)
    for part in range(FF // D):
        columns = slice(part * D, (part + 1) * D)
        bias_up = row_vector(vec, 24 + blocks * part, blocks)
        for image in range(images_here):
            place = slice(image * TOKENS, (image + 1) * TOKENS)
            up_value = dot_plain(normed[place, :], w_up[:, columns]) + bias_up
            act, slo = gelu_parts(up_value)
            active[place, columns] = act.astype(jnp.bfloat16)
            slope[place, columns] = slo
    bias_down = row_vector(vec, 21, blocks)
    for image in range(images_here):
        place = slice(image * TOKENS, (image + 1) * TOKENS)
        next_ref[place, :] = mid[place, :] + dot_plain(active[place, :], w_down[...]) + bias_down


def layer_forward(state, vec, weights):
    tokens_here = state.shape[0]
    images_here = tokens_here // TOKENS
    outs = [
        (state.shape, WIDE),
        ((tokens_here, 3 * D), LOW),
        ((images_here * HEADS, TOKENS, TOKENS), WIDE),
        ((tokens_here, D), LOW),
        ((tokens_here, D), WIDE),
        ((tokens_here, FF), LOW),
        ((tokens_here, FF), WIDE),
    ]
    scratch = [(state.shape, LOW)]
    state_next, *saved = call_kernel(
        forward_kernel, "layer_forward", 7, 8, outs, scratch, state, vec, *weights
    )
    return (state_next, saved)


def backward_kernel(
    grad_ref,
    state_ref,
    vec,
    w_qkv,
    w_out,
    w_up,
    w_down,
    qkv,
    probs,
    mid,
    slope,
    grad_in_ref,
    sums_ref,
    grad_up,
    normed_two,
    grad_low,
    grad_qkv,
    normed_one,
    attended,
    grad_mid,
):
    blocks = D // LANES
    images_here = grad_ref.shape[0] // TOKENS
    places = [slice(i * TOKENS, (i + 1) * TOKENS) for i in range(images_here)]
    put_vector(sums_ref, 21, column_sum(grad_ref[...]))
    grad_low[...] = grad_ref[...].astype(jnp.bfloat16)
    for part in range(FF // D):
        columns = slice(part * D, (part + 1) * D)
        total = 0.0
        for place in places:
            value = contract_last(grad_low[place, :], w_down[columns, :]) * slope[place, columns]
            total = total + column_sum(value)
            grad_up[place, columns] = value.astype(jnp.bfloat16)
        put_vector(sums_ref, 24 + blocks * part, total)
    gain, bias = row_vector(vec, 6, blocks), row_vector(vec, 9, blocks)
    sums = [0.0, 0.0, 0.0]
    for place in places:
        normal, inverse = norm_parts(mid[place, :])
        normed_two[place, :] = (normal * gain + bias).astype(jnp.bfloat16)
        grad_normed = contract_last(grad_up[place, :], w_up[...])
        sums[0] = sums[0] + column_sum(grad_normed * normal)
        sums[1] = sums[1] + column_sum(grad_normed)
        value = grad_ref[place, :] + norm_back(grad_normed, normal, inverse, gain)
        sums[2] = sums[2] + column_sum(value)
        grad_mid[place, :] = value
        grad_low[place, :] = value.astype(jnp.bfloat16)
    put_vector(sums_ref, 6, sums[0])
    put_vector(sums_ref, 9, sums[1])
    put_vector(sums_ref, 18, sums[2])
    for place in places:
        attended[place, :] = contract_last(grad_low[place, :], w_out[...]).astype(jnp.bfloat16)
    left_lane = lax.broadcasted_iota(jnp.int32, (TOKENS, LANES), 1) < HEAD
    for pair in range(HEADS // 2):
        sum_query, sum_value = 0.0, 0.0
        for image, place in enumerate(places):
            spans = [slice(i * D + pair * LANES, i * D + (pair + 1) * LANES) for i in range(3)]
            queries, keys, values = [qkv[place, span] for span in spans]
            grad_here = attended[place, pair * LANES : (pair + 1) * LANES]
            results = []
            for side in range(2):
                own = left_lane if side == 0 else jnp.logical_not(left_lane)
                head_grad = jnp.where(own, grad_here, jnp.zeros_like(grad_here))
                prob = probs[image * HEADS + 2 * pair + side]
                grad_probs = contract_last(head_grad, values)
                grad_values = contract_rows(prob.astype(jnp.bfloat16), grad_here)
                inner = jnp.sum(grad_probs * prob, -1, keepdims=True)
                grad_scores = (prob * (grad_probs - inner) * HEAD ** (-0.5)).astype(jnp.bfloat16)
                grad_queries = dot_plain(grad_scores, keys)
                grad_keys = contract_rows(grad_scores, queries)
                results.append((grad_queries, grad_keys, grad_values))
            joined = [jnp.where(left_lane, results[0][i], results[1][i]) for i in range(3)]
            for i in range(3):
                grad_qkv[place, spans[i]] = joined[i].astype(jnp.bfloat16)
            sum_query = sum_query + column_sum(joined[0])
            sum_value = sum_value + column_sum(joined[2])
        put_vector(sums_ref, 12 + pair, sum_query)
        put_vector(sums_ref, 15 + pair, sum_value)
    gain, bias = row_vector(vec, 0, blocks), row_vector(vec, 3, blocks)
    sums = [0.0, 0.0]
    for place in places:
        normal, inverse = norm_parts(state_ref[place, :])
        normed_one[place, :] = (normal * gain + bias).astype(jnp.bfloat16)
        grad_normed = contract_last(grad_qkv[place, :], w_qkv[...])
        sums[0] = sums[0] + column_sum(grad_normed * normal)
        sums[1] = sums[1] + column_sum(grad_normed)
        grad_in_ref[place, :] = grad_mid[place, :] + norm_back(grad_normed, normal, inverse, gain)
    put_vector(sums_ref, 0, sums[0])
    put_vector(sums_ref, 3, sums[1])


def layer_backward(grad_state, state, vec, weights, saved):
    qkv, probs, attended, mid, active, slope = saved
    tokens_here = grad_state.shape[0]
    outs = [(grad_state.shape, WIDE), ((ROW_VEC, LANES), WIDE)]
    outs = outs + [((tokens_here, width), LOW) for width in (FF, D, D, 3 * D, D)]
    scratch = [(grad_state.shape, LOW), (grad_state.shape, WIDE)]
    args = [grad_state, state, vec, *weights, qkv, probs, mid, slope]
    outs = call_kernel(backward_kernel, "layer_backward", 7, 8, outs, scratch, *args)
    grad_in, sums, up_low, normed_two, mid_low, qkv_low, normed_one = outs
    factors = (active, normed_two, up_low, attended, mid_low, normed_one, qkv_low)
    return (grad_in, (sums, grad_state, *factors))


def weight_grad_kernel(
    masks,
    half,
    rows,
    extra,
    sums_ref,
    grad_ref,
    active,
    normed_two,
    grad_up,
    attended,
    mid_low,
    normed_one,
    grad_qkv,
    keep_ref,
    send_ref,
    grad_low,
    flat,
):
    blocks = D // LANES
    flat[0:ROW_VEC, :] = sums_ref[...]
    flat[ROW_END:, :] = jnp.zeros((flat.shape[0] - ROW_END, LANES), jnp.float32)
    grad_low[...] = grad_ref[...].astype(jnp.bfloat16)
    for part in range(FF // D):
        columns = slice(part * D, (part + 1) * D)
        block = contract_rows(active[:, columns], grad_low[...])
        put_block(flat, ROW_DOWN, D, block, part * D, 0)
    for part in range(FF // D):
        columns = slice(part * D, (part + 1) * D)
        block = contract_rows(normed_two[...], grad_up[:, columns])
        put_block(flat, ROW_UP, FF, block, 0, blocks * part)
    put_block(flat, ROW_OUT, D, contract_rows(attended[...], mid_low[...]), 0, 0)
    for part in range(3):
        columns = slice(part * D, (part + 1) * D)
        block = contract_rows(normed_one[...], grad_qkv[:, columns])
        put_block(flat, ROW_QKV, 3 * D, block, 0, blocks * part)
    store_shards(keep_ref, send_ref, flat, masks, half, rows, rows)
    tail = extra[...]
    for slot in range(half):
        keep_ref[slot, rows:, :] = tail
        send_ref[slot, rows:, :] = tail


def weight_grads(factors, extra, rows, padded, plan, devices, order):
    half = devices // 2
    kernel = functools.partial(weight_grad_kernel, slot_masks(plan, devices), half, rows)
    outs = [((half, padded, LANES), LOW)] * 2
    scratch = [(factors[1].shape, LOW), ((round_up(2 * half * rows, 8), LANES), WIDE)]
    keep, send = call_kernel(kernel, "weight_grads", 4, 10, outs, scratch, extra, *factors)
    order.end(send)
    return Scatter(keep, send, plan, devices, order)


def embed_kernel(
    masks,
    half,
    rows,
    images,
    mine,
    theirs,
    state_ref,
    small_ref,
    head_ref,
    flat,
    head,
    patch,
    position,
):
    pieces = (mine, theirs)
    for shard in range(2 * half + 1):
        flat[shard * rows : shard * rows + 1, :] = jnp.zeros((1, LANES), jnp.float32)
    for slot, owners in enumerate(owner_pairs(masks, half)):
        for piece, owner in zip(pieces, owners):
            value = piece[slot, : rows + 1, :].astype(jnp.float32)
            flat[pl.ds(owner * rows + 1, rows - 1), :] = value[1:rows]
            flat[pl.ds(owner * rows, 1), :] += value[0:1]
            flat[pl.ds((owner + 1) * rows, 1), :] += value[rows : rows + 1]
    lane = lax.broadcasted_iota(jnp.int32, (24, LANES), 1)
    low = pltpu.roll(flat[0:24, :], LANES - OUTER_SHIFT, 1)
    later = pltpu.roll(flat[1:25, :], LANES - OUTER_SHIFT, 1)
    small = jnp.where(lane < LANES - OUTER_SHIFT, low, later)
    line = lax.broadcasted_iota(jnp.int32, (24, LANES), 0)
    past = (line - 4 * D // LANES) * LANES + lane >= CLASSES
    small_ref[...] = jnp.where(past, 0.0, small)
    blocks = D // LANES
    for c, block in enumerate(take_matrix(flat, OROW_POS, SEQ, D)):
        position[:SEQ, c * LANES : (c + 1) * LANES] = block
    for c, block in enumerate(take_matrix(flat, OROW_PATCH, PATCH_IN, D)):
        patch[:, c * LANES : (c + 1) * LANES] = block.astype(jnp.bfloat16)
    bias_patch = row_vector(small_ref, 3 * blocks, blocks)
    for image in range(images.shape[0]):
        base = image * TOKENS
        state_ref[base + SEQ : base + TOKENS, :] = jnp.zeros((TOKENS - SEQ, D), jnp.float32)
        state_ref[base : base + 1, :] = row_vector(small_ref, 0, blocks) + position[0:1, :]
        value = dot_plain(images[image], patch[...]) + bias_patch
        state_ref[base + 1 : base + SEQ, :] = value + position[1:SEQ, :]
    for p in range(16):
        shift, base = (CLASSES * p) % LANES, OROW_HEAD + (CLASSES * p) // LANES
        part = [flat[pl.ds(base + c, 24, stride=125), :] for c in range(9 if shift else 8)]
        if shift:
            part = [pltpu.roll(block, LANES - shift, 1) for block in part]
        for c in range(8):
            block = jnp.where(lane < LANES - shift, part[c], part[c + 1]) if shift else part[c]
            if c == 7:
                block = jnp.where(lane < CLASSES - 7 * LANES, block, 0.0)
            head[c, pl.ds(p, 24, stride=16), :] = block
    for c in range(8):
        head_ref[:, c * LANES : (c + 1) * LANES] = head[c].astype(jnp.bfloat16)


def embed_images(images, pieces, plan, rows):
    half = pieces[0].shape[0]
    kernel = functools.partial(embed_kernel, slot_masks(plan, 2 * half), half, rows)
    outs = [
        ((images.shape[0] * TOKENS, D), WIDE),
        ((24, LANES), WIDE),
        ((D, CLASS_PAD), LOW),
    ]
    scratch = [
        ((round_up(2 * half * rows + 1, 8), LANES), WIDE),
        ((CLASS_PAD // LANES, D, LANES), WIDE),
        ((PATCH_IN, D), LOW),
        ((TOKENS, D), WIDE),
    ]
    return call_kernel(kernel, "embed_images", 2, 8, outs, scratch, images, *pieces)


def head_kernel(
    labels,
    valid,
    state_ref,
    small,
    w_head,
    count,
    extra_ref,
    grad_ref,
    normed_ref,
    logit_grad_ref,
    vec_ref,
    rows_in,
):
    blocks = D // LANES
    images_here = state_ref.shape[0] // TOKENS
    rows_in[...] = jnp.zeros(rows_in.shape, jnp.float32)
    for image in range(images_here):
        rows_in[image : image + 1, :] = state_ref[image * TOKENS : image * TOKENS + 1, :]
    normal, inverse = norm_parts(rows_in[...])
    gain, bias = row_vector(small, blocks, blocks), row_vector(small, 2 * blocks, blocks)
    normed_final = (normal * gain + bias).astype(jnp.bfloat16)
    bias_head = row_vector(small, 4 * blocks, CLASS_PAD // LANES)
    logits = dot_plain(normed_final, w_head[...]) + bias_head
    shape = logits.shape
    column = lax.broadcasted_iota(jnp.int32, shape, 1)
    line = lax.broadcasted_iota(jnp.int32, (shape[0], 1), 0)
    real = column < CLASSES
    label = jnp.zeros((shape[0], 1), jnp.int32)
    present = jnp.zeros((shape[0], 1), jnp.float32)
    for image in range(images_here):
        label = jnp.where(line == image, labels[image], label)
        present = jnp.where(line == image, valid[image].astype(jnp.float32), present)
    top_logit = jnp.max(jnp.where(real, logits, -1e30), -1, keepdims=True)
    exponent = jnp.where(real, jnp.exp(jnp.minimum(logits - top_logit, 0.0)), 0.0)
    total_exp = jnp.sum(exponent, -1, keepdims=True)
    log_total = jnp.log(total_exp) + top_logit
    target = jnp.where(column == label, 1.0 - smooth + smooth / CLASSES, smooth / CLASSES)
    target = jnp.where(real, target, 0.0)
    per_image = log_total - jnp.sum(target * logits, -1, keepdims=True)
    loss_here = jnp.sum(present * per_image, 0, keepdims=True)
    loss_high = loss_here.astype(jnp.bfloat16).astype(jnp.float32)
    loss_mid = (loss_here - loss_high).astype(jnp.bfloat16).astype(jnp.float32)
    loss_low = loss_here - loss_high - loss_mid
    me = lax.axis_index("fsdp")
    spare = extra_ref.shape
    place = lax.broadcasted_iota(jnp.int32, spare, 0) * LANES
    place = place + lax.broadcasted_iota(jnp.int32, spare, 1)
    extra = jnp.where(place == 3 * me, loss_high, 0.0)
    extra = jnp.where(place == 3 * me + 1, loss_mid, extra)
    extra_ref[...] = jnp.where(place == 3 * me + 2, loss_low, extra).astype(jnp.bfloat16)

    scale = present * (1.0 / count[0:1, 0:1])
    grad_logits = (exponent * (1.0 / total_exp) - target) * scale
    grad_logits_low = grad_logits.astype(jnp.bfloat16)
    grad_normed = contract_last(grad_logits_low, w_head[...])
    grad_final = norm_back(grad_normed, normal, inverse, gain)
    grad_ref[...] = jnp.zeros(grad_ref.shape, jnp.float32)
    for image in range(images_here):
        grad_ref[image * TOKENS : image * TOKENS + 1, :] = grad_final[image : image + 1, :]
    normed_ref[...] = jnp.where(line < images_here, normed_final, jnp.zeros_like(normed_final))
    logit_grad_ref[...] = grad_logits_low
    vec_ref[...] = jnp.zeros(vec_ref.shape, jnp.float32)
    put_vector(vec_ref, blocks, column_sum(grad_normed * normal))
    put_vector(vec_ref, 2 * blocks, column_sum(grad_normed))
    put_vector(vec_ref, 4 * blocks, column_sum(grad_logits))


def head_step(labels, valid, state, small, w_head, count, spare):
    lines = 16
    outs = [
        ((spare, LANES), LOW),
        (state.shape, WIDE),
        ((lines, D), LOW),
        ((lines, CLASS_PAD), LOW),
        ((24, LANES), WIDE),
    ]
    args = (labels, valid, state, small, w_head, count)
    return call_kernel(head_kernel, "head_step", 2, 4, outs, [((lines, D), WIDE)], *args, smem=2)


def outer_grad_kernel(
    masks,
    half,
    rows,
    grad_ref,
    images,
    normed_final,
    logit_grad,
    vec,
    keep_ref,
    send_ref,
    flat,
    head,
    small,
):
    blocks = D // LANES
    images_here = images.shape[0]
    bases = [image * TOKENS for image in range(images_here)]
    small[...] = vec[...]
    token = sum(grad_ref[base : base + 1, :] for base in bases)
    put_vector(small, 0, token)
    total = sum(grad_ref[base : base + SEQ, :] for base in bases)
    put_block(flat, OROW_POS, D, total, 0, 0)
    put_vector(small, 3 * blocks, column_sum(total) - token)
    lane = lax.broadcasted_iota(jnp.int32, (24, LANES), 1)
    line = lax.broadcasted_iota(jnp.int32, (24, LANES), 0)
    moved = pltpu.roll(small[...], OUTER_SHIFT, 1)
    above = jnp.where(line == 0, 0.0, pltpu.roll(moved, 1, 0))
    moved = jnp.where(lane < OUTER_SHIFT, above, moved)
    flat[0:OROW_POS, :] = moved[0:OROW_POS]
    grads = [grad_ref[base + 1 : base + SEQ, :].astype(jnp.bfloat16) for base in bases]
    for part in range(PATCH_IN // D):
        columns = slice(part * D, (part + 1) * D)
        block = sum(contract_rows(images[i, :, columns], grads[i]) for i in range(images_here))
        put_block(flat, OROW_PATCH, D, block, part * D, 0)
    for c in range(8):
        head[c] = contract_rows(normed_final[...], logit_grad[:, c * LANES : (c + 1) * LANES])

    def block_of(p, c):
        return head[c, pl.ds(p, 24, stride=16), :]

    for i in range(125):
        p, start = LANES * i // CLASSES, LANES * i % CLASSES
        c, shift = start // LANES, start % LANES
        value = block_of(p, c)
        if shift:
            value = pltpu.roll(value, LANES - shift, 1)
            if c < 7:
                later = pltpu.roll(block_of(p, c + 1), LANES - shift, 1)
                value = jnp.where(lane < LANES - shift, value, later)
        here = CLASSES - start
        if here < LANES:
            value = jnp.where(lane < here, value, pltpu.roll(block_of(p + 1, 0), here, 1))
        flat[pl.ds(OROW_HEAD + i, 24, stride=125), :] = value
    end = OROW_HEAD + 24 * 125
    flat[end:, :] = jnp.zeros((flat.shape[0] - end, LANES), jnp.float32)
    store_shards(keep_ref, send_ref, flat, masks, half, rows + 1, rows)


def outer_backward(
    grad_state, images, normed_final, logit_grad, vec, rows, padded, plan, devices, order
):
    half = devices // 2
    kernel = functools.partial(outer_grad_kernel, slot_masks(plan, devices), half, rows)
    outs = [((half, padded, LANES), LOW)] * 2
    scratch = [
        ((round_up(2 * half * rows + 1, 8), LANES), WIDE),
        ((CLASS_PAD // LANES, D, LANES), WIDE),
        ((24, LANES), WIDE),
    ]
    args = (grad_state, images, normed_final, logit_grad, vec)
    keep, send = call_kernel(kernel, "outer_backward", 2, 8, outs, scratch, *args)
    order.end(send)
    return Scatter(keep, send, plan, devices, order)


def nesterov(params, momentum, average, grads):
    momentum_new = 0.5 * momentum + grads
    params_new = params - step_rate * (grads + 0.5 * momentum_new)
    return (params_new, momentum_new, 0.5 * average + 0.5 * params_new)


def shards(
    images,
    labels,
    valid,
    layer_params,
    layer_momentum,
    layer_average,
    outer_params,
    outer_momentum,
    outer_average,
):
    devices = lax.axis_size("fsdp")
    layer_rows = layer_params.shape[1] // LANES
    layer_padded = round_up(layer_rows + 3 * devices // LANES + 1, 8)
    outer_rows = outer_params.shape[0] // LANES
    outer_padded = round_up(outer_rows + 1, 16)

    def layer_shard(params, layer_index, tail):
        shard = params[layer_index].reshape(layer_rows, LANES).astype(jnp.bfloat16)
        tail = jnp.pad(tail, ((0, layer_padded - layer_rows - 1), (0, 0)))
        return jnp.concatenate([shard, tail.astype(jnp.bfloat16)])

    outer_shard = jnp.pad(outer_params, (OUTER_SHIFT, LANES - OUTER_SHIFT)).reshape(-1, LANES)
    outer_shard = jnp.pad(outer_shard, ((0, outer_padded - outer_rows - 1), (0, 0)))
    outer_shard = outer_shard.astype(jnp.bfloat16)
    empty = jnp.zeros((1, LANES), jnp.float32)
    first_shard = layer_shard(layer_params, 0, empty)
    order = Order(first_shard)
    one = Gather(first_shard, Z_FIRST, devices, order)
    kept = []

    def forward(state, pieces, plan):
        vec, weights, counts = layer_unpack(pieces, plan, 0, layer_rows)
        state_next, saved = layer_forward(state, vec, weights)
        kept.append((state, vec, weights, saved))
        order.end(state_next)
        return (state_next, counts)

    one.start()
    outer_later = order.begin(outer_shard)
    outer = Gather(outer_later, Z_FIRST, devices, order)
    order.end(outer_later)
    order.fence()
    outer.start()
    params_later, valid_later = order.begin((layer_params, valid))
    count = jnp.sum(valid_later).astype(jnp.float32).reshape(1, 1)
    count_row = jnp.pad(count, ((0, 0), (0, LANES - 1)))
    two = Gather(layer_shard(params_later, 1, count_row), Z_STEPS, devices, order)
    three = Gather(layer_shard(params_later, 2, empty), Z_STEPS, devices, order)
    order.end((two.column, three.column))
    order.fence()
    one.take()
    one.start()
    order.fence()
    two.start()
    order.fence()
    outer.take()
    outer.start()
    order.fence()
    one.take()
    one.start()
    order.fence()
    two.take()
    two.start()
    outer.take()
    outer.start()
    order.fence()
    three.start()
    order.fence()
    two.take()
    two.start()
    order.fence()
    three.take()
    three.start()
    order.fence()
    one.take()
    outer.take()
    two.take()
    two.start()
    three.take()
    three.start()
    outer.start()
    one.start()
    order.fence()
    pieces = outer.take_across()
    state, small, w_head = embed_images(images, pieces, Z_FIRST, outer_rows)
    order.end(state)
    state, unused = forward(state, one.take_across(), Z_FIRST)
    two.take()
    three.take()
    three.start()
    two.start()
    order.fence()
    state, image_counts = forward(state, two.take_across(), Z_STEPS)
    three.take()
    three.start()
    order.fence()
    state, unused = forward(state, three.take_across(), Z_STEPS)
    image_count = image_counts[0, 0]
    extra, grad_state, normed_final, logit_grad, vec_grad = head_step(
        labels, valid, state, small, w_head, image_counts, layer_padded - layer_rows
    )

    def backward(layer_index, grad_state):
        grad_state, factors = layer_backward(order.begin(grad_state), *kept[layer_index])
        order.end(grad_state)
        return (grad_state, factors)

    def packed(factors, plan):
        first, *rest = factors
        factors = (order.begin(first), *rest)
        return weight_grads(
            factors, extra, layer_rows, layer_padded, plan, devices, order
        )

    def turn_back(layer_index, grad_state):
        grad_state, factors = backward(layer_index, grad_state)
        return (grad_state, packed(factors))

    order.fence()
    order.fence()
    grad_state, factors_three = backward(2, grad_state)
    three = packed(factors_three, Z_FIRST)
    three.start()
    three.take()
    three.start()
    grad_state, factors_two = backward(1, grad_state)
    two = packed(factors_two, Z_FIRST)
    three.take()
    order.fence()
    three.start()
    two.start()
    two.take()
    two.start()
    order.fence(20)
    grad_state, factors_one = backward(0, grad_state)
    order.fence()
    three.take()
    three.start()
    one = packed(factors_one, Z_FIRST)
    order.fence()
    order.fence()
    outer = outer_backward(
        order.begin(grad_state),
        images,
        normed_final,
        logit_grad,
        vec_grad,
        outer_rows,
        outer_padded,
        Z_FIRST,
        devices,
        order,
    )
    order.fence()
    three.take()
    outer.start()
    two.take()
    order.fence()
    one.start()
    two.start()
    order.fence()
    order.fence(20)
    one.take()
    one.start()
    outer.take()
    two.take()
    two.start()
    order.fence()
    one.take()
    outer.start()
    order.fence()
    order.fence()
    order.fence()
    two.take()
    one.start()
    one.take()
    one.start()
    outer.take()
    order.fence(20)
    outer.start()
    outer.take()
    outer.start()
    one.take()
    outer.take()
    order.fence()
    sums = (one, two, three)
    layer_summed = [item.total for item in sums]
    outer_summed = outer.total
    loss_sum = jnp.sum(layer_summed[2][layer_rows:]) + order.token[0, 0]
    layer_grads = [summed[:layer_rows].reshape(-1) for summed in layer_summed]
    outer_grad = outer_summed[: outer_rows + 1].reshape(-1)
    outer_grad = outer_grad[OUTER_SHIFT : OUTER_SHIFT + outer_rows * LANES]
    layer_grad = jnp.stack(layer_grads)
    layer_new, layer_mom_new, layer_avg_new = nesterov(
        layer_params, layer_momentum, layer_average, layer_grad
    )
    outer_new, outer_mom_new, outer_avg_new = nesterov(
        outer_params, outer_momentum, outer_average, outer_grad
    )
    return (
        loss_sum,
        image_count,
        layer_new,
        layer_mom_new,
        layer_avg_new,
        outer_new,
        outer_mom_new,
        outer_avg_new,
    )


def solution(mesh):
    return jax.shard_map(
        shards,
        mesh=mesh,
        in_specs=(
            P("fsdp", None, None),
            P("fsdp"),
            P("fsdp"),
            P(None, "fsdp"),
            P(None, "fsdp"),
            P(None, "fsdp"),
            P("fsdp"),
            P("fsdp"),
            P("fsdp"),
        ),
        out_specs=(
            P(),
            P(),
            P(None, "fsdp"),
            P(None, "fsdp"),
            P(None, "fsdp"),
            P("fsdp"),
            P("fsdp"),
            P("fsdp"),
        ),
        check_vma=False,
    )
```

```python
import functools

import jax
import jax.numpy as jnp
import numpy as np
from jax import lax
from jax.experimental import pallas as pl
from jax.experimental.pallas import tpu as pltpu
from jax.sharding import PartitionSpec as P

D = 384
HEADS = 6
HEAD = 64
FF = 1536
CLASSES = 1000
CLASS_PAD = 1024
PATCH_IN = 768
PATCHES = 196
SEQ = 197
LAYERS = 3
LANES = 128
TOKENS = 208

eps_norm = 1e-06
smooth = 0.1
step_rate = 20.0
root_half = 0.7071067811865476
inv_root_two_pi = 0.3989422804014327

MIB = 1024 * 1024


def cost(microseconds):
    return pl.CostEstimate(
        flops=int(microseconds * 1e9), bytes_accessed=int(microseconds * 3.5e6), transcendentals=0
    )


ROW_VEC = 36
ROW_QKV = ROW_VEC
ROW_OUT = ROW_QKV + 3 * D * D // LANES
ROW_UP = ROW_OUT + D * D // LANES
ROW_DOWN = ROW_UP + D * FF // LANES
ROW_END = ROW_DOWN + D * FF // LANES

OUTER_SHIFT = 24
SMALL_ROWS = 4 * D // LANES + CLASS_PAD // LANES
OROW_POS = (4 * D + CLASSES + OUTER_SHIFT) // LANES
OROW_PATCH = OROW_POS + SEQ * D // LANES
OROW_HEAD = OROW_PATCH + PATCH_IN * D // LANES


def round_up(value, unit):
    return (value + unit - 1) // unit * unit


def bits_of(devices):
    count = devices.bit_length() - 1
    assert 1 << count == devices
    return count


def steps_of(plan, devices):
    if devices != 32:
        return [[(1 << bit, 1 << bit)] for bit in range(1, bits_of(devices))]
    kinds = {
        "z": [(8, 8), (16, 16), (24, 24)],
        "z two": [(16, 16)],
        "z one": [(8, 8)],
        "near": [(4, 2)],
        "far": [(2, 4)],
    }
    return [kinds[name] for name in plan]


Z_FIRST = ("z", "near", "far")
Z_STEPS = ("z two", "z one", "near", "far")


def slot_masks(plan, devices):
    masks = [(0, 0)]
    for partners in steps_of(plan, devices):
        masks = masks + [(a ^ p, b ^ q) for p, q in partners for a, b in masks]
    return tuple(zip(*masks))


def swap(values, masks, devices):
    pairs = [(i, i ^ masks[i & 1]) for i in range(devices)]
    return lax.ppermute(values, "fsdp", pairs)


def fence_kernel(token, out):
    out[...] = token[...]


class Order:
    def __init__(self, value):
        self.token = jnp.zeros((8, LANES), jnp.float32)
        self.latest = value

    def begin(self, value):
        value, self.latest, self.token = lax.optimization_barrier(
            (value, self.latest, self.token)
        )
        return value

    def end(self, value):
        self.latest = value
        return value

    def fence(self, microseconds=0.01):
        self.begin(())
        self.token = pl.pallas_call(
            fence_kernel,
            out_shape=jax.ShapeDtypeStruct((8, LANES), jnp.float32),
            in_specs=[pl.BlockSpec(memory_space=pltpu.VMEM)],
            out_specs=pl.BlockSpec(memory_space=pltpu.VMEM),
            compiler_params=pltpu.CompilerParams(vmem_limit_bytes=MIB),
            cost_estimate=cost(microseconds),
            name="fence",
        )(self.token)


class Gather:
    def __init__(self, shard, plan, devices, order):
        self.devices = devices
        self.order = order
        self.steps = steps_of(plan, devices)
        self.column = shard[None]
        self.plan_length = len(plan)

    def start(self):
        while len(self.steps) > self.plan_length:
            self.exchange()
            self.take()
        self.exchange()

    def exchange(self):
        self.column = self.order.begin(self.column)
        partners = self.steps.pop(0) if self.steps else [(1, 1)]
        self.arriving = [swap(self.column, masks, self.devices) for masks in partners]

    def take(self):
        first, *rest = self.arriving
        self.column = jnp.concatenate([self.column, self.order.begin(first)] + rest)
        self.order.end(self.column)

    def take_across(self):
        return (self.column, self.order.end(self.order.begin(self.arriving[0])))


class Scatter:
    def __init__(self, keep, send, plan, devices, order):
        self.devices = devices
        self.order = order
        self.steps = [[(1, 1)]] + steps_of(plan, devices)[::-1]
        self.total = keep
        self.low = [send]
        self.starts = 0
        self.plan_length = len(plan)

    def start(self):
        self.exchange()
        self.starts = self.starts + 1
        while self.starts > self.plan_length and self.steps:
            self.take()
            self.exchange()

    def exchange(self):
        partners = self.steps.pop(0)
        low = self.order.begin(self.low)
        self.arriving = [swap(part, masks, self.devices) for part, masks in zip(low, partners)]

    def take(self):
        first, *rest = self.arriving
        parts = [part.astype(jnp.float32) for part in [self.order.begin(first)] + rest]
        total = self.total.astype(jnp.float32)
        if len(parts) == 3:
            total = total + ((parts[0] + parts[1]) + parts[2])
        else:
            total = total + parts[0]
        if not self.steps:
            self.total = self.order.end(total[0])
            return
        groups = 1 + len(self.steps[0])
        size = total.shape[0] // groups
        self.total = total[:size]
        sent = total[size:].astype(jnp.bfloat16)
        self.low = [sent[i * size : (i + 1) * size] for i in range(groups - 1)]
        self.order.end(sent)


def select_mask(core, masks, slot):
    first, second = masks[0][slot], masks[1][slot]
    if first == second:
        return first
    return jnp.where(core == 0, first, second)


def owner_pairs(masks, half):
    me = lax.axis_index("fsdp")
    core = lax.rem(me, 2)
    other = jnp.bitwise_xor(me, 1)
    return [
        (
            jnp.bitwise_xor(me, select_mask(core, masks, slot)),
            jnp.bitwise_xor(other, select_mask(1 - core, masks, slot)),
        )
        for slot in range(half)
    ]


def load_shards(pieces, flat, masks, half, base, rows):
    for slot, owners in enumerate(owner_pairs(masks, half)):
        for piece, owner in zip(pieces, owners):
            value = piece[slot, base : base + rows, :].astype(jnp.float32)
            flat[pl.ds(owner * rows, rows), :] = value


def store_shards(keep_ref, send_ref, flat, masks, half, rows, stride):
    for slot, owners in enumerate(owner_pairs(masks, half)):
        for ref, owner in zip((keep_ref, send_ref), owners):
            ref[slot, :rows, :] = flat[pl.ds(owner * stride, rows), :].astype(jnp.bfloat16)


def row_vector(ref, row, blocks):
    return jnp.concatenate([ref[row + i : row + i + 1, :] for i in range(blocks)], axis=1)


def put_vector(ref, row, vector):
    for i in range(vector.shape[1] // LANES):
        ref[row + i : row + i + 1, :] = vector[:, i * LANES : (i + 1) * LANES]


def take_matrix(flat, row, height, width):
    blocks = width // LANES
    return [flat[pl.ds(row + c, height, stride=blocks), :] for c in range(blocks)]


def put_block(flat, row, width, block, first_row, first_block):
    blocks = width // LANES
    height = block.shape[0]
    for c in range(block.shape[1] // LANES):
        place = row + first_row * blocks + first_block + c
        flat[pl.ds(place, height, stride=blocks), :] = block[:, c * LANES : (c + 1) * LANES]


def dot_plain(left, right):
    return jnp.dot(left, right, preferred_element_type=jnp.float32)


def contract_rows(left, right):
    return lax.dot_general(
        left, right, (((0,), (0,)), ((), ())), preferred_element_type=jnp.float32
    )


def contract_last(left, right):
    return lax.dot_general(
        left, right, (((1,), (1,)), ((), ())), preferred_element_type=jnp.float32
    )


def norm_parts(values):
    center = values - jnp.mean(values, -1, keepdims=True)
    inverse = lax.rsqrt(jnp.mean(center * center, -1, keepdims=True) + eps_norm)
    return (center * inverse, inverse)


def norm_back(grad_normed, normal, inverse, gain):
    scaled = grad_normed * gain
    return inverse * (
        scaled
        - jnp.mean(scaled, -1, keepdims=True)
        - normal * jnp.mean(scaled * normal, -1, keepdims=True)
    )


def gelu_parts(values):
    below = 0.5 * (1.0 + lax.erf(values * root_half))
    bell = jnp.exp(-0.5 * values * values)
    return (values * below, below + values * bell * inv_root_two_pi)


def column_sum(values):
    return jnp.sum(values, 0, keepdims=True)


def unpack_kernel(
    masks,
    half,
    base,
    rows,
    count_row,
    mine,
    theirs,
    vec,
    count_ref,
    w_qkv,
    w_out,
    w_up,
    w_down,
    flat,
):
    pieces = (mine, theirs)
    load_shards(pieces, flat, masks, half, base, rows)
    vec[...] = flat[0:ROW_VEC, :]
    count = jnp.zeros((1, LANES), jnp.float32)
    for slot in range(half):
        for piece in pieces:
            count = count + piece[slot, count_row : count_row + 1, :].astype(jnp.float32)
    count_ref[...] = count
    for ref, row in ((w_qkv, ROW_QKV), (w_out, ROW_OUT), (w_up, ROW_UP), (w_down, ROW_DOWN)):
        for c, block in enumerate(take_matrix(flat, row, *ref.shape)):
            ref[:, c * LANES : (c + 1) * LANES] = block.astype(jnp.bfloat16)


def call_kernel(kernel, name, microseconds, megabytes, outs, scratch, *args, smem=0):
    spaces = [pltpu.SMEM] * smem + [pltpu.VMEM] * (len(args) - smem)
    return pl.pallas_call(
        kernel,
        out_shape=[jax.ShapeDtypeStruct(shape, kind) for shape, kind in outs],
        in_specs=[pl.BlockSpec(memory_space=space) for space in spaces],
        out_specs=[pl.BlockSpec(memory_space=pltpu.VMEM)] * len(outs),
        scratch_shapes=[pltpu.VMEM(shape, kind) for shape, kind in scratch],
        compiler_params=pltpu.CompilerParams(vmem_limit_bytes=megabytes * MIB),
        cost_estimate=cost(0.01),
        name=name,
    )(*args)


LOW = jnp.bfloat16
WIDE = jnp.float32
MATRICES = [(D, 3 * D), (D, D), (D, FF), (FF, D)]


def layer_unpack(pieces, plan, base, rows):
    half = pieces[0].shape[0]
    kernel = functools.partial(
        unpack_kernel, slot_masks(plan, 2 * half), half, base, rows, base + rows
    )
    outs = [((ROW_VEC, LANES), WIDE), ((1, LANES), WIDE)] + [(shape, LOW) for shape in MATRICES]
    scratch = [((round_up(2 * half * rows, 8), LANES), WIDE)]
    vec, count, *weights = call_kernel(kernel, "layer_unpack", 3, 10, outs, scratch, *pieces)
    return (vec, weights, count)


def forward_kernel(
    state_ref,
    vec,
    w_qkv,
    w_out,
    w_up,
    w_down,
    next_ref,
    qkv,
    probs,
    attended,
    mid,
    active,
    slope,
    normed,
    probs_low,
):
    blocks = D // LANES
    images_here = state_ref.shape[0] // TOKENS
    gain, bias = row_vector(vec, 0, blocks), row_vector(vec, 3, blocks)
    for image in range(images_here):
        place = slice(image * TOKENS, (image + 1) * TOKENS)
        normal, inverse = norm_parts(state_ref[place, :])
        normed[place, :] = (normal * gain + bias).astype(jnp.bfloat16)
    for part in range(3):
        columns = slice(part * D, (part + 1) * D)
        value = dot_plain(normed[...], w_qkv[:, columns])
        if part != 1:
            value = value + row_vector(vec, 12 if part == 0 else 15, blocks)
        qkv[:, columns] = value.astype(jnp.bfloat16)

    left_lane = lax.broadcasted_iota(jnp.int32, (TOKENS, LANES), 1) < HEAD
    real_key = lax.broadcasted_iota(jnp.int32, (TOKENS, TOKENS), 1) < SEQ
    for image in range(images_here):
        place = slice(image * TOKENS, (image + 1) * TOKENS)
        for pair in range(HEADS // 2):
            queries = qkv[place, pair * LANES : (pair + 1) * LANES]
            keys = qkv[place, D + pair * LANES : D + (pair + 1) * LANES]
            for side in range(2):
                own = left_lane if side == 0 else jnp.logical_not(left_lane)
                head_queries = jnp.where(own, queries, jnp.zeros_like(queries))
                scores = contract_last(head_queries, keys) * HEAD ** (-0.5)
                scores = jnp.where(real_key, scores, -1e30)
                exponent = jnp.exp(scores - jnp.max(scores, -1, keepdims=True))
                prob = exponent * (1.0 / jnp.sum(exponent, -1, keepdims=True))
                probs[image * HEADS + 2 * pair + side] = prob
                probs_low[image * HEADS + 2 * pair + side] = prob.astype(jnp.bfloat16)
    for image in range(images_here):
        place = slice(image * TOKENS, (image + 1) * TOKENS)
        for pair in range(HEADS // 2):
            values = qkv[place, 2 * D + pair * LANES : 2 * D + (pair + 1) * LANES]
            head = image * HEADS + 2 * pair
            first = dot_plain(probs_low[head], values)
            second = dot_plain(probs_low[head + 1], values)
            joined = jnp.where(left_lane, first, second)
            attended[place, pair * LANES : (pair + 1) * LANES] = joined.astype(jnp.bfloat16)

    bias_out = row_vector(vec, 18, blocks)
    gain, bias = row_vector(vec, 6, blocks), row_vector(vec, 9, blocks)
    for image in range(images_here):
        place = slice(image * TOKENS, (image + 1) * TOKENS)
        value = state_ref[place, :] + dot_plain(attended[place, :], w_out[...]) + bias_out
        mid[place, :] = value
        normal, inverse = norm_parts(value)
        normed[place, :] = (normal * gain + bias).astype(jnp.bfloat16)
    for part in range(FF // D):
        columns = slice(part * D, (part + 1) * D)
        bias_up = row_vector(vec, 24 + blocks * part, blocks)
        for image in range(images_here):
            place = slice(image * TOKENS, (image + 1) * TOKENS)
            up_value = dot_plain(normed[place, :], w_up[:, columns]) + bias_up
            act, slo = gelu_parts(up_value)
            active[place, columns] = act.astype(jnp.bfloat16)
            slope[place, columns] = slo
    bias_down = row_vector(vec, 21, blocks)
    for image in range(images_here):
        place = slice(image * TOKENS, (image + 1) * TOKENS)
        next_ref[place, :] = mid[place, :] + dot_plain(active[place, :], w_down[...]) + bias_down


def layer_forward(state, vec, weights):
    tokens_here = state.shape[0]
    images_here = tokens_here // TOKENS
    outs = [
        (state.shape, WIDE),
        ((tokens_here, 3 * D), LOW),
        ((images_here * HEADS, TOKENS, TOKENS), WIDE),
        ((tokens_here, D), LOW),
        ((tokens_here, D), WIDE),
        ((tokens_here, FF), LOW),
        ((tokens_here, FF), WIDE),
    ]
    scratch = [(state.shape, LOW), (outs[2][0], LOW)]
    state_next, *saved = call_kernel(
        forward_kernel, "layer_forward", 7, 8, outs, scratch, state, vec, *weights
    )
    return (state_next, saved)


def backward_kernel(
    grad_ref,
    state_ref,
    vec,
    w_qkv,
    w_out,
    w_up,
    w_down,
    qkv,
    probs,
    mid,
    slope,
    grad_in_ref,
    sums_ref,
    grad_up,
    normed_two,
    grad_low,
    grad_qkv,
    normed_one,
    attended,
    grad_mid,
    grad_scores,
    probs_low,
):
    blocks = D // LANES
    images_here = grad_ref.shape[0] // TOKENS
    places = [slice(i * TOKENS, (i + 1) * TOKENS) for i in range(images_here)]
    put_vector(sums_ref, 21, column_sum(grad_ref[...]))
    grad_low[...] = grad_ref[...].astype(jnp.bfloat16)
    for part in range(FF // D):
        columns = slice(part * D, (part + 1) * D)
        total = 0.0
        for place in places:
            value = contract_last(grad_low[place, :], w_down[columns, :]) * slope[place, columns]
            total = total + column_sum(value)
            grad_up[place, columns] = value.astype(jnp.bfloat16)
        put_vector(sums_ref, 24 + blocks * part, total)
    gain, bias = row_vector(vec, 6, blocks), row_vector(vec, 9, blocks)
    sums = [0.0, 0.0, 0.0]
    for place in places:
        normal, inverse = norm_parts(mid[place, :])
        normed_two[place, :] = (normal * gain + bias).astype(jnp.bfloat16)
        grad_normed = contract_last(grad_up[place, :], w_up[...])
        sums[0] = sums[0] + column_sum(grad_normed * normal)
        sums[1] = sums[1] + column_sum(grad_normed)
        value = grad_ref[place, :] + norm_back(grad_normed, normal, inverse, gain)
        sums[2] = sums[2] + column_sum(value)
        grad_mid[place, :] = value
        grad_low[place, :] = value.astype(jnp.bfloat16)
    put_vector(sums_ref, 6, sums[0])
    put_vector(sums_ref, 9, sums[1])
    put_vector(sums_ref, 18, sums[2])
    for place in places:
        attended[place, :] = contract_last(grad_low[place, :], w_out[...]).astype(jnp.bfloat16)
    left_lane = lax.broadcasted_iota(jnp.int32, (TOKENS, LANES), 1) < HEAD
    for pair in range(HEADS // 2):
        for image, place in enumerate(places):
            values = qkv[place, 2 * D + pair * LANES : 2 * D + (pair + 1) * LANES]
            grad_here = attended[place, pair * LANES : (pair + 1) * LANES]
            for side in range(2):
                head = image * HEADS + 2 * pair + side
                own = left_lane if side == 0 else jnp.logical_not(left_lane)
                head_grad = jnp.where(own, grad_here, jnp.zeros_like(grad_here))
                prob = probs[head]
                grad_probs = contract_last(head_grad, values)
                inner = jnp.sum(grad_probs * prob, -1, keepdims=True)
                grad_scores[head] = (prob * (grad_probs - inner) * HEAD ** (-0.5)).astype(
                    jnp.bfloat16
                )
                probs_low[head] = prob.astype(jnp.bfloat16)
    for pair in range(HEADS // 2):
        sum_query, sum_value = 0.0, 0.0
        for image, place in enumerate(places):
            spans = [slice(i * D + pair * LANES, i * D + (pair + 1) * LANES) for i in range(3)]
            queries, keys = qkv[place, spans[0]], qkv[place, spans[1]]
            grad_here = attended[place, pair * LANES : (pair + 1) * LANES]
            results = []
            for side in range(2):
                head = image * HEADS + 2 * pair + side
                grad_queries = dot_plain(grad_scores[head], keys)
                grad_keys = contract_rows(grad_scores[head], queries)
                grad_values = contract_rows(probs_low[head], grad_here)
                results.append((grad_queries, grad_keys, grad_values))
            joined = [jnp.where(left_lane, results[0][i], results[1][i]) for i in range(3)]
            for i in range(3):
                grad_qkv[place, spans[i]] = joined[i].astype(jnp.bfloat16)
            sum_query = sum_query + column_sum(joined[0])
            sum_value = sum_value + column_sum(joined[2])
        put_vector(sums_ref, 12 + pair, sum_query)
        put_vector(sums_ref, 15 + pair, sum_value)
    gain, bias = row_vector(vec, 0, blocks), row_vector(vec, 3, blocks)
    sums = [0.0, 0.0]
    for place in places:
        normal, inverse = norm_parts(state_ref[place, :])
        normed_one[place, :] = (normal * gain + bias).astype(jnp.bfloat16)
        grad_normed = contract_last(grad_qkv[place, :], w_qkv[...])
        sums[0] = sums[0] + column_sum(grad_normed * normal)
        sums[1] = sums[1] + column_sum(grad_normed)
        grad_in_ref[place, :] = grad_mid[place, :] + norm_back(grad_normed, normal, inverse, gain)
    put_vector(sums_ref, 0, sums[0])
    put_vector(sums_ref, 3, sums[1])


def layer_backward(grad_state, state, vec, weights, saved):
    qkv, probs, attended, mid, active, slope = saved
    tokens_here = grad_state.shape[0]
    outs = [(grad_state.shape, WIDE), ((ROW_VEC, LANES), WIDE)]
    outs = outs + [((tokens_here, width), LOW) for width in (FF, D, D, 3 * D, D)]
    scratch = [(grad_state.shape, LOW), (grad_state.shape, WIDE)] + [(probs.shape, LOW)] * 2
    args = [grad_state, state, vec, *weights, qkv, probs, mid, slope]
    outs = call_kernel(backward_kernel, "layer_backward", 7, 10, outs, scratch, *args)
    grad_in, sums, up_low, normed_two, mid_low, qkv_low, normed_one = outs
    factors = (active, normed_two, up_low, attended, mid_low, normed_one, qkv_low)
    return (grad_in, (sums, grad_state, *factors))


def weight_grad_kernel(
    masks,
    half,
    rows,
    extra,
    sums_ref,
    grad_ref,
    active,
    normed_two,
    grad_up,
    attended,
    mid_low,
    normed_one,
    grad_qkv,
    keep_ref,
    send_ref,
    grad_low,
    flat,
):
    blocks = D // LANES
    flat[0:ROW_VEC, :] = sums_ref[...]
    flat[ROW_END:, :] = jnp.zeros((flat.shape[0] - ROW_END, LANES), jnp.float32)
    grad_low[...] = grad_ref[...].astype(jnp.bfloat16)
    for part in range(FF // D):
        columns = slice(part * D, (part + 1) * D)
        block = contract_rows(active[:, columns], grad_low[...])
        put_block(flat, ROW_DOWN, D, block, part * D, 0)
    for part in range(FF // D):
        columns = slice(part * D, (part + 1) * D)
        block = contract_rows(normed_two[...], grad_up[:, columns])
        put_block(flat, ROW_UP, FF, block, 0, blocks * part)
    put_block(flat, ROW_OUT, D, contract_rows(attended[...], mid_low[...]), 0, 0)
    for part in range(3):
        columns = slice(part * D, (part + 1) * D)
        block = contract_rows(normed_one[...], grad_qkv[:, columns])
        put_block(flat, ROW_QKV, 3 * D, block, 0, blocks * part)
    store_shards(keep_ref, send_ref, flat, masks, half, rows, rows)
    tail = extra[...]
    for slot in range(half):
        keep_ref[slot, rows:, :] = tail
        send_ref[slot, rows:, :] = tail


def weight_grads(factors, extra, rows, padded, plan, devices, order):
    half = devices // 2
    kernel = functools.partial(weight_grad_kernel, slot_masks(plan, devices), half, rows)
    outs = [((half, padded, LANES), LOW)] * 2
    scratch = [(factors[1].shape, LOW), ((round_up(2 * half * rows, 8), LANES), WIDE)]
    keep, send = call_kernel(kernel, "weight_grads", 4, 10, outs, scratch, extra, *factors)
    order.end(send)
    return Scatter(keep, send, plan, devices, order)


def embed_kernel(
    masks,
    half,
    rows,
    images,
    mine,
    theirs,
    state_ref,
    small_ref,
    head_ref,
    flat,
    head,
    patch,
    position,
):
    pieces = (mine, theirs)
    for shard in range(2 * half + 1):
        flat[shard * rows : shard * rows + 1, :] = jnp.zeros((1, LANES), jnp.float32)
    for slot, owners in enumerate(owner_pairs(masks, half)):
        for piece, owner in zip(pieces, owners):
            value = piece[slot, : rows + 1, :].astype(jnp.float32)
            flat[pl.ds(owner * rows + 1, rows - 1), :] = value[1:rows]
            flat[pl.ds(owner * rows, 1), :] += value[0:1]
            flat[pl.ds((owner + 1) * rows, 1), :] += value[rows : rows + 1]
    lane = lax.broadcasted_iota(jnp.int32, (24, LANES), 1)
    low = pltpu.roll(flat[0:24, :], LANES - OUTER_SHIFT, 1)
    later = pltpu.roll(flat[1:25, :], LANES - OUTER_SHIFT, 1)
    small = jnp.where(lane < LANES - OUTER_SHIFT, low, later)
    line = lax.broadcasted_iota(jnp.int32, (24, LANES), 0)
    past = (line - 4 * D // LANES) * LANES + lane >= CLASSES
    small_ref[...] = jnp.where(past, 0.0, small)
    blocks = D // LANES
    for c, block in enumerate(take_matrix(flat, OROW_POS, SEQ, D)):
        position[:SEQ, c * LANES : (c + 1) * LANES] = block
    for c, block in enumerate(take_matrix(flat, OROW_PATCH, PATCH_IN, D)):
        patch[:, c * LANES : (c + 1) * LANES] = block.astype(jnp.bfloat16)
    bias_patch = row_vector(small_ref, 3 * blocks, blocks)
    for image in range(images.shape[0]):
        base = image * TOKENS
        state_ref[base + SEQ : base + TOKENS, :] = jnp.zeros((TOKENS - SEQ, D), jnp.float32)
        state_ref[base : base + 1, :] = row_vector(small_ref, 0, blocks) + position[0:1, :]
        value = dot_plain(images[image], patch[...]) + bias_patch
        state_ref[base + 1 : base + SEQ, :] = value + position[1:SEQ, :]
    for p in range(16):
        shift, base = (CLASSES * p) % LANES, OROW_HEAD + (CLASSES * p) // LANES
        part = [flat[pl.ds(base + c, 24, stride=125), :] for c in range(9 if shift else 8)]
        if shift:
            part = [pltpu.roll(block, LANES - shift, 1) for block in part]
        for c in range(8):
            block = jnp.where(lane < LANES - shift, part[c], part[c + 1]) if shift else part[c]
            if c == 7:
                block = jnp.where(lane < CLASSES - 7 * LANES, block, 0.0)
            head[c, pl.ds(p, 24, stride=16), :] = block
    for c in range(8):
        head_ref[:, c * LANES : (c + 1) * LANES] = head[c].astype(jnp.bfloat16)


def embed_images(images, pieces, plan, rows):
    half = pieces[0].shape[0]
    kernel = functools.partial(embed_kernel, slot_masks(plan, 2 * half), half, rows)
    outs = [
        ((images.shape[0] * TOKENS, D), WIDE),
        ((24, LANES), WIDE),
        ((D, CLASS_PAD), LOW),
    ]
    scratch = [
        ((round_up(2 * half * rows + 1, 8), LANES), WIDE),
        ((CLASS_PAD // LANES, D, LANES), WIDE),
        ((PATCH_IN, D), LOW),
        ((TOKENS, D), WIDE),
    ]
    return call_kernel(kernel, "embed_images", 2, 8, outs, scratch, images, *pieces)


def head_kernel(
    labels,
    valid,
    state_ref,
    small,
    w_head,
    count,
    extra_ref,
    grad_ref,
    normed_ref,
    logit_grad_ref,
    vec_ref,
    rows_in,
):
    blocks = D // LANES
    images_here = state_ref.shape[0] // TOKENS
    rows_in[...] = jnp.zeros(rows_in.shape, jnp.float32)
    for image in range(images_here):
        rows_in[image : image + 1, :] = state_ref[image * TOKENS : image * TOKENS + 1, :]
    normal, inverse = norm_parts(rows_in[...])
    gain, bias = row_vector(small, blocks, blocks), row_vector(small, 2 * blocks, blocks)
    normed_final = (normal * gain + bias).astype(jnp.bfloat16)
    bias_head = row_vector(small, 4 * blocks, CLASS_PAD // LANES)
    logits = dot_plain(normed_final, w_head[...]) + bias_head
    shape = logits.shape
    column = lax.broadcasted_iota(jnp.int32, shape, 1)
    line = lax.broadcasted_iota(jnp.int32, (shape[0], 1), 0)
    real = column < CLASSES
    label = jnp.zeros((shape[0], 1), jnp.int32)
    present = jnp.zeros((shape[0], 1), jnp.float32)
    for image in range(images_here):
        label = jnp.where(line == image, labels[image], label)
        present = jnp.where(line == image, valid[image].astype(jnp.float32), present)
    top_logit = jnp.max(jnp.where(real, logits, -1e30), -1, keepdims=True)
    exponent = jnp.where(real, jnp.exp(jnp.minimum(logits - top_logit, 0.0)), 0.0)
    total_exp = jnp.sum(exponent, -1, keepdims=True)
    log_total = jnp.log(total_exp) + top_logit
    target = jnp.where(column == label, 1.0 - smooth + smooth / CLASSES, smooth / CLASSES)
    target = jnp.where(real, target, 0.0)
    per_image = log_total - jnp.sum(target * logits, -1, keepdims=True)
    loss_here = jnp.sum(present * per_image, 0, keepdims=True)
    loss_high = loss_here.astype(jnp.bfloat16).astype(jnp.float32)
    loss_mid = (loss_here - loss_high).astype(jnp.bfloat16).astype(jnp.float32)
    loss_low = loss_here - loss_high - loss_mid
    me = lax.axis_index("fsdp")
    spare = extra_ref.shape
    place = lax.broadcasted_iota(jnp.int32, spare, 0) * LANES
    place = place + lax.broadcasted_iota(jnp.int32, spare, 1)
    extra = jnp.where(place == 3 * me, loss_high, 0.0)
    extra = jnp.where(place == 3 * me + 1, loss_mid, extra)
    extra_ref[...] = jnp.where(place == 3 * me + 2, loss_low, extra).astype(jnp.bfloat16)

    scale = present * (1.0 / count[0:1, 0:1])
    grad_logits = (exponent * (1.0 / total_exp) - target) * scale
    grad_logits_low = grad_logits.astype(jnp.bfloat16)
    grad_normed = contract_last(grad_logits_low, w_head[...])
    grad_final = norm_back(grad_normed, normal, inverse, gain)
    grad_ref[...] = jnp.zeros(grad_ref.shape, jnp.float32)
    for image in range(images_here):
        grad_ref[image * TOKENS : image * TOKENS + 1, :] = grad_final[image : image + 1, :]
    normed_ref[...] = jnp.where(line < images_here, normed_final, jnp.zeros_like(normed_final))
    logit_grad_ref[...] = grad_logits_low
    vec_ref[...] = jnp.zeros(vec_ref.shape, jnp.float32)
    put_vector(vec_ref, blocks, column_sum(grad_normed * normal))
    put_vector(vec_ref, 2 * blocks, column_sum(grad_normed))
    put_vector(vec_ref, 4 * blocks, column_sum(grad_logits))


def head_step(labels, valid, state, small, w_head, count, spare):
    lines = 16
    outs = [
        ((spare, LANES), LOW),
        (state.shape, WIDE),
        ((lines, D), LOW),
        ((lines, CLASS_PAD), LOW),
        ((24, LANES), WIDE),
    ]
    args = (labels, valid, state, small, w_head, count)
    return call_kernel(head_kernel, "head_step", 2, 4, outs, [((lines, D), WIDE)], *args, smem=2)


def outer_grad_kernel(
    masks,
    half,
    rows,
    grad_ref,
    images,
    normed_final,
    logit_grad,
    vec,
    keep_ref,
    send_ref,
    flat,
    head,
    small,
):
    blocks = D // LANES
    images_here = images.shape[0]
    bases = [image * TOKENS for image in range(images_here)]
    small[...] = vec[...]
    token = sum(grad_ref[base : base + 1, :] for base in bases)
    put_vector(small, 0, token)
    total = sum(grad_ref[base : base + SEQ, :] for base in bases)
    put_block(flat, OROW_POS, D, total, 0, 0)
    put_vector(small, 3 * blocks, column_sum(total) - token)
    lane = lax.broadcasted_iota(jnp.int32, (24, LANES), 1)
    line = lax.broadcasted_iota(jnp.int32, (24, LANES), 0)
    moved = pltpu.roll(small[...], OUTER_SHIFT, 1)
    above = jnp.where(line == 0, 0.0, pltpu.roll(moved, 1, 0))
    moved = jnp.where(lane < OUTER_SHIFT, above, moved)
    flat[0:OROW_POS, :] = moved[0:OROW_POS]
    grads = [grad_ref[base + 1 : base + SEQ, :].astype(jnp.bfloat16) for base in bases]
    for part in range(PATCH_IN // D):
        columns = slice(part * D, (part + 1) * D)
        block = sum(contract_rows(images[i, :, columns], grads[i]) for i in range(images_here))
        put_block(flat, OROW_PATCH, D, block, part * D, 0)
    for c in range(8):
        head[c] = contract_rows(normed_final[...], logit_grad[:, c * LANES : (c + 1) * LANES])

    def block_of(p, c):
        return head[c, pl.ds(p, 24, stride=16), :]

    for i in range(125):
        p, start = LANES * i // CLASSES, LANES * i % CLASSES
        c, shift = start // LANES, start % LANES
        value = block_of(p, c)
        if shift:
            value = pltpu.roll(value, LANES - shift, 1)
            if c < 7:
                later = pltpu.roll(block_of(p, c + 1), LANES - shift, 1)
                value = jnp.where(lane < LANES - shift, value, later)
        here = CLASSES - start
        if here < LANES:
            value = jnp.where(lane < here, value, pltpu.roll(block_of(p + 1, 0), here, 1))
        flat[pl.ds(OROW_HEAD + i, 24, stride=125), :] = value
    end = OROW_HEAD + 24 * 125
    flat[end:, :] = jnp.zeros((flat.shape[0] - end, LANES), jnp.float32)
    store_shards(keep_ref, send_ref, flat, masks, half, rows + 1, rows)


def outer_backward(
    grad_state, images, normed_final, logit_grad, vec, rows, padded, plan, devices, order
):
    half = devices // 2
    kernel = functools.partial(outer_grad_kernel, slot_masks(plan, devices), half, rows)
    outs = [((half, padded, LANES), LOW)] * 2
    scratch = [
        ((round_up(2 * half * rows + 1, 8), LANES), WIDE),
        ((CLASS_PAD // LANES, D, LANES), WIDE),
        ((24, LANES), WIDE),
    ]
    args = (grad_state, images, normed_final, logit_grad, vec)
    keep, send = call_kernel(kernel, "outer_backward", 2, 8, outs, scratch, *args)
    order.end(send)
    return Scatter(keep, send, plan, devices, order)


def outer_update_kernel(
    total, params, momentum, average, params_out, momentum_out, average_out
):
    rows = params.shape[0]
    lane = lax.broadcasted_iota(jnp.int32, (rows, LANES), 1)
    here = pltpu.roll(total[0:rows, :], LANES - OUTER_SHIFT, 1)
    later = pltpu.roll(total[1 : rows + 1, :], LANES - OUTER_SHIFT, 1)
    grads = jnp.where(lane < LANES - OUTER_SHIFT, here, later)
    results = nesterov(params[...], momentum[...], average[...], grads)
    for ref, value in zip((params_out, momentum_out, average_out), results):
        ref[...] = value


def outer_update(total, *args):
    args = [arg.reshape(-1, LANES) for arg in args]
    outs = [(arg.shape, WIDE) for arg in args]
    results = call_kernel(outer_update_kernel, "outer_update", 1, 4, outs, [], total, *args)
    return [result.reshape(-1) for result in results]


def nesterov(params, momentum, average, grads):
    momentum_new = 0.5 * momentum + grads
    params_new = params - step_rate * (grads + 0.5 * momentum_new)
    return (params_new, momentum_new, 0.5 * average + 0.5 * params_new)


def shards(
    images,
    labels,
    valid,
    layer_params,
    layer_momentum,
    layer_average,
    outer_params,
    outer_momentum,
    outer_average,
):
    devices = lax.axis_size("fsdp")
    layer_rows = layer_params.shape[1] // LANES
    layer_padded = round_up(layer_rows + 3 * devices // LANES + 1, 8)
    outer_rows = outer_params.shape[0] // LANES
    outer_padded = round_up(outer_rows + 1, 16)

    def layer_shard(params, layer_index, tail):
        shard = params[layer_index].reshape(layer_rows, LANES).astype(jnp.bfloat16)
        tail = jnp.pad(tail, ((0, layer_padded - layer_rows - 1), (0, 0)))
        return jnp.concatenate([shard, tail.astype(jnp.bfloat16)])

    outer_shard = jnp.pad(outer_params, (OUTER_SHIFT, LANES - OUTER_SHIFT)).reshape(-1, LANES)
    outer_shard = jnp.pad(outer_shard, ((0, outer_padded - outer_rows - 1), (0, 0)))
    outer_shard = outer_shard.astype(jnp.bfloat16)
    empty = jnp.zeros((1, LANES), jnp.float32)
    first_shard = layer_shard(layer_params, 0, empty)
    order = Order(first_shard)
    one = Gather(first_shard, Z_FIRST, devices, order)
    kept = []

    def forward(state, pieces, plan):
        vec, weights, counts = layer_unpack(pieces, plan, 0, layer_rows)
        state_next, saved = layer_forward(state, vec, weights)
        kept.append((state, vec, weights, saved))
        order.end(state_next)
        return (state_next, counts)

    one.start()
    outer_later = order.begin(outer_shard)
    outer = Gather(outer_later, Z_FIRST, devices, order)
    order.end(outer_later)
    order.fence()
    outer.start()
    params_later, valid_later = order.begin((layer_params, valid))
    count = jnp.sum(valid_later).astype(jnp.float32).reshape(1, 1)
    count_row = jnp.pad(count, ((0, 0), (0, LANES - 1)))
    two = Gather(layer_shard(params_later, 1, count_row), Z_STEPS, devices, order)
    three = Gather(layer_shard(params_later, 2, empty), Z_STEPS, devices, order)
    order.end((two.column, three.column))
    order.fence()
    one.take()
    one.start()
    order.fence()
    two.start()
    order.fence()
    outer.take()
    outer.start()
    order.fence()
    one.take()
    one.start()
    order.fence()
    two.take()
    two.start()
    outer.take()
    outer.start()
    order.fence()
    three.start()
    order.fence()
    two.take()
    two.start()
    order.fence()
    three.take()
    three.start()
    order.fence()
    one.take()
    outer.take()
    two.take()
    two.start()
    three.take()
    three.start()
    outer.start()
    one.start()
    order.fence()
    pieces = outer.take_across()
    state, small, w_head = embed_images(images, pieces, Z_FIRST, outer_rows)
    order.end(state)
    state, unused = forward(state, one.take_across(), Z_FIRST)
    two.take()
    three.take()
    three.start()
    two.start()
    order.fence()
    state, image_counts = forward(state, two.take_across(), Z_STEPS)
    three.take()
    three.start()
    order.fence()
    state, unused = forward(state, three.take_across(), Z_STEPS)
    image_count = image_counts[0, 0]
    extra, grad_state, normed_final, logit_grad, vec_grad = head_step(
        labels, valid, state, small, w_head, image_counts, layer_padded - layer_rows
    )

    def backward(layer_index, grad_state):
        grad_state, factors = layer_backward(order.begin(grad_state), *kept[layer_index])
        order.end(grad_state)
        return (grad_state, factors)

    def packed(factors, plan):
        first, *rest = factors
        factors = (order.begin(first), *rest)
        return weight_grads(
            factors, extra, layer_rows, layer_padded, plan, devices, order
        )

    def turn_back(layer_index, grad_state):
        grad_state, factors = backward(layer_index, grad_state)
        return (grad_state, packed(factors))

    order.fence()
    order.fence()
    grad_state, factors_three = backward(2, grad_state)
    three = packed(factors_three, Z_FIRST)
    three.start()
    three.take()
    three.start()
    grad_state, factors_two = backward(1, grad_state)
    two = packed(factors_two, Z_FIRST)
    three.take()
    order.fence()
    three.start()
    two.start()
    two.take()
    two.start()
    order.fence(20)
    grad_state, factors_one = backward(0, grad_state)
    order.fence()
    three.take()
    three.start()
    one = packed(factors_one, Z_FIRST)
    order.fence()
    order.fence()
    outer = outer_backward(
        order.begin(grad_state),
        images,
        normed_final,
        logit_grad,
        vec_grad,
        outer_rows,
        outer_padded,
        Z_FIRST,
        devices,
        order,
    )
    order.fence()
    three.take()
    outer.start()
    two.take()
    order.fence()
    one.start()
    two.start()
    order.fence()
    order.fence(20)
    one.take()
    one.start()
    outer.take()
    two.take()
    two.start()
    order.fence()
    one.take()
    outer.start()
    order.fence()
    order.fence()
    order.fence()
    two.take()
    one.start()
    one.take()
    one.start()
    outer.take()
    order.fence(20)
    outer.start()
    outer.take()
    outer.start()
    one.take()
    outer.take()
    order.fence()
    sums = (one, two, three)
    layer_summed = [item.total for item in sums]
    outer_summed = outer.total
    loss_sum = jnp.sum(layer_summed[2][layer_rows:]) + order.token[0, 0]
    layer_grads = [summed[:layer_rows].reshape(-1) for summed in layer_summed]
    layer_grad = jnp.stack(layer_grads)
    layer_new, layer_mom_new, layer_avg_new = nesterov(
        layer_params, layer_momentum, layer_average, layer_grad
    )
    outer_new, outer_mom_new, outer_avg_new = outer_update(
        outer_summed, outer_params, outer_momentum, outer_average
    )
    return (
        loss_sum,
        image_count,
        layer_new,
        layer_mom_new,
        layer_avg_new,
        outer_new,
        outer_mom_new,
        outer_avg_new,
    )


def solution(mesh):
    return jax.shard_map(
        shards,
        mesh=mesh,
        in_specs=(
            P("fsdp", None, None),
            P("fsdp"),
            P("fsdp"),
            P(None, "fsdp"),
            P(None, "fsdp"),
            P(None, "fsdp"),
            P("fsdp"),
            P("fsdp"),
            P("fsdp"),
        ),
        out_specs=(
            P(),
            P(),
            P(None, "fsdp"),
            P(None, "fsdp"),
            P(None, "fsdp"),
            P("fsdp"),
            P("fsdp"),
            P("fsdp"),
        ),
        check_vma=False,
    )
```

```python
import functools

import jax
import jax.numpy as jnp
import numpy as np
from jax import lax
from jax.experimental import pallas as pl
from jax.experimental.pallas import tpu as pltpu
from jax.sharding import PartitionSpec as P

D = 384
HEADS = 6
HEAD = 64
FF = 1536
CLASSES = 1000
CLASS_PAD = 1024
PATCH_IN = 768
PATCHES = 196
SEQ = 197
LAYERS = 3
LANES = 128
TOKENS = 208

eps_norm = 1e-06
smooth = 0.1
step_rate = 20.0
root_half = 0.7071067811865476
inv_root_two_pi = 0.3989422804014327

MIB = 1024 * 1024


def cost(microseconds):
    return pl.CostEstimate(
        flops=int(microseconds * 1e9), bytes_accessed=int(microseconds * 3.5e6), transcendentals=0
    )


ROW_VEC = 36
ROW_QKV = ROW_VEC
ROW_OUT = ROW_QKV + 3 * D * D // LANES
ROW_UP = ROW_OUT + D * D // LANES
ROW_DOWN = ROW_UP + D * FF // LANES
ROW_END = ROW_DOWN + D * FF // LANES

OUTER_SHIFT = 24
SMALL_ROWS = 4 * D // LANES + CLASS_PAD // LANES
OROW_POS = (4 * D + CLASSES + OUTER_SHIFT) // LANES
OROW_PATCH = OROW_POS + SEQ * D // LANES
OROW_HEAD = OROW_PATCH + PATCH_IN * D // LANES


def round_up(value, unit):
    return (value + unit - 1) // unit * unit


def bits_of(devices):
    count = devices.bit_length() - 1
    assert 1 << count == devices
    return count


def steps_of(plan, devices):
    if devices != 32:
        return [[(1 << bit, 1 << bit)] for bit in range(1, bits_of(devices))]
    kinds = {
        "z": [(8, 8), (16, 16), (24, 24)],
        "z two": [(16, 16)],
        "z one": [(8, 8)],
        "near": [(4, 2)],
        "far": [(2, 4)],
    }
    return [kinds[name] for name in plan]


Z_FIRST = ("z", "near", "far")
Z_STEPS = ("z two", "z one", "near", "far")


def slot_masks(plan, devices):
    masks = [(0, 0)]
    for partners in steps_of(plan, devices):
        masks = masks + [(a ^ p, b ^ q) for p, q in partners for a, b in masks]
    return tuple(zip(*masks))


def swap(values, masks, devices):
    pairs = [(i, i ^ masks[i & 1]) for i in range(devices)]
    return lax.ppermute(values, "fsdp", pairs)


def fence_kernel(token, out):
    out[...] = token[...]


class Order:
    def __init__(self, value):
        self.token = jnp.zeros((8, LANES), jnp.float32)
        self.latest = value

    def begin(self, value):
        value, self.latest, self.token = lax.optimization_barrier(
            (value, self.latest, self.token)
        )
        return value

    def end(self, value):
        self.latest = value
        return value

    def fence(self, microseconds=0.01):
        self.begin(())
        self.token = pl.pallas_call(
            fence_kernel,
            out_shape=jax.ShapeDtypeStruct((8, LANES), jnp.float32),
            in_specs=[pl.BlockSpec(memory_space=pltpu.VMEM)],
            out_specs=pl.BlockSpec(memory_space=pltpu.VMEM),
            compiler_params=pltpu.CompilerParams(vmem_limit_bytes=MIB),
            cost_estimate=cost(microseconds),
            name="fence",
        )(self.token)


class Gather:
    def __init__(self, shard, plan, devices, order, halves=False):
        self.halves = halves
        self.devices = devices
        self.order = order
        self.steps = steps_of(plan, devices)
        self.column = shard[None]
        self.plan_length = len(plan)

    def start(self):
        while len(self.steps) > self.plan_length:
            self.exchange()
            self.take()
        self.exchange()

    def exchange(self):
        self.column = self.order.begin(self.column)
        if not self.steps:
            half = self.column.shape[0] // 2
            value = self.column[half:] if self.halves else self.column
            self.arriving = [swap(value, (1, 1), self.devices)]
            return
        partners = self.steps.pop(0)
        self.arriving = [swap(self.column, masks, self.devices) for masks in partners]
        if self.halves and not self.steps:
            self.early = [swap(self.column, (1, 1), self.devices)]

    def take(self):
        if self.halves and not self.steps:
            self.early = [self.order.end(self.order.begin(self.early[0]))]
        first, *rest = self.arriving
        self.column = jnp.concatenate([self.column, self.order.begin(first)] + rest)
        self.order.end(self.column)

    def take_across(self):
        last = self.order.end(self.order.begin(self.arriving[0]))
        return (self.column, *(self.early if self.halves else ()), last)


class Scatter:
    def __init__(self, keep, sends, plan, devices, order):
        self.devices = devices
        self.order = order
        self.steps = [[(1, 1)] * len(sends)] + steps_of(plan, devices)[::-1]
        self.total = keep
        self.low = sends[::-1]
        self.late = None
        self.starts = 0
        self.plan_length = len(plan)

    def start(self):
        self.exchange()
        self.starts = self.starts + 1
        while self.starts > self.plan_length and self.steps:
            self.take()
            self.exchange()

    def exchange(self):
        partners = self.steps.pop(0)
        low = self.order.begin(self.low)
        self.arriving = [swap(part, masks, self.devices) for part, masks in zip(low, partners)]

    def take(self):
        first, *rest = self.arriving
        parts = [part.astype(jnp.float32) for part in [self.order.begin(first)] + rest]
        total = self.total.astype(jnp.float32)
        if len(parts) == 2:
            half = parts[0].shape[0]
            self.total, self.late = total[:half], parts[1]
            self.low = [self.order.end((total[half:] + parts[0]).astype(jnp.bfloat16))]
            return
        if self.late is not None:
            total, self.late = total + self.late, None
        if len(parts) == 3:
            total = total + ((parts[0] + parts[1]) + parts[2])
        else:
            total = total + parts[0]
        if not self.steps:
            self.total = self.order.end(total[0])
            return
        groups = 1 + len(self.steps[0])
        size = total.shape[0] // groups
        self.total = total[:size]
        sent = total[size:].astype(jnp.bfloat16)
        self.low = [sent[i * size : (i + 1) * size] for i in range(groups - 1)]
        self.order.end(sent)


def select_mask(core, masks, slot):
    first, second = masks[0][slot], masks[1][slot]
    if first == second:
        return first
    return jnp.where(core == 0, first, second)


def owner_pairs(masks, half):
    me = lax.axis_index("fsdp")
    core = lax.rem(me, 2)
    other = jnp.bitwise_xor(me, 1)
    return [
        (
            jnp.bitwise_xor(me, select_mask(core, masks, slot)),
            jnp.bitwise_xor(other, select_mask(1 - core, masks, slot)),
        )
        for slot in range(half)
    ]


def load_shards(pieces, flat, masks, half, base, rows):
    mine, *theirs = pieces
    size = half // len(theirs)
    for slot, (own, other) in enumerate(owner_pairs(masks, half)):
        value = mine[slot, base : base + rows, :].astype(jnp.float32)
        flat[pl.ds(own * rows, rows), :] = value
        value = theirs[slot // size][slot % size, base : base + rows, :].astype(jnp.float32)
        flat[pl.ds(other * rows, rows), :] = value


def store_shards(keep_ref, send_refs, flat, masks, half, rows, stride):
    size = half // len(send_refs)
    for slot, (own, other) in enumerate(owner_pairs(masks, half)):
        keep_ref[slot, :rows, :] = flat[pl.ds(own * stride, rows), :].astype(jnp.bfloat16)
        value = flat[pl.ds(other * stride, rows), :].astype(jnp.bfloat16)
        send_refs[slot // size][slot % size, :rows, :] = value


def row_vector(ref, row, blocks):
    return jnp.concatenate([ref[row + i : row + i + 1, :] for i in range(blocks)], axis=1)


def put_vector(ref, row, vector):
    for i in range(vector.shape[1] // LANES):
        ref[row + i : row + i + 1, :] = vector[:, i * LANES : (i + 1) * LANES]


def take_matrix(flat, row, height, width):
    blocks = width // LANES
    return [flat[pl.ds(row + c, height, stride=blocks), :] for c in range(blocks)]


def put_block(flat, row, width, block, first_row, first_block):
    blocks = width // LANES
    height = block.shape[0]
    for c in range(block.shape[1] // LANES):
        place = row + first_row * blocks + first_block + c
        flat[pl.ds(place, height, stride=blocks), :] = block[:, c * LANES : (c + 1) * LANES]


def dot_plain(left, right):
    return jnp.dot(left, right, preferred_element_type=jnp.float32)


def contract_rows(left, right):
    return lax.dot_general(
        left, right, (((0,), (0,)), ((), ())), preferred_element_type=jnp.float32
    )


def contract_last(left, right):
    return lax.dot_general(
        left, right, (((1,), (1,)), ((), ())), preferred_element_type=jnp.float32
    )


def norm_parts(values):
    center = values - jnp.mean(values, -1, keepdims=True)
    inverse = lax.rsqrt(jnp.mean(center * center, -1, keepdims=True) + eps_norm)
    return (center * inverse, inverse)


def norm_back(grad_normed, normal, inverse, gain):
    scaled = grad_normed * gain
    return inverse * (
        scaled
        - jnp.mean(scaled, -1, keepdims=True)
        - normal * jnp.mean(scaled * normal, -1, keepdims=True)
    )


def gelu_parts(values):
    below = 0.5 * (1.0 + lax.erf(values * root_half))
    bell = jnp.exp(-0.5 * values * values)
    return (values * below, below + values * bell * inv_root_two_pi)


def column_sum(values):
    return jnp.sum(values, 0, keepdims=True)


def unpack_kernel(masks, half, base, rows, count_row, *refs):
    *pieces, vec, count_ref, w_qkv, w_out, w_up, w_down, flat = refs
    load_shards(pieces, flat, masks, half, base, rows)
    vec[...] = flat[0:ROW_VEC, :]
    count = jnp.zeros((1, LANES), jnp.float32)
    for piece in pieces:
        for slot in range(piece.shape[0]):
            count = count + piece[slot, count_row : count_row + 1, :].astype(jnp.float32)
    count_ref[...] = count
    for ref, row in ((w_qkv, ROW_QKV), (w_out, ROW_OUT), (w_up, ROW_UP), (w_down, ROW_DOWN)):
        for c, block in enumerate(take_matrix(flat, row, *ref.shape)):
            ref[:, c * LANES : (c + 1) * LANES] = block.astype(jnp.bfloat16)


def call_kernel(kernel, name, microseconds, megabytes, outs, scratch, *args, smem=0):
    spaces = [pltpu.SMEM] * smem + [pltpu.VMEM] * (len(args) - smem)
    return pl.pallas_call(
        kernel,
        out_shape=[jax.ShapeDtypeStruct(shape, kind) for shape, kind in outs],
        in_specs=[pl.BlockSpec(memory_space=space) for space in spaces],
        out_specs=[pl.BlockSpec(memory_space=pltpu.VMEM)] * len(outs),
        scratch_shapes=[pltpu.VMEM(shape, kind) for shape, kind in scratch],
        compiler_params=pltpu.CompilerParams(vmem_limit_bytes=megabytes * MIB),
        cost_estimate=cost(0.01),
        name=name,
    )(*args)


LOW = jnp.bfloat16
WIDE = jnp.float32
MATRICES = [(D, 3 * D), (D, D), (D, FF), (FF, D)]


def layer_unpack(pieces, plan, base, rows):
    half = pieces[0].shape[0]
    kernel = functools.partial(
        unpack_kernel, slot_masks(plan, 2 * half), half, base, rows, base + rows
    )
    outs = [((ROW_VEC, LANES), WIDE), ((1, LANES), WIDE)] + [(shape, LOW) for shape in MATRICES]
    scratch = [((round_up(2 * half * rows, 8), LANES), WIDE)]
    vec, count, *weights = call_kernel(kernel, "layer_unpack", 3, 10, outs, scratch, *pieces)
    return (vec, weights, count)


def forward_kernel(
    state_ref,
    vec,
    w_qkv,
    w_out,
    w_up,
    w_down,
    next_ref,
    qkv,
    probs,
    attended,
    mid,
    active,
    slope,
    normed,
    probs_low,
):
    blocks = D // LANES
    images_here = state_ref.shape[0] // TOKENS
    gain, bias = row_vector(vec, 0, blocks), row_vector(vec, 3, blocks)
    for image in range(images_here):
        place = slice(image * TOKENS, (image + 1) * TOKENS)
        normal, inverse = norm_parts(state_ref[place, :])
        normed[place, :] = (normal * gain + bias).astype(jnp.bfloat16)
    for part in range(3):
        columns = slice(part * D, (part + 1) * D)
        value = dot_plain(normed[...], w_qkv[:, columns])
        if part != 1:
            value = value + row_vector(vec, 12 if part == 0 else 15, blocks)
        qkv[:, columns] = value.astype(jnp.bfloat16)

    left_lane = lax.broadcasted_iota(jnp.int32, (TOKENS, LANES), 1) < HEAD
    real_key = lax.broadcasted_iota(jnp.int32, (TOKENS, TOKENS), 1) < SEQ
    for image in range(images_here):
        place = slice(image * TOKENS, (image + 1) * TOKENS)
        for pair in range(HEADS // 2):
            queries = qkv[place, pair * LANES : (pair + 1) * LANES]
            keys = qkv[place, D + pair * LANES : D + (pair + 1) * LANES]
            for side in range(2):
                own = left_lane if side == 0 else jnp.logical_not(left_lane)
                head_queries = jnp.where(own, queries, jnp.zeros_like(queries))
                scores = contract_last(head_queries, keys) * HEAD ** (-0.5)
                scores = jnp.where(real_key, scores, -1e30)
                exponent = jnp.exp(scores - jnp.max(scores, -1, keepdims=True))
                prob = exponent * (1.0 / jnp.sum(exponent, -1, keepdims=True))
                probs[image * HEADS + 2 * pair + side] = prob
                probs_low[image * HEADS + 2 * pair + side] = prob.astype(jnp.bfloat16)
    for image in range(images_here):
        place = slice(image * TOKENS, (image + 1) * TOKENS)
        for pair in range(HEADS // 2):
            values = qkv[place, 2 * D + pair * LANES : 2 * D + (pair + 1) * LANES]
            head = image * HEADS + 2 * pair
            first = dot_plain(probs_low[head], values)
            second = dot_plain(probs_low[head + 1], values)
            joined = jnp.where(left_lane, first, second)
            attended[place, pair * LANES : (pair + 1) * LANES] = joined.astype(jnp.bfloat16)

    bias_out = row_vector(vec, 18, blocks)
    gain, bias = row_vector(vec, 6, blocks), row_vector(vec, 9, blocks)
    for image in range(images_here):
        place = slice(image * TOKENS, (image + 1) * TOKENS)
        value = state_ref[place, :] + dot_plain(attended[place, :], w_out[...]) + bias_out
        mid[place, :] = value
        normal, inverse = norm_parts(value)
        normed[place, :] = (normal * gain + bias).astype(jnp.bfloat16)
    for part in range(FF // D):
        columns = slice(part * D, (part + 1) * D)
        bias_up = row_vector(vec, 24 + blocks * part, blocks)
        for image in range(images_here):
            place = slice(image * TOKENS, (image + 1) * TOKENS)
            up_value = dot_plain(normed[place, :], w_up[:, columns]) + bias_up
            act, slo = gelu_parts(up_value)
            active[place, columns] = act.astype(jnp.bfloat16)
            slope[place, columns] = slo
    bias_down = row_vector(vec, 21, blocks)
    for image in range(images_here):
        place = slice(image * TOKENS, (image + 1) * TOKENS)
        next_ref[place, :] = mid[place, :] + dot_plain(active[place, :], w_down[...]) + bias_down


def layer_forward(state, vec, weights):
    tokens_here = state.shape[0]
    images_here = tokens_here // TOKENS
    outs = [
        (state.shape, WIDE),
        ((tokens_here, 3 * D), LOW),
        ((images_here * HEADS, TOKENS, TOKENS), WIDE),
        ((tokens_here, D), LOW),
        ((tokens_here, D), WIDE),
        ((tokens_here, FF), LOW),
        ((tokens_here, FF), WIDE),
    ]
    scratch = [(state.shape, LOW), (outs[2][0], LOW)]
    state_next, *saved = call_kernel(
        forward_kernel, "layer_forward", 7, 8, outs, scratch, state, vec, *weights
    )
    return (state_next, saved)


def backward_kernel(
    grad_ref,
    state_ref,
    vec,
    w_qkv,
    w_out,
    w_up,
    w_down,
    qkv,
    probs,
    mid,
    slope,
    grad_in_ref,
    sums_ref,
    grad_up,
    normed_two,
    grad_low,
    grad_qkv,
    normed_one,
    attended,
    grad_mid,
    grad_scores,
    probs_low,
):
    blocks = D // LANES
    images_here = grad_ref.shape[0] // TOKENS
    places = [slice(i * TOKENS, (i + 1) * TOKENS) for i in range(images_here)]
    put_vector(sums_ref, 21, column_sum(grad_ref[...]))
    grad_low[...] = grad_ref[...].astype(jnp.bfloat16)
    for part in range(FF // D):
        columns = slice(part * D, (part + 1) * D)
        total = 0.0
        for place in places:
            value = contract_last(grad_low[place, :], w_down[columns, :]) * slope[place, columns]
            total = total + column_sum(value)
            grad_up[place, columns] = value.astype(jnp.bfloat16)
        put_vector(sums_ref, 24 + blocks * part, total)
    gain, bias = row_vector(vec, 6, blocks), row_vector(vec, 9, blocks)
    sums = [0.0, 0.0, 0.0]
    for place in places:
        normal, inverse = norm_parts(mid[place, :])
        normed_two[place, :] = (normal * gain + bias).astype(jnp.bfloat16)
        grad_normed = contract_last(grad_up[place, :], w_up[...])
        sums[0] = sums[0] + column_sum(grad_normed * normal)
        sums[1] = sums[1] + column_sum(grad_normed)
        value = grad_ref[place, :] + norm_back(grad_normed, normal, inverse, gain)
        sums[2] = sums[2] + column_sum(value)
        grad_mid[place, :] = value
        grad_low[place, :] = value.astype(jnp.bfloat16)
    put_vector(sums_ref, 6, sums[0])
    put_vector(sums_ref, 9, sums[1])
    put_vector(sums_ref, 18, sums[2])
    for place in places:
        attended[place, :] = contract_last(grad_low[place, :], w_out[...]).astype(jnp.bfloat16)
    left_lane = lax.broadcasted_iota(jnp.int32, (TOKENS, LANES), 1) < HEAD
    for pair in range(HEADS // 2):
        for image, place in enumerate(places):
            values = qkv[place, 2 * D + pair * LANES : 2 * D + (pair + 1) * LANES]
            grad_here = attended[place, pair * LANES : (pair + 1) * LANES]
            for side in range(2):
                head = image * HEADS + 2 * pair + side
                own = left_lane if side == 0 else jnp.logical_not(left_lane)
                head_grad = jnp.where(own, grad_here, jnp.zeros_like(grad_here))
                prob = probs[head]
                grad_probs = contract_last(head_grad, values)
                inner = jnp.sum(grad_probs * prob, -1, keepdims=True)
                grad_scores[head] = (prob * (grad_probs - inner) * HEAD ** (-0.5)).astype(
                    jnp.bfloat16
                )
                probs_low[head] = prob.astype(jnp.bfloat16)
    for pair in range(HEADS // 2):
        sum_query, sum_value = 0.0, 0.0
        for image, place in enumerate(places):
            spans = [slice(i * D + pair * LANES, i * D + (pair + 1) * LANES) for i in range(3)]
            queries, keys = qkv[place, spans[0]], qkv[place, spans[1]]
            grad_here = attended[place, pair * LANES : (pair + 1) * LANES]
            results = []
            for side in range(2):
                head = image * HEADS + 2 * pair + side
                grad_queries = dot_plain(grad_scores[head], keys)
                grad_keys = contract_rows(grad_scores[head], queries)
                grad_values = contract_rows(probs_low[head], grad_here)
                results.append((grad_queries, grad_keys, grad_values))
            joined = [jnp.where(left_lane, results[0][i], results[1][i]) for i in range(3)]
            for i in range(3):
                grad_qkv[place, spans[i]] = joined[i].astype(jnp.bfloat16)
            sum_query = sum_query + column_sum(joined[0])
            sum_value = sum_value + column_sum(joined[2])
        put_vector(sums_ref, 12 + pair, sum_query)
        put_vector(sums_ref, 15 + pair, sum_value)
    gain, bias = row_vector(vec, 0, blocks), row_vector(vec, 3, blocks)
    sums = [0.0, 0.0]
    for place in places:
        normal, inverse = norm_parts(state_ref[place, :])
        normed_one[place, :] = (normal * gain + bias).astype(jnp.bfloat16)
        grad_normed = contract_last(grad_qkv[place, :], w_qkv[...])
        sums[0] = sums[0] + column_sum(grad_normed * normal)
        sums[1] = sums[1] + column_sum(grad_normed)
        grad_in_ref[place, :] = grad_mid[place, :] + norm_back(grad_normed, normal, inverse, gain)
    put_vector(sums_ref, 0, sums[0])
    put_vector(sums_ref, 3, sums[1])


def layer_backward(grad_state, state, vec, weights, saved):
    qkv, probs, attended, mid, active, slope = saved
    tokens_here = grad_state.shape[0]
    outs = [(grad_state.shape, WIDE), ((ROW_VEC, LANES), WIDE)]
    outs = outs + [((tokens_here, width), LOW) for width in (FF, D, D, 3 * D, D)]
    scratch = [(grad_state.shape, LOW), (grad_state.shape, WIDE)] + [(probs.shape, LOW)] * 2
    args = [grad_state, state, vec, *weights, qkv, probs, mid, slope]
    outs = call_kernel(backward_kernel, "layer_backward", 7, 10, outs, scratch, *args)
    grad_in, sums, up_low, normed_two, mid_low, qkv_low, normed_one = outs
    factors = (active, normed_two, up_low, attended, mid_low, normed_one, qkv_low)
    return (grad_in, (sums, grad_state, *factors))


def weight_grad_kernel(
    masks,
    half,
    rows,
    extra,
    sums_ref,
    grad_ref,
    active,
    normed_two,
    grad_up,
    attended,
    mid_low,
    normed_one,
    grad_qkv,
    keep_ref,
    send_first,
    send_last,
    grad_low,
    flat,
):
    blocks = D // LANES
    flat[0:ROW_VEC, :] = sums_ref[...]
    flat[ROW_END:, :] = jnp.zeros((flat.shape[0] - ROW_END, LANES), jnp.float32)
    grad_low[...] = grad_ref[...].astype(jnp.bfloat16)
    for part in range(FF // D):
        columns = slice(part * D, (part + 1) * D)
        block = contract_rows(active[:, columns], grad_low[...])
        put_block(flat, ROW_DOWN, D, block, part * D, 0)
    for part in range(FF // D):
        columns = slice(part * D, (part + 1) * D)
        block = contract_rows(normed_two[...], grad_up[:, columns])
        put_block(flat, ROW_UP, FF, block, 0, blocks * part)
    put_block(flat, ROW_OUT, D, contract_rows(attended[...], mid_low[...]), 0, 0)
    for part in range(3):
        columns = slice(part * D, (part + 1) * D)
        block = contract_rows(normed_one[...], grad_qkv[:, columns])
        put_block(flat, ROW_QKV, 3 * D, block, 0, blocks * part)
    store_shards(keep_ref, (send_first, send_last), flat, masks, half, rows, rows)
    tail = extra[...]
    for ref in (keep_ref, send_first, send_last):
        for slot in range(ref.shape[0]):
            ref[slot, rows:, :] = tail


def weight_grads(factors, extra, rows, padded, plan, devices, order):
    half = devices // 2
    kernel = functools.partial(weight_grad_kernel, slot_masks(plan, devices), half, rows)
    outs = [((half, padded, LANES), LOW)] + [((half // 2, padded, LANES), LOW)] * 2
    scratch = [(factors[1].shape, LOW), ((round_up(2 * half * rows, 8), LANES), WIDE)]
    keep, *sends = call_kernel(kernel, "weight_grads", 4, 10, outs, scratch, extra, *factors)
    order.end(sends)
    return Scatter(keep, sends, plan, devices, order)


def embed_kernel(
    masks,
    half,
    rows,
    images,
    mine,
    theirs,
    state_ref,
    small_ref,
    head_ref,
    flat,
    head,
    patch,
    position,
):
    pieces = (mine, theirs)
    for shard in range(2 * half + 1):
        flat[shard * rows : shard * rows + 1, :] = jnp.zeros((1, LANES), jnp.float32)
    for slot, owners in enumerate(owner_pairs(masks, half)):
        for piece, owner in zip(pieces, owners):
            value = piece[slot, : rows + 1, :].astype(jnp.float32)
            flat[pl.ds(owner * rows + 1, rows - 1), :] = value[1:rows]
            flat[pl.ds(owner * rows, 1), :] += value[0:1]
            flat[pl.ds((owner + 1) * rows, 1), :] += value[rows : rows + 1]
    lane = lax.broadcasted_iota(jnp.int32, (24, LANES), 1)
    low = pltpu.roll(flat[0:24, :], LANES - OUTER_SHIFT, 1)
    later = pltpu.roll(flat[1:25, :], LANES - OUTER_SHIFT, 1)
    small = jnp.where(lane < LANES - OUTER_SHIFT, low, later)
    line = lax.broadcasted_iota(jnp.int32, (24, LANES), 0)
    past = (line - 4 * D // LANES) * LANES + lane >= CLASSES
    small_ref[...] = jnp.where(past, 0.0, small)
    blocks = D // LANES
    for c, block in enumerate(take_matrix(flat, OROW_POS, SEQ, D)):
        position[:SEQ, c * LANES : (c + 1) * LANES] = block
    for c, block in enumerate(take_matrix(flat, OROW_PATCH, PATCH_IN, D)):
        patch[:, c * LANES : (c + 1) * LANES] = block.astype(jnp.bfloat16)
    bias_patch = row_vector(small_ref, 3 * blocks, blocks)
    for image in range(images.shape[0]):
        base = image * TOKENS
        state_ref[base + SEQ : base + TOKENS, :] = jnp.zeros((TOKENS - SEQ, D), jnp.float32)
        state_ref[base : base + 1, :] = row_vector(small_ref, 0, blocks) + position[0:1, :]
        value = dot_plain(images[image], patch[...]) + bias_patch
        state_ref[base + 1 : base + SEQ, :] = value + position[1:SEQ, :]
    for p in range(16):
        shift, base = (CLASSES * p) % LANES, OROW_HEAD + (CLASSES * p) // LANES
        part = [flat[pl.ds(base + c, 24, stride=125), :] for c in range(9 if shift else 8)]
        if shift:
            part = [pltpu.roll(block, LANES - shift, 1) for block in part]
        for c in range(8):
            block = jnp.where(lane < LANES - shift, part[c], part[c + 1]) if shift else part[c]
            if c == 7:
                block = jnp.where(lane < CLASSES - 7 * LANES, block, 0.0)
            head[c, pl.ds(p, 24, stride=16), :] = block
    for c in range(8):
        head_ref[:, c * LANES : (c + 1) * LANES] = head[c].astype(jnp.bfloat16)


def embed_images(images, pieces, plan, rows):
    half = pieces[0].shape[0]
    kernel = functools.partial(embed_kernel, slot_masks(plan, 2 * half), half, rows)
    outs = [
        ((images.shape[0] * TOKENS, D), WIDE),
        ((24, LANES), WIDE),
        ((D, CLASS_PAD), LOW),
    ]
    scratch = [
        ((round_up(2 * half * rows + 1, 8), LANES), WIDE),
        ((CLASS_PAD // LANES, D, LANES), WIDE),
        ((PATCH_IN, D), LOW),
        ((TOKENS, D), WIDE),
    ]
    return call_kernel(kernel, "embed_images", 2, 8, outs, scratch, images, *pieces)


def head_kernel(
    labels,
    valid,
    state_ref,
    small,
    w_head,
    count,
    extra_ref,
    grad_ref,
    normed_ref,
    logit_grad_ref,
    vec_ref,
    rows_in,
):
    blocks = D // LANES
    images_here = state_ref.shape[0] // TOKENS
    rows_in[...] = jnp.zeros(rows_in.shape, jnp.float32)
    for image in range(images_here):
        rows_in[image : image + 1, :] = state_ref[image * TOKENS : image * TOKENS + 1, :]
    normal, inverse = norm_parts(rows_in[...])
    gain, bias = row_vector(small, blocks, blocks), row_vector(small, 2 * blocks, blocks)
    normed_final = (normal * gain + bias).astype(jnp.bfloat16)
    bias_head = row_vector(small, 4 * blocks, CLASS_PAD // LANES)
    logits = dot_plain(normed_final, w_head[...]) + bias_head
    shape = logits.shape
    column = lax.broadcasted_iota(jnp.int32, shape, 1)
    line = lax.broadcasted_iota(jnp.int32, (shape[0], 1), 0)
    real = column < CLASSES
    label = jnp.zeros((shape[0], 1), jnp.int32)
    present = jnp.zeros((shape[0], 1), jnp.float32)
    for image in range(images_here):
        label = jnp.where(line == image, labels[image], label)
        present = jnp.where(line == image, valid[image].astype(jnp.float32), present)
    top_logit = jnp.max(jnp.where(real, logits, -1e30), -1, keepdims=True)
    exponent = jnp.where(real, jnp.exp(jnp.minimum(logits - top_logit, 0.0)), 0.0)
    total_exp = jnp.sum(exponent, -1, keepdims=True)
    log_total = jnp.log(total_exp) + top_logit
    target = jnp.where(column == label, 1.0 - smooth + smooth / CLASSES, smooth / CLASSES)
    target = jnp.where(real, target, 0.0)
    per_image = log_total - jnp.sum(target * logits, -1, keepdims=True)
    loss_here = jnp.sum(present * per_image, 0, keepdims=True)
    loss_high = loss_here.astype(jnp.bfloat16).astype(jnp.float32)
    loss_mid = (loss_here - loss_high).astype(jnp.bfloat16).astype(jnp.float32)
    loss_low = loss_here - loss_high - loss_mid
    me = lax.axis_index("fsdp")
    spare = extra_ref.shape
    place = lax.broadcasted_iota(jnp.int32, spare, 0) * LANES
    place = place + lax.broadcasted_iota(jnp.int32, spare, 1)
    extra = jnp.where(place == 3 * me, loss_high, 0.0)
    extra = jnp.where(place == 3 * me + 1, loss_mid, extra)
    extra_ref[...] = jnp.where(place == 3 * me + 2, loss_low, extra).astype(jnp.bfloat16)

    scale = present * (1.0 / count[0:1, 0:1])
    grad_logits = (exponent * (1.0 / total_exp) - target) * scale
    grad_logits_low = grad_logits.astype(jnp.bfloat16)
    grad_normed = contract_last(grad_logits_low, w_head[...])
    grad_final = norm_back(grad_normed, normal, inverse, gain)
    grad_ref[...] = jnp.zeros(grad_ref.shape, jnp.float32)
    for image in range(images_here):
        grad_ref[image * TOKENS : image * TOKENS + 1, :] = grad_final[image : image + 1, :]
    normed_ref[...] = jnp.where(line < images_here, normed_final, jnp.zeros_like(normed_final))
    logit_grad_ref[...] = grad_logits_low
    vec_ref[...] = jnp.zeros(vec_ref.shape, jnp.float32)
    put_vector(vec_ref, blocks, column_sum(grad_normed * normal))
    put_vector(vec_ref, 2 * blocks, column_sum(grad_normed))
    put_vector(vec_ref, 4 * blocks, column_sum(grad_logits))


def head_step(labels, valid, state, small, w_head, count, spare):
    lines = 16
    outs = [
        ((spare, LANES), LOW),
        (state.shape, WIDE),
        ((lines, D), LOW),
        ((lines, CLASS_PAD), LOW),
        ((24, LANES), WIDE),
    ]
    args = (labels, valid, state, small, w_head, count)
    return call_kernel(head_kernel, "head_step", 2, 4, outs, [((lines, D), WIDE)], *args, smem=2)


def outer_grad_kernel(
    masks,
    half,
    rows,
    grad_ref,
    images,
    normed_final,
    logit_grad,
    vec,
    keep_ref,
    send_ref,
    flat,
    head,
    small,
):
    blocks = D // LANES
    images_here = images.shape[0]
    bases = [image * TOKENS for image in range(images_here)]
    small[...] = vec[...]
    token = sum(grad_ref[base : base + 1, :] for base in bases)
    put_vector(small, 0, token)
    total = sum(grad_ref[base : base + SEQ, :] for base in bases)
    put_block(flat, OROW_POS, D, total, 0, 0)
    put_vector(small, 3 * blocks, column_sum(total) - token)
    lane = lax.broadcasted_iota(jnp.int32, (24, LANES), 1)
    line = lax.broadcasted_iota(jnp.int32, (24, LANES), 0)
    moved = pltpu.roll(small[...], OUTER_SHIFT, 1)
    above = jnp.where(line == 0, 0.0, pltpu.roll(moved, 1, 0))
    moved = jnp.where(lane < OUTER_SHIFT, above, moved)
    flat[0:OROW_POS, :] = moved[0:OROW_POS]
    grads = [grad_ref[base + 1 : base + SEQ, :].astype(jnp.bfloat16) for base in bases]
    for part in range(PATCH_IN // D):
        columns = slice(part * D, (part + 1) * D)
        block = sum(contract_rows(images[i, :, columns], grads[i]) for i in range(images_here))
        put_block(flat, OROW_PATCH, D, block, part * D, 0)
    for c in range(8):
        head[c] = contract_rows(normed_final[...], logit_grad[:, c * LANES : (c + 1) * LANES])

    def block_of(p, c):
        return head[c, pl.ds(p, 24, stride=16), :]

    for i in range(125):
        p, start = LANES * i // CLASSES, LANES * i % CLASSES
        c, shift = start // LANES, start % LANES
        value = block_of(p, c)
        if shift:
            value = pltpu.roll(value, LANES - shift, 1)
            if c < 7:
                later = pltpu.roll(block_of(p, c + 1), LANES - shift, 1)
                value = jnp.where(lane < LANES - shift, value, later)
        here = CLASSES - start
        if here < LANES:
            value = jnp.where(lane < here, value, pltpu.roll(block_of(p + 1, 0), here, 1))
        flat[pl.ds(OROW_HEAD + i, 24, stride=125), :] = value
    end = OROW_HEAD + 24 * 125
    flat[end:, :] = jnp.zeros((flat.shape[0] - end, LANES), jnp.float32)
    store_shards(keep_ref, (send_ref,), flat, masks, half, rows + 1, rows)


def outer_backward(
    grad_state, images, normed_final, logit_grad, vec, rows, padded, plan, devices, order
):
    half = devices // 2
    kernel = functools.partial(outer_grad_kernel, slot_masks(plan, devices), half, rows)
    outs = [((half, padded, LANES), LOW)] * 2
    scratch = [
        ((round_up(2 * half * rows + 1, 8), LANES), WIDE),
        ((CLASS_PAD // LANES, D, LANES), WIDE),
        ((24, LANES), WIDE),
    ]
    args = (grad_state, images, normed_final, logit_grad, vec)
    keep, send = call_kernel(kernel, "outer_backward", 2, 8, outs, scratch, *args)
    order.end(send)
    return Scatter(keep, [send], plan, devices, order)


def outer_update_kernel(
    total, params, momentum, average, params_out, momentum_out, average_out
):
    rows = params.shape[0]
    lane = lax.broadcasted_iota(jnp.int32, (rows, LANES), 1)
    here = pltpu.roll(total[0:rows, :], LANES - OUTER_SHIFT, 1)
    later = pltpu.roll(total[1 : rows + 1, :], LANES - OUTER_SHIFT, 1)
    grads = jnp.where(lane < LANES - OUTER_SHIFT, here, later)
    results = nesterov(params[...], momentum[...], average[...], grads)
    for ref, value in zip((params_out, momentum_out, average_out), results):
        ref[...] = value


def outer_update(total, *args):
    args = [arg.reshape(-1, LANES) for arg in args]
    outs = [(arg.shape, WIDE) for arg in args]
    results = call_kernel(outer_update_kernel, "outer_update", 1, 4, outs, [], total, *args)
    return [result.reshape(-1) for result in results]


def nesterov(params, momentum, average, grads):
    momentum_new = 0.5 * momentum + grads
    params_new = params - step_rate * (grads + 0.5 * momentum_new)
    return (params_new, momentum_new, 0.5 * average + 0.5 * params_new)


def shards(
    images,
    labels,
    valid,
    layer_params,
    layer_momentum,
    layer_average,
    outer_params,
    outer_momentum,
    outer_average,
):
    devices = lax.axis_size("fsdp")
    layer_rows = layer_params.shape[1] // LANES
    layer_padded = round_up(layer_rows + 3 * devices // LANES + 1, 8)
    outer_rows = outer_params.shape[0] // LANES
    outer_padded = round_up(outer_rows + 1, 16)

    def layer_shard(params, layer_index, tail):
        shard = params[layer_index].reshape(layer_rows, LANES).astype(jnp.bfloat16)
        tail = jnp.pad(tail, ((0, layer_padded - layer_rows - 1), (0, 0)))
        return jnp.concatenate([shard, tail.astype(jnp.bfloat16)])

    outer_shard = jnp.pad(outer_params, (OUTER_SHIFT, LANES - OUTER_SHIFT)).reshape(-1, LANES)
    outer_shard = jnp.pad(outer_shard, ((0, outer_padded - outer_rows - 1), (0, 0)))
    outer_shard = outer_shard.astype(jnp.bfloat16)
    empty = jnp.zeros((1, LANES), jnp.float32)
    first_shard = layer_shard(layer_params, 0, empty)
    order = Order(first_shard)
    one = Gather(first_shard, Z_FIRST, devices, order)
    kept = []

    def forward(state, pieces, plan):
        vec, weights, counts = layer_unpack(pieces, plan, 0, layer_rows)
        state_next, saved = layer_forward(state, vec, weights)
        kept.append((state, vec, weights, saved))
        order.end(state_next)
        return (state_next, counts)

    one.start()
    outer_later = order.begin(outer_shard)
    outer = Gather(outer_later, Z_FIRST, devices, order)
    order.end(outer_later)
    order.fence()
    outer.start()
    params_later, valid_later = order.begin((layer_params, valid))
    count = jnp.sum(valid_later).astype(jnp.float32).reshape(1, 1)
    count_row = jnp.pad(count, ((0, 0), (0, LANES - 1)))
    two = Gather(layer_shard(params_later, 1, count_row), Z_STEPS, devices, order)
    three = Gather(layer_shard(params_later, 2, empty), Z_STEPS, devices, order, True)
    order.end((two.column, three.column))
    order.fence()
    one.take()
    one.start()
    order.fence()
    two.start()
    order.fence()
    outer.take()
    outer.start()
    order.fence()
    one.take()
    one.start()
    order.fence()
    two.take()
    two.start()
    outer.take()
    outer.start()
    order.fence()
    three.start()
    order.fence()
    two.take()
    two.start()
    order.fence()
    three.take()
    three.start()
    order.fence()
    one.take()
    outer.take()
    two.take()
    two.start()
    three.take()
    three.start()
    outer.start()
    one.start()
    order.fence()
    pieces = outer.take_across()
    state, small, w_head = embed_images(images, pieces, Z_FIRST, outer_rows)
    order.end(state)
    state, unused = forward(state, one.take_across(), Z_FIRST)
    two.take()
    three.take()
    three.start()
    two.start()
    order.fence()
    state, image_counts = forward(state, two.take_across(), Z_STEPS)
    three.take()
    three.start()
    order.fence()
    state, unused = forward(state, three.take_across(), Z_STEPS)
    image_count = image_counts[0, 0]
    extra, grad_state, normed_final, logit_grad, vec_grad = head_step(
        labels, valid, state, small, w_head, image_counts, layer_padded - layer_rows
    )

    def backward(layer_index, grad_state):
        grad_state, factors = layer_backward(order.begin(grad_state), *kept[layer_index])
        order.end(grad_state)
        return (grad_state, factors)

    def packed(factors, plan):
        first, *rest = factors
        factors = (order.begin(first), *rest)
        return weight_grads(
            factors, extra, layer_rows, layer_padded, plan, devices, order
        )

    def turn_back(layer_index, grad_state):
        grad_state, factors = backward(layer_index, grad_state)
        return (grad_state, packed(factors))

    order.fence()
    grad_state, factors_three = backward(2, grad_state)
    three = packed(factors_three, Z_FIRST)
    three.start()
    order.fence()
    three.take()
    three.start()
    grad_state, factors_two = backward(1, grad_state)
    two = packed(factors_two, Z_FIRST)
    three.take()
    three.start()
    order.fence(20)
    two.start()
    two.take()
    two.start()
    grad_state, factors_one = backward(0, grad_state)
    order.fence()
    three.take()
    order.fence()
    order.fence()
    three.start()
    one = packed(factors_one, Z_FIRST)
    order.fence()
    order.fence()
    outer = outer_backward(
        order.begin(grad_state),
        images,
        normed_final,
        logit_grad,
        vec_grad,
        outer_rows,
        outer_padded,
        Z_FIRST,
        devices,
        order,
    )
    order.fence()
    three.take()
    outer.start()
    two.take()
    order.fence()
    one.start()
    two.start()
    order.fence(20)
    one.take()
    one.start()
    outer.take()
    two.take()
    two.start()
    order.fence()
    order.fence()
    one.take()
    order.fence(7)
    outer.start()
    two.take()
    order.fence(7)
    order.fence()
    one.start()
    one.take()
    one.start()
    outer.take()
    order.fence(20)
    order.fence()
    outer.start()
    order.fence()
    outer.take()
    outer.start()
    one.take()
    outer.take()
    sums = (one, two, three)
    layer_summed = [item.total for item in sums]
    outer_summed = outer.total
    loss_sum = jnp.sum(layer_summed[2][layer_rows:]) + order.token[0, 0]
    layer_grads = [summed[:layer_rows].reshape(-1) for summed in layer_summed]
    layer_grad = jnp.stack(layer_grads)
    layer_new, layer_mom_new, layer_avg_new = nesterov(
        layer_params, layer_momentum, layer_average, layer_grad
    )
    outer_new, outer_mom_new, outer_avg_new = outer_update(
        outer_summed, outer_params, outer_momentum, outer_average
    )
    return (
        loss_sum,
        image_count,
        layer_new,
        layer_mom_new,
        layer_avg_new,
        outer_new,
        outer_mom_new,
        outer_avg_new,
    )


def solution(mesh):
    return jax.shard_map(
        shards,
        mesh=mesh,
        in_specs=(
            P("fsdp", None, None),
            P("fsdp"),
            P("fsdp"),
            P(None, "fsdp"),
            P(None, "fsdp"),
            P(None, "fsdp"),
            P("fsdp"),
            P("fsdp"),
            P("fsdp"),
        ),
        out_specs=(
            P(),
            P(),
            P(None, "fsdp"),
            P(None, "fsdp"),
            P(None, "fsdp"),
            P("fsdp"),
            P("fsdp"),
            P("fsdp"),
        ),
        check_vma=False,
    )
```

```python
import functools

import jax
import jax.numpy as jnp
import numpy as np
from jax import lax
from jax.experimental import pallas as pl
from jax.experimental.pallas import tpu as pltpu
from jax.sharding import PartitionSpec as P

D = 384
HEADS = 6
HEAD = 64
FF = 1536
CLASSES = 1000
CLASS_PAD = 1024
PATCH_IN = 768
PATCHES = 196
SEQ = 197
LAYERS = 3
LANES = 128
TOKENS = 208

eps_norm = 1e-06
smooth = 0.1
step_rate = 20.0
root_half = 0.7071067811865476
inv_root_two_pi = 0.3989422804014327

MIB = 1024 * 1024


def cost(microseconds):
    return pl.CostEstimate(
        flops=int(microseconds * 1e9), bytes_accessed=int(microseconds * 3.5e6), transcendentals=0
    )


ROW_VEC = 36
ROW_QKV = ROW_VEC
ROW_OUT = ROW_QKV + 3 * D * D // LANES
ROW_UP = ROW_OUT + D * D // LANES
ROW_DOWN = ROW_UP + D * FF // LANES
ROW_END = ROW_DOWN + D * FF // LANES

OUTER_SHIFT = 24
SMALL_ROWS = 4 * D // LANES + CLASS_PAD // LANES
OROW_POS = (4 * D + CLASSES + OUTER_SHIFT) // LANES
OROW_PATCH = OROW_POS + SEQ * D // LANES
OROW_HEAD = OROW_PATCH + PATCH_IN * D // LANES


def round_up(value, unit):
    return (value + unit - 1) // unit * unit


def bits_of(devices):
    count = devices.bit_length() - 1
    assert 1 << count == devices
    return count


def steps_of(plan, devices):
    if devices != 32:
        return [[(1 << bit, 1 << bit)] for bit in range(1, bits_of(devices))]
    kinds = {
        "z": [(8, 8), (16, 16), (24, 24)],
        "z two": [(16, 16)],
        "z one": [(8, 8)],
        "near": [(4, 2)],
        "far": [(2, 4)],
    }
    return [kinds[name] for name in plan]


Z_FIRST = ("z", "near", "far")
Z_STEPS = ("z two", "z one", "near", "far")


def slot_masks(plan, devices):
    masks = [(0, 0)]
    for partners in steps_of(plan, devices):
        masks = masks + [(a ^ p, b ^ q) for p, q in partners for a, b in masks]
    return tuple(zip(*masks))


def swap(values, masks, devices):
    pairs = [(i, i ^ masks[i & 1]) for i in range(devices)]
    return lax.ppermute(values, "fsdp", pairs)


def used_rows(layer_index):
    return 16 if layer_index == LAYERS - 1 else TOKENS


def fence_kernel(token, out):
    out[...] = token[...]


class Order:
    def __init__(self, value):
        self.token = jnp.zeros((8, LANES), jnp.float32)
        self.latest = value

    def begin(self, value):
        value, self.latest, self.token = lax.optimization_barrier(
            (value, self.latest, self.token)
        )
        return value

    def end(self, value):
        self.latest = value
        return value

    def fence(self, microseconds=0.01):
        self.begin(())
        self.token = pl.pallas_call(
            fence_kernel,
            out_shape=jax.ShapeDtypeStruct((8, LANES), jnp.float32),
            in_specs=[pl.BlockSpec(memory_space=pltpu.VMEM)],
            out_specs=pl.BlockSpec(memory_space=pltpu.VMEM),
            compiler_params=pltpu.CompilerParams(vmem_limit_bytes=MIB),
            cost_estimate=cost(microseconds),
            name="fence",
        )(self.token)


class Gather:
    def __init__(self, shard, plan, devices, order, halves=False):
        self.halves = halves
        self.devices = devices
        self.order = order
        self.steps = steps_of(plan, devices)
        self.column = shard[None]
        self.plan_length = len(plan)

    def start(self):
        while len(self.steps) > self.plan_length:
            self.exchange()
            self.take()
        self.exchange()

    def exchange(self):
        self.column = self.order.begin(self.column)
        if not self.steps:
            half = self.column.shape[0] // 2
            value = self.column[half:] if self.halves else self.column
            self.arriving = [swap(value, (1, 1), self.devices)]
            return
        partners = self.steps.pop(0)
        self.arriving = [swap(self.column, masks, self.devices) for masks in partners]
        if self.halves and not self.steps:
            self.early = [swap(self.column, (1, 1), self.devices)]

    def take(self):
        if self.halves and not self.steps:
            self.early = [self.order.end(self.order.begin(self.early[0]))]
        first, *rest = self.arriving
        self.column = jnp.concatenate([self.column, self.order.begin(first)] + rest)
        self.order.end(self.column)

    def take_across(self):
        last = self.order.end(self.order.begin(self.arriving[0]))
        return (self.column, *(self.early if self.halves else ()), last)


class Scatter:
    def __init__(self, keep, sends, plan, devices, order):
        self.devices = devices
        self.order = order
        self.steps = [[(1, 1)] * len(sends)] + steps_of(plan, devices)[::-1]
        self.total = keep
        self.low = sends[::-1]
        self.late = None
        self.starts = 0
        self.plan_length = len(plan)

    def start(self):
        self.exchange()
        self.starts = self.starts + 1
        while self.starts > self.plan_length and self.steps:
            self.take()
            self.exchange()

    def exchange(self):
        partners = self.steps.pop(0)
        low = self.order.begin(self.low)
        self.arriving = [swap(part, masks, self.devices) for part, masks in zip(low, partners)]

    def take(self):
        first, *rest = self.arriving
        parts = [part.astype(jnp.float32) for part in [self.order.begin(first)] + rest]
        total = self.total.astype(jnp.float32)
        if len(parts) == 2:
            half = parts[0].shape[0]
            self.total, self.late = total[:half], parts[1]
            self.low = [self.order.end((total[half:] + parts[0]).astype(jnp.bfloat16))]
            return
        if self.late is not None:
            total, self.late = total + self.late, None
        if len(parts) == 3:
            total = total + ((parts[0] + parts[1]) + parts[2])
        else:
            total = total + parts[0]
        if not self.steps:
            self.total = self.order.end(total[0])
            return
        groups = 1 + len(self.steps[0])
        size = total.shape[0] // groups
        self.total = total[:size]
        sent = total[size:].astype(jnp.bfloat16)
        self.low = [sent[i * size : (i + 1) * size] for i in range(groups - 1)]
        self.order.end(sent)


def select_mask(core, masks, slot):
    first, second = masks[0][slot], masks[1][slot]
    if first == second:
        return first
    return jnp.where(core == 0, first, second)


def owner_pairs(masks, half):
    me = lax.axis_index("fsdp")
    core = lax.rem(me, 2)
    other = jnp.bitwise_xor(me, 1)
    return [
        (
            jnp.bitwise_xor(me, select_mask(core, masks, slot)),
            jnp.bitwise_xor(other, select_mask(1 - core, masks, slot)),
        )
        for slot in range(half)
    ]


def load_shards(pieces, flat, masks, half, base, rows):
    mine, *theirs = pieces
    size = half // len(theirs)
    for slot, (own, other) in enumerate(owner_pairs(masks, half)):
        value = mine[slot, base : base + rows, :].astype(jnp.float32)
        flat[pl.ds(own * rows, rows), :] = value
        value = theirs[slot // size][slot % size, base : base + rows, :].astype(jnp.float32)
        flat[pl.ds(other * rows, rows), :] = value


def store_shards(keep_ref, send_refs, flat, masks, half, rows, stride):
    size = half // len(send_refs)
    for slot, (own, other) in enumerate(owner_pairs(masks, half)):
        keep_ref[slot, :rows, :] = flat[pl.ds(own * stride, rows), :].astype(jnp.bfloat16)
        value = flat[pl.ds(other * stride, rows), :].astype(jnp.bfloat16)
        send_refs[slot // size][slot % size, :rows, :] = value


def row_vector(ref, row, blocks):
    return jnp.concatenate([ref[row + i : row + i + 1, :] for i in range(blocks)], axis=1)


def put_vector(ref, row, vector):
    for i in range(vector.shape[1] // LANES):
        ref[row + i : row + i + 1, :] = vector[:, i * LANES : (i + 1) * LANES]


def take_matrix(flat, row, height, width):
    blocks = width // LANES
    return [flat[pl.ds(row + c, height, stride=blocks), :] for c in range(blocks)]


def put_block(flat, row, width, block, first_row, first_block):
    blocks = width // LANES
    height = block.shape[0]
    for c in range(block.shape[1] // LANES):
        place = row + first_row * blocks + first_block + c
        flat[pl.ds(place, height, stride=blocks), :] = block[:, c * LANES : (c + 1) * LANES]


def dot_plain(left, right):
    return jnp.dot(left, right, preferred_element_type=jnp.float32)


def contract_rows(left, right):
    return lax.dot_general(
        left, right, (((0,), (0,)), ((), ())), preferred_element_type=jnp.float32
    )


def contract_last(left, right):
    return lax.dot_general(
        left, right, (((1,), (1,)), ((), ())), preferred_element_type=jnp.float32
    )


def norm_parts(values):
    center = values - jnp.mean(values, -1, keepdims=True)
    inverse = lax.rsqrt(jnp.mean(center * center, -1, keepdims=True) + eps_norm)
    return (center * inverse, inverse)


def norm_back(grad_normed, normal, inverse, gain):
    scaled = grad_normed * gain
    return inverse * (
        scaled
        - jnp.mean(scaled, -1, keepdims=True)
        - normal * jnp.mean(scaled * normal, -1, keepdims=True)
    )


def gelu_parts(values):
    below = 0.5 * (1.0 + lax.erf(values * root_half))
    bell = jnp.exp(-0.5 * values * values)
    return (values * below, below + values * bell * inv_root_two_pi)


def column_sum(values):
    return jnp.sum(values, 0, keepdims=True)


def unpack_kernel(masks, half, base, rows, count_row, *refs):
    *pieces, vec, count_ref, w_qkv, w_out, w_up, w_down, flat = refs
    load_shards(pieces, flat, masks, half, base, rows)
    vec[...] = flat[0:ROW_VEC, :]
    count = jnp.zeros((1, LANES), jnp.float32)
    for piece in pieces:
        for slot in range(piece.shape[0]):
            count = count + piece[slot, count_row : count_row + 1, :].astype(jnp.float32)
    count_ref[...] = count
    for ref, row in ((w_qkv, ROW_QKV), (w_out, ROW_OUT), (w_up, ROW_UP), (w_down, ROW_DOWN)):
        for c, block in enumerate(take_matrix(flat, row, *ref.shape)):
            ref[:, c * LANES : (c + 1) * LANES] = block.astype(jnp.bfloat16)


def call_kernel(kernel, name, microseconds, megabytes, outs, scratch, *args, smem=0):
    spaces = [pltpu.SMEM] * smem + [pltpu.VMEM] * (len(args) - smem)
    return pl.pallas_call(
        kernel,
        out_shape=[jax.ShapeDtypeStruct(shape, kind) for shape, kind in outs],
        in_specs=[pl.BlockSpec(memory_space=space) for space in spaces],
        out_specs=[pl.BlockSpec(memory_space=pltpu.VMEM)] * len(outs),
        scratch_shapes=[pltpu.VMEM(shape, kind) for shape, kind in scratch],
        compiler_params=pltpu.CompilerParams(vmem_limit_bytes=megabytes * MIB),
        cost_estimate=cost(0.01),
        name=name,
    )(*args)


LOW = jnp.bfloat16
WIDE = jnp.float32
MATRICES = [(D, 3 * D), (D, D), (D, FF), (FF, D)]


def layer_unpack(pieces, plan, base, rows):
    half = pieces[0].shape[0]
    kernel = functools.partial(
        unpack_kernel, slot_masks(plan, 2 * half), half, base, rows, base + rows
    )
    outs = [((ROW_VEC, LANES), WIDE), ((1, LANES), WIDE)] + [(shape, LOW) for shape in MATRICES]
    scratch = [((round_up(2 * half * rows, 8), LANES), WIDE)]
    vec, count, *weights = call_kernel(kernel, "layer_unpack", 3, 10, outs, scratch, *pieces)
    return (vec, weights, count)


def forward_kernel(
    used,
    state_ref,
    vec,
    w_qkv,
    w_out,
    w_up,
    w_down,
    next_ref,
    qkv,
    probs,
    attended,
    mid,
    active,
    slope,
    normed,
    probs_low,
):
    blocks = D // LANES
    images_here = state_ref.shape[0] // TOKENS
    gain, bias = row_vector(vec, 0, blocks), row_vector(vec, 3, blocks)
    for image in range(images_here):
        place = slice(image * TOKENS, (image + 1) * TOKENS)
        normal, inverse = norm_parts(state_ref[place, :])
        normed[place, :] = (normal * gain + bias).astype(jnp.bfloat16)
    for part in range(3):
        columns = slice(part * D, (part + 1) * D)
        value = dot_plain(normed[...], w_qkv[:, columns])
        if part != 1:
            value = value + row_vector(vec, 12 if part == 0 else 15, blocks)
        qkv[:, columns] = value.astype(jnp.bfloat16)

    left_lane = lax.broadcasted_iota(jnp.int32, (used, LANES), 1) < HEAD
    real_key = lax.broadcasted_iota(jnp.int32, (used, TOKENS), 1) < SEQ
    for image in range(images_here):
        place = slice(image * TOKENS, (image + 1) * TOKENS)
        rows = slice(image * TOKENS, image * TOKENS + used)
        for pair in range(HEADS // 2):
            queries = qkv[rows, pair * LANES : (pair + 1) * LANES]
            keys = qkv[place, D + pair * LANES : D + (pair + 1) * LANES]
            for side in range(2):
                own = left_lane if side == 0 else jnp.logical_not(left_lane)
                head_queries = jnp.where(own, queries, jnp.zeros_like(queries))
                scores = contract_last(head_queries, keys) * HEAD ** (-0.5)
                scores = jnp.where(real_key, scores, -1e30)
                exponent = jnp.exp(scores - jnp.max(scores, -1, keepdims=True))
                prob = exponent * (1.0 / jnp.sum(exponent, -1, keepdims=True))
                probs[image * HEADS + 2 * pair + side, :used, :] = prob
                probs_low[image * HEADS + 2 * pair + side, :used, :] = prob.astype(jnp.bfloat16)
    for image in range(images_here):
        place = slice(image * TOKENS, (image + 1) * TOKENS)
        rows = slice(image * TOKENS, image * TOKENS + used)
        for pair in range(HEADS // 2):
            values = qkv[place, 2 * D + pair * LANES : 2 * D + (pair + 1) * LANES]
            head = image * HEADS + 2 * pair
            first = dot_plain(probs_low[head, :used, :], values)
            second = dot_plain(probs_low[head + 1, :used, :], values)
            joined = jnp.where(left_lane, first, second)
            attended[rows, pair * LANES : (pair + 1) * LANES] = joined.astype(jnp.bfloat16)

    bias_out = row_vector(vec, 18, blocks)
    gain, bias = row_vector(vec, 6, blocks), row_vector(vec, 9, blocks)
    for image in range(images_here):
        place = slice(image * TOKENS, (image + 1) * TOKENS)
        rows = slice(image * TOKENS, image * TOKENS + used)
        value = state_ref[rows, :] + dot_plain(attended[rows, :], w_out[...]) + bias_out
        mid[rows, :] = value
        normal, inverse = norm_parts(value)
        normed[rows, :] = (normal * gain + bias).astype(jnp.bfloat16)
    for part in range(FF // D):
        columns = slice(part * D, (part + 1) * D)
        bias_up = row_vector(vec, 24 + blocks * part, blocks)
        for image in range(images_here):
            rows = slice(image * TOKENS, image * TOKENS + used)
            up_value = dot_plain(normed[rows, :], w_up[:, columns]) + bias_up
            act, slo = gelu_parts(up_value)
            active[rows, columns] = act.astype(jnp.bfloat16)
            slope[rows, columns] = slo
    bias_down = row_vector(vec, 21, blocks)
    for image in range(images_here):
        place = slice(image * TOKENS, (image + 1) * TOKENS)
        rows = slice(image * TOKENS, image * TOKENS + used)
        next_ref[rows, :] = mid[rows, :] + dot_plain(active[rows, :], w_down[...]) + bias_down


def layer_forward(state, vec, weights, used):
    tokens_here = state.shape[0]
    images_here = tokens_here // TOKENS
    outs = [
        (state.shape, WIDE),
        ((tokens_here, 3 * D), LOW),
        ((images_here * HEADS, TOKENS, TOKENS), WIDE),
        ((tokens_here, D), LOW),
        ((tokens_here, D), WIDE),
        ((tokens_here, FF), LOW),
        ((tokens_here, FF), WIDE),
    ]
    scratch = [(state.shape, LOW), (outs[2][0], LOW)]
    state_next, *saved = call_kernel(
        functools.partial(forward_kernel, used), "layer_forward", 7, 8, outs, scratch, state, vec, *weights
    )
    return (state_next, saved)


def backward_kernel(
    used,
    grad_ref,
    state_ref,
    vec,
    w_qkv,
    w_out,
    w_up,
    w_down,
    qkv,
    probs,
    mid,
    slope,
    grad_in_ref,
    sums_ref,
    grad_up,
    normed_two,
    grad_low,
    grad_qkv,
    normed_one,
    attended,
    grad_mid,
    grad_scores,
    probs_low,
):
    blocks = D // LANES
    images_here = grad_ref.shape[0] // TOKENS
    wholes = [slice(i * TOKENS, (i + 1) * TOKENS) for i in range(images_here)]
    places = [slice(i * TOKENS, i * TOKENS + used) for i in range(images_here)]
    if used < TOKENS:
        grad_mid[...] = jnp.zeros(grad_mid.shape, jnp.float32)
        grad_qkv[...] = jnp.zeros(grad_qkv.shape, jnp.bfloat16)
    put_vector(sums_ref, 21, sum(column_sum(grad_ref[place, :]) for place in places))
    for place in places:
        grad_low[place, :] = grad_ref[place, :].astype(jnp.bfloat16)
    for part in range(FF // D):
        columns = slice(part * D, (part + 1) * D)
        total = 0.0
        for place in places:
            value = contract_last(grad_low[place, :], w_down[columns, :]) * slope[place, columns]
            total = total + column_sum(value)
            grad_up[place, columns] = value.astype(jnp.bfloat16)
        put_vector(sums_ref, 24 + blocks * part, total)
    gain, bias = row_vector(vec, 6, blocks), row_vector(vec, 9, blocks)
    sums = [0.0, 0.0, 0.0]
    for place in places:
        normal, inverse = norm_parts(mid[place, :])
        normed_two[place, :] = (normal * gain + bias).astype(jnp.bfloat16)
        grad_normed = contract_last(grad_up[place, :], w_up[...])
        sums[0] = sums[0] + column_sum(grad_normed * normal)
        sums[1] = sums[1] + column_sum(grad_normed)
        value = grad_ref[place, :] + norm_back(grad_normed, normal, inverse, gain)
        sums[2] = sums[2] + column_sum(value)
        grad_mid[place, :] = value
        grad_low[place, :] = value.astype(jnp.bfloat16)
    put_vector(sums_ref, 6, sums[0])
    put_vector(sums_ref, 9, sums[1])
    put_vector(sums_ref, 18, sums[2])
    for place in places:
        attended[place, :] = contract_last(grad_low[place, :], w_out[...]).astype(jnp.bfloat16)
    left_lane = lax.broadcasted_iota(jnp.int32, (used, LANES), 1) < HEAD
    left_whole = lax.broadcasted_iota(jnp.int32, (TOKENS, LANES), 1) < HEAD
    for pair in range(HEADS // 2):
        for image, place in enumerate(places):
            values = qkv[wholes[image], 2 * D + pair * LANES : 2 * D + (pair + 1) * LANES]
            grad_here = attended[place, pair * LANES : (pair + 1) * LANES]
            for side in range(2):
                head = image * HEADS + 2 * pair + side
                own = left_lane if side == 0 else jnp.logical_not(left_lane)
                head_grad = jnp.where(own, grad_here, jnp.zeros_like(grad_here))
                prob = probs[head, :used, :]
                grad_probs = contract_last(head_grad, values)
                inner = jnp.sum(grad_probs * prob, -1, keepdims=True)
                grad_scores[head, :used, :] = (prob * (grad_probs - inner) * HEAD ** (-0.5)).astype(
                    jnp.bfloat16
                )
                probs_low[head, :used, :] = prob.astype(jnp.bfloat16)
    for pair in range(HEADS // 2):
        sum_query, sum_value = 0.0, 0.0
        for image, place in enumerate(places):
            spans = [slice(i * D + pair * LANES, i * D + (pair + 1) * LANES) for i in range(3)]
            queries, keys = qkv[place, spans[0]], qkv[wholes[image], spans[1]]
            grad_here = attended[place, pair * LANES : (pair + 1) * LANES]
            results = []
            for side in range(2):
                head = image * HEADS + 2 * pair + side
                grad_queries = dot_plain(grad_scores[head, :used, :], keys)
                grad_keys = contract_rows(grad_scores[head, :used, :], queries)
                grad_values = contract_rows(probs_low[head, :used, :], grad_here)
                results.append((grad_queries, grad_keys, grad_values))
            sides = (left_lane, left_whole, left_whole)
            joined = [jnp.where(sides[i], results[0][i], results[1][i]) for i in range(3)]
            for i, lines in enumerate((place, wholes[image], wholes[image])):
                grad_qkv[lines, spans[i]] = joined[i].astype(jnp.bfloat16)
            sum_query = sum_query + column_sum(joined[0])
            sum_value = sum_value + column_sum(joined[2])
        put_vector(sums_ref, 12 + pair, sum_query)
        put_vector(sums_ref, 15 + pair, sum_value)
    gain, bias = row_vector(vec, 0, blocks), row_vector(vec, 3, blocks)
    sums = [0.0, 0.0]
    for place in wholes:
        normal, inverse = norm_parts(state_ref[place, :])
        normed_one[place, :] = (normal * gain + bias).astype(jnp.bfloat16)
        grad_normed = contract_last(grad_qkv[place, :], w_qkv[...])
        sums[0] = sums[0] + column_sum(grad_normed * normal)
        sums[1] = sums[1] + column_sum(grad_normed)
        grad_in_ref[place, :] = grad_mid[place, :] + norm_back(grad_normed, normal, inverse, gain)
    put_vector(sums_ref, 0, sums[0])
    put_vector(sums_ref, 3, sums[1])


def layer_backward(grad_state, state, vec, weights, saved, used):
    qkv, probs, attended, mid, active, slope = saved
    tokens_here = grad_state.shape[0]
    outs = [(grad_state.shape, WIDE), ((ROW_VEC, LANES), WIDE)]
    outs = outs + [((tokens_here, width), LOW) for width in (FF, D, D, 3 * D, D)]
    scratch = [(grad_state.shape, LOW), (grad_state.shape, WIDE)] + [(probs.shape, LOW)] * 2
    args = [grad_state, state, vec, *weights, qkv, probs, mid, slope]
    outs = call_kernel(functools.partial(backward_kernel, used), "layer_backward", 7, 10, outs, scratch, *args)
    grad_in, sums, up_low, normed_two, mid_low, qkv_low, normed_one = outs
    factors = (active, normed_two, up_low, attended, mid_low, normed_one, qkv_low)
    return (grad_in, (sums, grad_state, *factors))


def weight_grad_kernel(
    masks,
    half,
    rows,
    used,
    extra,
    sums_ref,
    grad_ref,
    active,
    normed_two,
    grad_up,
    attended,
    mid_low,
    normed_one,
    grad_qkv,
    keep_ref,
    send_first,
    send_last,
    grad_low,
    flat,
):
    blocks = D // LANES
    flat[0:ROW_VEC, :] = sums_ref[...]
    flat[ROW_END:, :] = jnp.zeros((flat.shape[0] - ROW_END, LANES), jnp.float32)
    images_here = grad_ref.shape[0] // TOKENS

    def lines(ref, columns=slice(None)):
        if used == TOKENS:
            return ref[:, columns]
        return jnp.concatenate([ref[i * TOKENS : i * TOKENS + used, columns] for i in range(images_here)])

    count = images_here * used
    grad_low[:count, :] = lines(grad_ref).astype(jnp.bfloat16)
    for part in range(FF // D):
        columns = slice(part * D, (part + 1) * D)
        block = contract_rows(lines(active, columns), grad_low[:count, :])
        put_block(flat, ROW_DOWN, D, block, part * D, 0)
    for part in range(FF // D):
        columns = slice(part * D, (part + 1) * D)
        block = contract_rows(lines(normed_two), lines(grad_up, columns))
        put_block(flat, ROW_UP, FF, block, 0, blocks * part)
    put_block(flat, ROW_OUT, D, contract_rows(lines(attended), lines(mid_low)), 0, 0)
    for part in range(3):
        columns = slice(part * D, (part + 1) * D)
        block = contract_rows(normed_one[...], grad_qkv[:, columns])
        put_block(flat, ROW_QKV, 3 * D, block, 0, blocks * part)
    store_shards(keep_ref, (send_first, send_last), flat, masks, half, rows, rows)
    tail = extra[...]
    for ref in (keep_ref, send_first, send_last):
        for slot in range(ref.shape[0]):
            ref[slot, rows:, :] = tail


def weight_grads(factors, extra, rows, padded, used, plan, devices, order):
    half = devices // 2
    kernel = functools.partial(weight_grad_kernel, slot_masks(plan, devices), half, rows, used)
    outs = [((half, padded, LANES), LOW)] + [((half // 2, padded, LANES), LOW)] * 2
    scratch = [(factors[1].shape, LOW), ((round_up(2 * half * rows, 8), LANES), WIDE)]
    keep, *sends = call_kernel(kernel, "weight_grads", 4, 10, outs, scratch, extra, *factors)
    order.end(sends)
    return Scatter(keep, sends, plan, devices, order)


def embed_kernel(
    masks,
    half,
    rows,
    images,
    mine,
    theirs,
    state_ref,
    small_ref,
    head_ref,
    flat,
    head,
    patch,
    position,
):
    pieces = (mine, theirs)
    for shard in range(2 * half + 1):
        flat[shard * rows : shard * rows + 1, :] = jnp.zeros((1, LANES), jnp.float32)
    for slot, owners in enumerate(owner_pairs(masks, half)):
        for piece, owner in zip(pieces, owners):
            value = piece[slot, : rows + 1, :].astype(jnp.float32)
            flat[pl.ds(owner * rows + 1, rows - 1), :] = value[1:rows]
            flat[pl.ds(owner * rows, 1), :] += value[0:1]
            flat[pl.ds((owner + 1) * rows, 1), :] += value[rows : rows + 1]
    lane = lax.broadcasted_iota(jnp.int32, (24, LANES), 1)
    low = pltpu.roll(flat[0:24, :], LANES - OUTER_SHIFT, 1)
    later = pltpu.roll(flat[1:25, :], LANES - OUTER_SHIFT, 1)
    small = jnp.where(lane < LANES - OUTER_SHIFT, low, later)
    line = lax.broadcasted_iota(jnp.int32, (24, LANES), 0)
    past = (line - 4 * D // LANES) * LANES + lane >= CLASSES
    small_ref[...] = jnp.where(past, 0.0, small)
    blocks = D // LANES
    for c, block in enumerate(take_matrix(flat, OROW_POS, SEQ, D)):
        position[:SEQ, c * LANES : (c + 1) * LANES] = block
    for c, block in enumerate(take_matrix(flat, OROW_PATCH, PATCH_IN, D)):
        patch[:, c * LANES : (c + 1) * LANES] = block.astype(jnp.bfloat16)
    bias_patch = row_vector(small_ref, 3 * blocks, blocks)
    for image in range(images.shape[0]):
        base = image * TOKENS
        state_ref[base + SEQ : base + TOKENS, :] = jnp.zeros((TOKENS - SEQ, D), jnp.float32)
        state_ref[base : base + 1, :] = row_vector(small_ref, 0, blocks) + position[0:1, :]
        value = dot_plain(images[image], patch[...]) + bias_patch
        state_ref[base + 1 : base + SEQ, :] = value + position[1:SEQ, :]
    for p in range(16):
        shift, base = (CLASSES * p) % LANES, OROW_HEAD + (CLASSES * p) // LANES
        part = [flat[pl.ds(base + c, 24, stride=125), :] for c in range(9 if shift else 8)]
        if shift:
            part = [pltpu.roll(block, LANES - shift, 1) for block in part]
        for c in range(8):
            block = jnp.where(lane < LANES - shift, part[c], part[c + 1]) if shift else part[c]
            if c == 7:
                block = jnp.where(lane < CLASSES - 7 * LANES, block, 0.0)
            head[c, pl.ds(p, 24, stride=16), :] = block
    for c in range(8):
        head_ref[:, c * LANES : (c + 1) * LANES] = head[c].astype(jnp.bfloat16)


def embed_images(images, pieces, plan, rows):
    half = pieces[0].shape[0]
    kernel = functools.partial(embed_kernel, slot_masks(plan, 2 * half), half, rows)
    outs = [
        ((images.shape[0] * TOKENS, D), WIDE),
        ((24, LANES), WIDE),
        ((D, CLASS_PAD), LOW),
    ]
    scratch = [
        ((round_up(2 * half * rows + 1, 8), LANES), WIDE),
        ((CLASS_PAD // LANES, D, LANES), WIDE),
        ((PATCH_IN, D), LOW),
        ((TOKENS, D), WIDE),
    ]
    return call_kernel(kernel, "embed_images", 2, 8, outs, scratch, images, *pieces)


def head_kernel(
    labels,
    valid,
    state_ref,
    small,
    w_head,
    count,
    extra_ref,
    grad_ref,
    normed_ref,
    logit_grad_ref,
    vec_ref,
    rows_in,
):
    blocks = D // LANES
    images_here = state_ref.shape[0] // TOKENS
    rows_in[...] = jnp.zeros(rows_in.shape, jnp.float32)
    for image in range(images_here):
        rows_in[image : image + 1, :] = state_ref[image * TOKENS : image * TOKENS + 1, :]
    normal, inverse = norm_parts(rows_in[...])
    gain, bias = row_vector(small, blocks, blocks), row_vector(small, 2 * blocks, blocks)
    normed_final = (normal * gain + bias).astype(jnp.bfloat16)
    bias_head = row_vector(small, 4 * blocks, CLASS_PAD // LANES)
    logits = dot_plain(normed_final, w_head[...]) + bias_head
    shape = logits.shape
    column = lax.broadcasted_iota(jnp.int32, shape, 1)
    line = lax.broadcasted_iota(jnp.int32, (shape[0], 1), 0)
    real = column < CLASSES
    label = jnp.zeros((shape[0], 1), jnp.int32)
    present = jnp.zeros((shape[0], 1), jnp.float32)
    for image in range(images_here):
        label = jnp.where(line == image, labels[image], label)
        present = jnp.where(line == image, valid[image].astype(jnp.float32), present)
    top_logit = jnp.max(jnp.where(real, logits, -1e30), -1, keepdims=True)
    exponent = jnp.where(real, jnp.exp(jnp.minimum(logits - top_logit, 0.0)), 0.0)
    total_exp = jnp.sum(exponent, -1, keepdims=True)
    log_total = jnp.log(total_exp) + top_logit
    target = jnp.where(column == label, 1.0 - smooth + smooth / CLASSES, smooth / CLASSES)
    target = jnp.where(real, target, 0.0)
    per_image = log_total - jnp.sum(target * logits, -1, keepdims=True)
    loss_here = jnp.sum(present * per_image, 0, keepdims=True)
    loss_high = loss_here.astype(jnp.bfloat16).astype(jnp.float32)
    loss_mid = (loss_here - loss_high).astype(jnp.bfloat16).astype(jnp.float32)
    loss_low = loss_here - loss_high - loss_mid
    me = lax.axis_index("fsdp")
    spare = extra_ref.shape
    place = lax.broadcasted_iota(jnp.int32, spare, 0) * LANES
    place = place + lax.broadcasted_iota(jnp.int32, spare, 1)
    extra = jnp.where(place == 3 * me, loss_high, 0.0)
    extra = jnp.where(place == 3 * me + 1, loss_mid, extra)
    extra_ref[...] = jnp.where(place == 3 * me + 2, loss_low, extra).astype(jnp.bfloat16)

    scale = present * (1.0 / count[0:1, 0:1])
    grad_logits = (exponent * (1.0 / total_exp) - target) * scale
    grad_logits_low = grad_logits.astype(jnp.bfloat16)
    grad_normed = contract_last(grad_logits_low, w_head[...])
    grad_final = norm_back(grad_normed, normal, inverse, gain)
    grad_ref[...] = jnp.zeros(grad_ref.shape, jnp.float32)
    for image in range(images_here):
        grad_ref[image * TOKENS : image * TOKENS + 1, :] = grad_final[image : image + 1, :]
    normed_ref[...] = jnp.where(line < images_here, normed_final, jnp.zeros_like(normed_final))
    logit_grad_ref[...] = grad_logits_low
    vec_ref[...] = jnp.zeros(vec_ref.shape, jnp.float32)
    put_vector(vec_ref, blocks, column_sum(grad_normed * normal))
    put_vector(vec_ref, 2 * blocks, column_sum(grad_normed))
    put_vector(vec_ref, 4 * blocks, column_sum(grad_logits))


def head_step(labels, valid, state, small, w_head, count, spare):
    lines = 16
    outs = [
        ((spare, LANES), LOW),
        (state.shape, WIDE),
        ((lines, D), LOW),
        ((lines, CLASS_PAD), LOW),
        ((24, LANES), WIDE),
    ]
    args = (labels, valid, state, small, w_head, count)
    return call_kernel(head_kernel, "head_step", 2, 4, outs, [((lines, D), WIDE)], *args, smem=2)


def outer_grad_kernel(
    masks,
    half,
    rows,
    grad_ref,
    images,
    normed_final,
    logit_grad,
    vec,
    keep_ref,
    send_ref,
    flat,
    head,
    small,
):
    blocks = D // LANES
    images_here = images.shape[0]
    bases = [image * TOKENS for image in range(images_here)]
    small[...] = vec[...]
    token = sum(grad_ref[base : base + 1, :] for base in bases)
    put_vector(small, 0, token)
    total = sum(grad_ref[base : base + SEQ, :] for base in bases)
    put_block(flat, OROW_POS, D, total, 0, 0)
    put_vector(small, 3 * blocks, column_sum(total) - token)
    lane = lax.broadcasted_iota(jnp.int32, (24, LANES), 1)
    line = lax.broadcasted_iota(jnp.int32, (24, LANES), 0)
    moved = pltpu.roll(small[...], OUTER_SHIFT, 1)
    above = jnp.where(line == 0, 0.0, pltpu.roll(moved, 1, 0))
    moved = jnp.where(lane < OUTER_SHIFT, above, moved)
    flat[0:OROW_POS, :] = moved[0:OROW_POS]
    grads = [grad_ref[base + 1 : base + SEQ, :].astype(jnp.bfloat16) for base in bases]
    for part in range(PATCH_IN // D):
        columns = slice(part * D, (part + 1) * D)
        block = sum(contract_rows(images[i, :, columns], grads[i]) for i in range(images_here))
        put_block(flat, OROW_PATCH, D, block, part * D, 0)
    for c in range(8):
        head[c] = contract_rows(normed_final[...], logit_grad[:, c * LANES : (c + 1) * LANES])

    def block_of(p, c):
        return head[c, pl.ds(p, 24, stride=16), :]

    for i in range(125):
        p, start = LANES * i // CLASSES, LANES * i % CLASSES
        c, shift = start // LANES, start % LANES
        value = block_of(p, c)
        if shift:
            value = pltpu.roll(value, LANES - shift, 1)
            if c < 7:
                later = pltpu.roll(block_of(p, c + 1), LANES - shift, 1)
                value = jnp.where(lane < LANES - shift, value, later)
        here = CLASSES - start
        if here < LANES:
            value = jnp.where(lane < here, value, pltpu.roll(block_of(p + 1, 0), here, 1))
        flat[pl.ds(OROW_HEAD + i, 24, stride=125), :] = value
    end = OROW_HEAD + 24 * 125
    flat[end:, :] = jnp.zeros((flat.shape[0] - end, LANES), jnp.float32)
    store_shards(keep_ref, (send_ref,), flat, masks, half, rows + 1, rows)


def outer_backward(
    grad_state, images, normed_final, logit_grad, vec, rows, padded, plan, devices, order
):
    half = devices // 2
    kernel = functools.partial(outer_grad_kernel, slot_masks(plan, devices), half, rows)
    outs = [((half, padded, LANES), LOW)] * 2
    scratch = [
        ((round_up(2 * half * rows + 1, 8), LANES), WIDE),
        ((CLASS_PAD // LANES, D, LANES), WIDE),
        ((24, LANES), WIDE),
    ]
    args = (grad_state, images, normed_final, logit_grad, vec)
    keep, send = call_kernel(kernel, "outer_backward", 2, 8, outs, scratch, *args)
    order.end(send)
    return Scatter(keep, [send], plan, devices, order)


def outer_update_kernel(
    total, params, momentum, average, params_out, momentum_out, average_out
):
    rows = params.shape[0]
    lane = lax.broadcasted_iota(jnp.int32, (rows, LANES), 1)
    here = pltpu.roll(total[0:rows, :], LANES - OUTER_SHIFT, 1)
    later = pltpu.roll(total[1 : rows + 1, :], LANES - OUTER_SHIFT, 1)
    grads = jnp.where(lane < LANES - OUTER_SHIFT, here, later)
    results = nesterov(params[...], momentum[...], average[...], grads)
    for ref, value in zip((params_out, momentum_out, average_out), results):
        ref[...] = value


def outer_update(total, *args):
    args = [arg.reshape(-1, LANES) for arg in args]
    outs = [(arg.shape, WIDE) for arg in args]
    results = call_kernel(outer_update_kernel, "outer_update", 1, 4, outs, [], total, *args)
    return [result.reshape(-1) for result in results]


def nesterov(params, momentum, average, grads):
    momentum_new = 0.5 * momentum + grads
    params_new = params - step_rate * (grads + 0.5 * momentum_new)
    return (params_new, momentum_new, 0.5 * average + 0.5 * params_new)


def shards(
    images,
    labels,
    valid,
    layer_params,
    layer_momentum,
    layer_average,
    outer_params,
    outer_momentum,
    outer_average,
):
    devices = lax.axis_size("fsdp")
    layer_rows = layer_params.shape[1] // LANES
    layer_padded = round_up(layer_rows + 3 * devices // LANES + 1, 8)
    outer_rows = outer_params.shape[0] // LANES
    outer_padded = round_up(outer_rows + 1, 16)

    def layer_shard(params, layer_index, tail):
        shard = params[layer_index].reshape(layer_rows, LANES).astype(jnp.bfloat16)
        tail = jnp.pad(tail, ((0, layer_padded - layer_rows - 1), (0, 0)))
        return jnp.concatenate([shard, tail.astype(jnp.bfloat16)])

    outer_shard = jnp.pad(outer_params, (OUTER_SHIFT, LANES - OUTER_SHIFT)).reshape(-1, LANES)
    outer_shard = jnp.pad(outer_shard, ((0, outer_padded - outer_rows - 1), (0, 0)))
    outer_shard = outer_shard.astype(jnp.bfloat16)
    empty = jnp.zeros((1, LANES), jnp.float32)
    first_shard = layer_shard(layer_params, 0, empty)
    order = Order(first_shard)
    one = Gather(first_shard, Z_FIRST, devices, order)
    kept = []

    def forward(state, pieces, plan):
        vec, weights, counts = layer_unpack(pieces, plan, 0, layer_rows)
        used = used_rows(len(kept))
        state_next, saved = layer_forward(state, vec, weights, used)
        kept.append((state, vec, weights, saved))
        order.end(state_next)
        return (state_next, counts)

    one.start()
    outer_later = order.begin(outer_shard)
    outer = Gather(outer_later, Z_FIRST, devices, order)
    order.end(outer_later)
    order.fence()
    outer.start()
    params_later, valid_later = order.begin((layer_params, valid))
    count = jnp.sum(valid_later).astype(jnp.float32).reshape(1, 1)
    count_row = jnp.pad(count, ((0, 0), (0, LANES - 1)))
    two = Gather(layer_shard(params_later, 1, count_row), Z_STEPS, devices, order)
    three = Gather(layer_shard(params_later, 2, empty), Z_STEPS, devices, order, True)
    order.end((two.column, three.column))
    order.fence()
    one.take()
    one.start()
    order.fence()
    two.start()
    order.fence()
    outer.take()
    outer.start()
    order.fence()
    one.take()
    one.start()
    order.fence()
    two.take()
    two.start()
    outer.take()
    outer.start()
    order.fence()
    three.start()
    order.fence()
    two.take()
    two.start()
    order.fence()
    three.take()
    three.start()
    order.fence()
    one.take()
    outer.take()
    two.take()
    two.start()
    three.take()
    three.start()
    outer.start()
    one.start()
    order.fence()
    pieces = outer.take_across()
    state, small, w_head = embed_images(images, pieces, Z_FIRST, outer_rows)
    order.end(state)
    state, unused = forward(state, one.take_across(), Z_FIRST)
    two.take()
    three.take()
    three.start()
    two.start()
    order.fence()
    state, image_counts = forward(state, two.take_across(), Z_STEPS)
    three.take()
    three.start()
    order.fence()
    state, unused = forward(state, three.take_across(), Z_STEPS)
    image_count = image_counts[0, 0]
    extra, grad_state, normed_final, logit_grad, vec_grad = head_step(
        labels, valid, state, small, w_head, image_counts, layer_padded - layer_rows
    )

    def backward(layer_index, grad_state):
        grad_state, factors = layer_backward(
            order.begin(grad_state), *kept[layer_index], used_rows(layer_index)
        )
        order.end(grad_state)
        return (grad_state, factors)

    def packed(factors, plan, used=TOKENS):
        first, *rest = factors
        factors = (order.begin(first), *rest)
        return weight_grads(
            factors, extra, layer_rows, layer_padded, used, plan, devices, order
        )

    def turn_back(layer_index, grad_state):
        grad_state, factors = backward(layer_index, grad_state)
        return (grad_state, packed(factors))

    order.fence()
    grad_state, factors_three = backward(2, grad_state)
    three = packed(factors_three, Z_FIRST, used_rows(2))
    three.start()
    order.fence()
    three.take()
    three.start()
    grad_state, factors_two = backward(1, grad_state)
    two = packed(factors_two, Z_FIRST)
    three.take()
    three.start()
    order.fence(20)
    two.start()
    two.take()
    two.start()
    grad_state, factors_one = backward(0, grad_state)
    order.fence()
    three.take()
    order.fence()
    order.fence()
    three.start()
    one = packed(factors_one, Z_FIRST)
    order.fence()
    order.fence()
    outer = outer_backward(
        order.begin(grad_state),
        images,
        normed_final,
        logit_grad,
        vec_grad,
        outer_rows,
        outer_padded,
        Z_FIRST,
        devices,
        order,
    )
    order.fence()
    three.take()
    outer.start()
    two.take()
    order.fence()
    one.start()
    two.start()
    order.fence(20)
    one.take()
    one.start()
    outer.take()
    two.take()
    two.start()
    order.fence()
    order.fence()
    one.take()
    order.fence(7)
    outer.start()
    two.take()
    order.fence(7)
    order.fence()
    one.start()
    one.take()
    one.start()
    outer.take()
    order.fence(20)
    order.fence()
    outer.start()
    order.fence()
    outer.take()
    outer.start()
    one.take()
    outer.take()
    sums = (one, two, three)
    layer_summed = [item.total for item in sums]
    outer_summed = outer.total
    loss_sum = jnp.sum(layer_summed[2][layer_rows:]) + order.token[0, 0]
    layer_grads = [summed[:layer_rows].reshape(-1) for summed in layer_summed]
    layer_grad = jnp.stack(layer_grads)
    layer_new, layer_mom_new, layer_avg_new = nesterov(
        layer_params, layer_momentum, layer_average, layer_grad
    )
    outer_new, outer_mom_new, outer_avg_new = outer_update(
        outer_summed, outer_params, outer_momentum, outer_average
    )
    return (
        loss_sum,
        image_count,
        layer_new,
        layer_mom_new,
        layer_avg_new,
        outer_new,
        outer_mom_new,
        outer_avg_new,
    )


def solution(mesh):
    return jax.shard_map(
        shards,
        mesh=mesh,
        in_specs=(
            P("fsdp", None, None),
            P("fsdp"),
            P("fsdp"),
            P(None, "fsdp"),
            P(None, "fsdp"),
            P(None, "fsdp"),
            P("fsdp"),
            P("fsdp"),
            P("fsdp"),
        ),
        out_specs=(
            P(),
            P(),
            P(None, "fsdp"),
            P(None, "fsdp"),
            P(None, "fsdp"),
            P("fsdp"),
            P("fsdp"),
            P("fsdp"),
        ),
        check_vma=False,
    )
```
